32 devices in a mesh: dp: 16 (over z, y, x), ctx: 2 (over core).
Axes of the slice: x: 2, y: 2, z: 4, core: 2. Of those that a mesh axis runs over, the one named last changes fastest.
Arguments:
- hidden_in: bfloat16 [16, 256, 1024], P('dp', 'ctx'), may hold values from -6 to 6
- cotangent: bfloat16 [16, 256, 1024], P('dp', 'ctx'), may hold values from -6 to 6
- block_order: int32 [16, 4], P('dp'), may hold values from 0 to 3, each once within a row
- w_query: float32 [1024, 2048], P('dp'), may hold values from -0.1875 to 0.1875
- key_weight: float32 [1024, 1024], P('dp'), may hold values from -0.1875 to 0.1875
- value_weight: float32 [1024, 1024], P('dp'), may hold values from -0.1875 to 0.1875
- w_output: float32 [2048, 1024], P('dp'), may hold values from -1 to 1
- w_gate: float32 [1024, 3072], P('dp'), may hold values from -0.1875 to 0.1875
- w_up: float32 [1024, 3072], P('dp'), may hold values from -0.1875 to 0.1875
- w_down: float32 [3072, 1024], P('dp'), may hold values from -0.109375 to 0.109375
- norm_gains: float32 [2304], P('dp'), may hold values from 0.5 to 1.5
- momentum_query: float32 [1024, 2048], P('dp'), may hold values from -0.625 to 0.625
- key_momentum: float32 [1024, 1024], P('dp'), may hold values from -0.625 to 0.625
- value_momentum: float32 [1024, 1024], P('dp'), may hold values from -0.625 to 0.625
- momentum_output: float32 [2048, 1024], P('dp'), may hold values from -0.625 to 0.625
- momentum_gate: float32 [1024, 3072], P('dp'), may hold values from -0.625 to 0.625
- momentum_up: float32 [1024, 3072], P('dp'), may hold values from -0.625 to 0.625
- momentum_down: float32 [3072, 1024], P('dp'), may hold values from -0.625 to 0.625
- momentum_gains: float32 [2304], P('dp'), may hold values from -0.625 to 0.625
Outputs:
- layer_out: bfloat16 [16, 256, 1024], P('dp', 'ctx')
- input_grad: bfloat16 [16, 256, 1024], P('dp', 'ctx')
- update_query: float32 [1024, 2048], P('dp')
- update_key: float32 [1024, 1024], P('dp')
- update_value: float32 [1024, 1024], P('dp')
- update_output: float32 [2048, 1024], P('dp')
- update_gate: float32 [1024, 3072], P('dp')
- update_up: float32 [1024, 3072], P('dp')
- update_down: float32 [3072, 1024], P('dp')
- update_gains: float32 [2304], P('dp')
- next_momentum_query: float32 [1024, 2048], P('dp')
- next_momentum_key: float32 [1024, 1024], P('dp')
- next_momentum_value: float32 [1024, 1024], P('dp')
- next_momentum_output: float32 [2048, 1024], P('dp')
- next_momentum_gate: float32 [1024, 3072], P('dp')
- next_momentum_up: float32 [1024, 3072], P('dp')
- next_momentum_down: float32 [3072, 1024], P('dp')
- next_momentum_gains: float32 [2304], P('dp')
The draws below stay inside these ranges and needn't reach their ends.
Inputs may be any that keep to these rules, and one draw needn't show every extreme that they name: `block_order`: each row is a permutation of the blocks 0 to 3.
All inputs are finite; a program needn't handle non-finite values.
Results may differ from the reference program's by a relative error of at most 0.029.
Values may be sent and summed in bfloat16 or wider, within the bound.
No kernel may reach another device: no remote copies, remote signals or barrier semaphores. Data moves between devices by JAX's collectives and lax.ppermute only.
A program may use at most 256 MiB of HBM per device.

```python
import jax
import jax.numpy as jnp
from jax import lax

MODEL_WIDTH = 1024
QUERY_HEAD_COUNT = 16
KEY_VALUE_HEADS = 8
HEAD_DIM = 128
FF = 3072
BLK = 64
SEQUENCE_LENGTH = 256
NBLK = 4
GAINS = 2304
N_DP = 16


def level_of(rng, shape, pieces, least, high):
    def one(axis_at, parts):
        draws = jax.random.uniform(jax.random.fold_in(jax.random.fold_in(rng, 6), axis_at), (parts,), jnp.float32, least / len(pieces), high / len(pieces))
        return jnp.repeat(jnp.exp(draws), shape[axis_at] // parts).reshape((-1,) + (1,) * (len(shape) - axis_at - 1))

    gain = one(*pieces[0])
    for cut in pieces[1:]:
        gain = gain * one(*cut)
    return gain


def scatter_about(own_key, extent, width, limit, cuts=(), held_as=jnp.bfloat16):
    gain = level_of(own_key, extent, cuts, -0.22, 0.18) if cuts else 1.0
    values = jax.random.normal(own_key, extent, jnp.float32) * width * gain
    return jnp.minimum(jnp.maximum(values, -limit), limit).astype(held_as)


def setup_inputs(seed: int = 0) -> dict:
    arg_keys = jax.random.split(jax.random.key(seed), 20)
    return {
        "hidden_in": scatter_about(arg_keys[0], (N_DP, SEQUENCE_LENGTH, MODEL_WIDTH), 1.0, 6.0, ((0, 16), (1, 2))),
        "cotangent": scatter_about(arg_keys[1], (N_DP, SEQUENCE_LENGTH, MODEL_WIDTH), 1.0, 6.0, ((0, 16), (1, 2))),
        "block_order": jax.vmap(lambda own: jax.random.permutation(own, NBLK))(jax.random.split(arg_keys[2], N_DP)).reshape((N_DP, NBLK)).astype(jnp.int32),
        "w_query": scatter_about(arg_keys[3], (MODEL_WIDTH, QUERY_HEAD_COUNT * HEAD_DIM), MODEL_WIDTH ** -0.5, 0.1875, ((0, 16),), jnp.float32),
        "key_weight": scatter_about(arg_keys[4], (MODEL_WIDTH, KEY_VALUE_HEADS * HEAD_DIM), MODEL_WIDTH ** -0.5, 0.1875, ((0, 16),), jnp.float32),
        "value_weight": scatter_about(arg_keys[5], (MODEL_WIDTH, KEY_VALUE_HEADS * HEAD_DIM), MODEL_WIDTH ** -0.5, 0.1875, ((0, 16),), jnp.float32),
        "w_output": scatter_about(arg_keys[6], (QUERY_HEAD_COUNT * HEAD_DIM, MODEL_WIDTH), (QUERY_HEAD_COUNT * HEAD_DIM // 64) ** -0.5, 1.0, ((0, 16),), jnp.float32),
        "w_gate": scatter_about(arg_keys[7], (MODEL_WIDTH, FF), MODEL_WIDTH ** -0.5, 0.1875, ((0, 16),), jnp.float32),
        "w_up": scatter_about(arg_keys[8], (MODEL_WIDTH, FF), MODEL_WIDTH ** -0.5, 0.1875, ((0, 16),), jnp.float32),
        "w_down": scatter_about(arg_keys[9], (FF, MODEL_WIDTH), FF ** -0.5, 0.109375, ((0, 16),), jnp.float32),
        "norm_gains": jnp.clip(1.0 + 0.1 * jax.random.normal(arg_keys[10], (GAINS,), jnp.float32), 0.5, 1.5),
        "momentum_query": scatter_about(arg_keys[11], (MODEL_WIDTH, QUERY_HEAD_COUNT * HEAD_DIM), 0.1, 0.625, ((0, 16),), jnp.float32),
        "key_momentum": scatter_about(arg_keys[12], (MODEL_WIDTH, KEY_VALUE_HEADS * HEAD_DIM), 0.1, 0.625, ((0, 16),), jnp.float32),
        "value_momentum": scatter_about(arg_keys[13], (MODEL_WIDTH, KEY_VALUE_HEADS * HEAD_DIM), 0.1, 0.625, ((0, 16),), jnp.float32),
        "momentum_output": scatter_about(arg_keys[14], (QUERY_HEAD_COUNT * HEAD_DIM, MODEL_WIDTH), 0.1, 0.625, ((0, 16),), jnp.float32),
        "momentum_gate": scatter_about(arg_keys[15], (MODEL_WIDTH, FF), 0.1, 0.625, ((0, 16),), jnp.float32),
        "momentum_up": scatter_about(arg_keys[16], (MODEL_WIDTH, FF), 0.1, 0.625, ((0, 16),), jnp.float32),
        "momentum_down": scatter_about(arg_keys[17], (FF, MODEL_WIDTH), 0.1, 0.625, ((0, 16),), jnp.float32),
        "momentum_gains": scatter_about(arg_keys[18], (GAINS,), 0.1, 0.625, ((0, 16),), jnp.float32),
    }


@jax.custom_vjp
def low(v):
    return lax.optimization_barrier(v.astype(jnp.bfloat16)).astype(jnp.float32)

@jax.custom_vjp
def low_back(v):
    return v

def low_keep(v):
    return (low(v), None)

def low_pass(kept, grad):
    return (grad,)

def back_keep(v):
    return (v, None)

def back_low(kept, grad):
    return (low(grad),)
low.defvjp(low_keep, low_pass)
low_back.defvjp(back_keep, back_low)
EPSILON = 1e-06
THETA = 1000000.0
BETA_ONE = 0.9
BETA_TWO = 0.5
SOFTEN = 0.005
DECAY_FACTOR = 1.0
HIGHEST = lax.Precision.HIGHEST

def matrix_product(left, right):
    return jnp.dot(left, right, precision=HIGHEST)

def rms_norm(values, gain_vec):
    return values * lax.rsqrt(lax.optimization_barrier(jnp.mean(values * values, axis=-1, keepdims=True)) + EPSILON) * gain_vec

def rotary_tables(positions, head_size):
    half_size = head_size // 2
    frequency = THETA ** (-(jnp.arange(half_size, dtype=jnp.float32) * 2.0 / head_size))
    angles = positions.astype(jnp.float32)[:, None] * frequency[None, :]
    angles = jnp.concatenate([angles, angles], axis=1)
    return (jnp.cos(angles), jnp.sin(angles))

def rotate(values, cosine, sine_table):
    half_size = values.shape[-1] // 2
    turned = jnp.concatenate([-values[..., half_size:], values[..., :half_size]], axis=-1)
    return values * cosine[:, None, :] + turned * sine_table[:, None, :]

def attention(queries, key_row_block, value_row_block, positions):
    row_count = min(512, SEQUENCE_LENGTH)
    group_repeat_count = QUERY_HEAD_COUNT // KEY_VALUE_HEADS
    keys_all = jnp.repeat(key_row_block, group_repeat_count, axis=1)
    values_all = jnp.repeat(value_row_block, group_repeat_count, axis=1)
    scaling = HEAD_DIM ** (-0.5)

    def query_block(group_item):
        query_rows, query_pos = group_item
        scores = jnp.einsum('qhd,khd->hqk', query_rows, keys_all, precision=HIGHEST) * scaling
        scores = low_back(scores)
        allowed = query_pos[:, None] >= positions[None, :]
        scores = jnp.where(allowed[None], scores, -1e+30)
        row_top = lax.optimization_barrier(jnp.max(scores, axis=-1, keepdims=True))
        weights = jnp.exp(scores - row_top)
        probs = low(weights / lax.optimization_barrier(jnp.sum(weights, axis=-1, keepdims=True)))
        mixture = jnp.einsum('hqk,khd->qhd', probs, values_all, precision=HIGHEST)
        return mixture.reshape(row_count, QUERY_HEAD_COUNT * HEAD_DIM)
    blocks = (queries.reshape(SEQUENCE_LENGTH // row_count, row_count, QUERY_HEAD_COUNT, HEAD_DIM), positions.reshape(SEQUENCE_LENGTH // row_count, row_count))
    return lax.map(jax.checkpoint(query_block), blocks).reshape(SEQUENCE_LENGTH, QUERY_HEAD_COUNT * HEAD_DIM)

def forward(tokens_f, w_query, key_weight, value_weight, w_output, w_gate, w_up, w_down, gains_all, positions):
    gain_attn = gains_all[:MODEL_WIDTH]
    gain_mlp = gains_all[MODEL_WIDTH:2 * MODEL_WIDTH]
    gain_query = gains_all[2 * MODEL_WIDTH:2 * MODEL_WIDTH + HEAD_DIM]
    gain_key = gains_all[2 * MODEL_WIDTH + HEAD_DIM:]
    normalized_input = low(rms_norm(tokens_f, gain_attn))
    queries = low_back(matrix_product(normalized_input, w_query)).reshape(SEQUENCE_LENGTH, QUERY_HEAD_COUNT, HEAD_DIM)
    key_row_block = low_back(matrix_product(normalized_input, key_weight)).reshape(SEQUENCE_LENGTH, KEY_VALUE_HEADS, HEAD_DIM)
    value_row_block = low(low_back(matrix_product(normalized_input, value_weight))).reshape(SEQUENCE_LENGTH, KEY_VALUE_HEADS, HEAD_DIM)
    cosine, sine_table = rotary_tables(positions, HEAD_DIM)
    queries = low(rotate(rms_norm(queries, gain_query), cosine, sine_table))
    key_row_block = low(rotate(rms_norm(key_row_block, gain_key), cosine, sine_table))
    mixture = low(low_back(attention(queries, key_row_block, value_row_block, positions)))
    middle = tokens_f + low_back(matrix_product(mixture, w_output))
    normed_two = low(rms_norm(middle, gain_mlp))
    gate_act = low_back(matrix_product(normed_two, w_gate))
    upward = low_back(matrix_product(normed_two, w_up))
    active = low(jax.nn.silu(gate_act) * upward)
    return middle + matrix_product(active, w_down)

def lion_update(weight_arr, moment_arr, grad_arr, decay_now):
    blended = BETA_ONE * moment_arr + (1.0 - BETA_ONE) * grad_arr
    direction = blended / jnp.sqrt(blended * blended + SOFTEN)
    return (direction + decay_now * weight_arr, BETA_TWO * moment_arr + (1.0 - BETA_TWO) * grad_arr)

def reference(hidden_in, cotangent, block_order, w_query, key_weight, value_weight, w_output, w_gate, w_up, w_down, norm_gains, momentum_query, key_momentum, value_momentum, momentum_output, momentum_gate, momentum_up, momentum_down, momentum_gains):
    masters = (w_query, key_weight, value_weight, w_output, w_gate, w_up, w_down, norm_gains)
    moments = (momentum_query, key_momentum, value_momentum, momentum_output, momentum_gate, momentum_up, momentum_down, momentum_gains)
    copies = tuple((low(master) for master in masters))
    offsets = jnp.arange(BLK, dtype=jnp.int32)

    def one_group(totals, group_item):
        tokens_in, grad_in, slot_order = group_item
        positions = (slot_order[:, None] * BLK + offsets[None, :]).reshape(SEQUENCE_LENGTH).astype(jnp.int32)

        def run_layer(tokens_f, *weight_list):
            return forward(tokens_f, *weight_list, positions)
        result, pullback = jax.vjp(run_layer, tokens_in.astype(jnp.float32), *copies)
        gradients = pullback(grad_in.astype(jnp.float32))
        totals = tuple((total + grad_arr for total, grad_arr in zip(totals, gradients[1:])))
        return (totals, (result.astype(jnp.bfloat16), gradients[0].astype(jnp.bfloat16)))
    zeros_all = tuple((jnp.zeros(copy_arr.shape, jnp.float32) for copy_arr in copies))
    sums, outputs = lax.scan(one_group, zeros_all, (hidden_in, cotangent, block_order))
    layer_out, input_grad = outputs
    norm_scale = lax.rsqrt(jnp.float32(N_DP * SEQUENCE_LENGTH))
    gradients = tuple((total * norm_scale for total in sums))
    updates = []
    new_moments = []
    for tensor_index in range(8):
        decay_here = DECAY_FACTOR if tensor_index < 7 else 0.0
        update_arr, new_moment = lion_update(masters[tensor_index], moments[tensor_index], gradients[tensor_index], decay_here)
        updates.append(update_arr)
        new_moments.append(new_moment)
    return (layer_out, input_grad, updates[0], updates[1], updates[2], updates[3], updates[4], updates[5], updates[6], updates[7], new_moments[0], new_moments[1], new_moments[2], new_moments[3], new_moments[4], new_moments[5], new_moments[6], new_moments[7])
```

```python
import jax
import jax.numpy as jnp
from jax import lax
from jax.sharding import PartitionSpec as P

EPSILON = 1e-06
THETA = 1000000.0
BETA_ONE = 0.9
BETA_TWO = 0.5
SOFTEN = 0.005
DECAY_FACTOR = 1.0


def rms_norm(values, gain_vec):
    return (
        values * lax.rsqrt(jnp.mean(values * values, axis=-1, keepdims=True) + EPSILON) * gain_vec
    )


def rotary_tables(positions, head_size):
    half_size = head_size // 2
    frequency = THETA ** (-(jnp.arange(half_size, dtype=jnp.float32) * 2.0 / head_size))
    angles = positions.astype(jnp.float32)[:, None] * frequency[None, :]
    angles = jnp.concatenate([angles, angles], axis=1)
    return (jnp.cos(angles), jnp.sin(angles))


def rotate(values, cosine, sine_table):
    half_size = values.shape[-1] // 2
    turned = jnp.concatenate([-values[..., half_size:], values[..., :half_size]], axis=-1)
    return values * cosine[:, None, :] + turned * sine_table[:, None, :]


def head_prep(projected, gain_vec, cosine, sine_table):
    shaped = projected.reshape(projected.shape[0], -1, gain_vec.shape[0])
    return rotate(rms_norm(shaped, gain_vec), cosine, sine_table)


def matmul(left, right):
    return jnp.dot(left, right, preferred_element_type=jnp.float32)


def contract_rows(left, right):
    return lax.dot_general(
        left, right, (((0,), (0,)), ((), ())), preferred_element_type=jnp.float32
    )


def contract_cols(left, right):
    return lax.dot_general(
        left, right, (((1,), (1,)), ((), ())), preferred_element_type=jnp.float32
    )


def head_scores(queries, key_row_block, query_pos, key_pos):
    scaling = queries.shape[-1] ** (-0.5)
    scores = (
        jnp.einsum("trd,kd->rtk", queries, key_row_block, preferred_element_type=jnp.float32)
        * scaling
    )
    allowed = query_pos[:, None] >= key_pos[None, :]
    return jnp.where(allowed[None], scores, -1e30)


def attend_head(query_pos, key_pos):

    def attend(group_item):
        queries, key_row_block, value_row_block = group_item
        scores = head_scores(queries, key_row_block, query_pos, key_pos)
        row_top = jnp.max(scores, axis=-1, keepdims=True)
        weights = jnp.exp(scores - row_top)
        row_total = jnp.sum(weights, axis=-1, keepdims=True)
        probs_low = (weights / row_total).astype(jnp.bfloat16)
        mixture = jnp.einsum(
            "rtk,kd->trd", probs_low, value_row_block, preferred_element_type=jnp.float32
        )
        return (mixture, (row_top + jnp.log(row_total))[..., 0])

    return attend


def attend_back(query_pos, key_pos):

    def backward(group_item):
        queries, key_row_block, value_row_block, grad_mix, log_total = group_item
        scaling = queries.shape[-1] ** (-0.5)
        scores = head_scores(queries, key_row_block, query_pos, key_pos)
        probs = jnp.exp(scores - log_total[..., None])
        grad_values = jnp.einsum(
            "rtk,trd->kd", probs.astype(jnp.bfloat16), grad_mix, preferred_element_type=jnp.float32
        )
        grad_probs = jnp.einsum(
            "trd,kd->rtk", grad_mix, value_row_block, preferred_element_type=jnp.float32
        )
        inner = jnp.sum(probs * grad_probs, axis=-1, keepdims=True)
        grad_scores = (probs * (grad_probs - inner)).astype(jnp.bfloat16)
        grad_queries = (
            jnp.einsum(
                "rtk,kd->trd", grad_scores, key_row_block, preferred_element_type=jnp.float32
            )
            * scaling
        )
        grad_keys = (
            jnp.einsum("rtk,trd->kd", grad_scores, queries, preferred_element_type=jnp.float32)
            * scaling
        )
        return (grad_queries, grad_keys, grad_values)

    return backward


def lion_step(masters, moments, gradients, norm_scale):
    updates = []
    new_moments = []
    for tensor_index in range(8):
        scaled = gradients[tensor_index] * norm_scale
        moment_arr = moments[tensor_index]
        blend_arr = BETA_ONE * moment_arr + (1.0 - BETA_ONE) * scaled
        direction = blend_arr / jnp.sqrt(blend_arr * blend_arr + SOFTEN)
        decay_here = DECAY_FACTOR if tensor_index < 7 else 0.0
        updates.append(direction + decay_here * masters[tensor_index])
        new_moments.append(BETA_TWO * moment_arr + (1.0 - BETA_TWO) * scaled)
    return (updates, new_moments)


def general_body(
    hidden_in,
    cotangent,
    block_order,
    w_query,
    key_weight,
    value_weight,
    w_output,
    w_gate,
    w_up,
    w_down,
    norm_gains,
    momentum_query,
    key_momentum,
    value_momentum,
    momentum_output,
    momentum_gate,
    momentum_up,
    momentum_down,
    momentum_gains,
):
    copies = (
        lax.all_gather(w_query.astype(jnp.bfloat16), "dp", axis=0, tiled=True),
        lax.all_gather(key_weight.astype(jnp.bfloat16), "dp", axis=0, tiled=True),
        lax.all_gather(value_weight.astype(jnp.bfloat16), "dp", axis=0, tiled=True),
        lax.all_gather(w_output.astype(jnp.bfloat16), "dp", axis=0, tiled=True),
        lax.all_gather(w_gate.astype(jnp.bfloat16), "dp", axis=0, tiled=True),
        lax.all_gather(w_up.astype(jnp.bfloat16), "dp", axis=0, tiled=True),
        lax.all_gather(w_down.astype(jnp.bfloat16), "dp", axis=0, tiled=True),
        lax.all_gather(norm_gains.astype(jnp.bfloat16), "dp", axis=0, tiled=True),
    )
    query_mat, key_mat, value_mat, output_mat, gate_mat, up_mat, down_mat, gains_low = copies
    gains_all = gains_low.astype(jnp.float32)
    width = hidden_in.shape[2]
    head_size = (gains_all.shape[0] - 2 * width) // 2
    kv_heads = key_mat.shape[1] // head_size
    query_heads = query_mat.shape[1] // head_size
    group_repeat_count = query_heads // kv_heads
    gain_attn = gains_all[:width]
    gain_mlp = gains_all[width : 2 * width]
    gain_query = gains_all[2 * width : 2 * width + head_size]
    gain_key = gains_all[2 * width + head_size :]
    tokens_in = hidden_in[0]
    token_count = tokens_in.shape[0]
    block_size = token_count // 2
    slot_order = block_order[0]
    key_pos = (
        slot_order[:, None] * block_size + jnp.arange(block_size, dtype=jnp.int32)[None, :]
    ).reshape(-1)
    query_pos = lax.dynamic_slice_in_dim(key_pos, lax.axis_index("ctx") * token_count, token_count)
    cosine, sine_table = rotary_tables(query_pos, head_size)
    tokens_f = tokens_in.astype(jnp.float32)
    normed_f, norm_pull = jax.vjp(rms_norm, tokens_f, gain_attn)
    normalized_input = normed_f.astype(jnp.bfloat16)
    query_pre = matmul(normalized_input, query_mat)
    key_pre = matmul(normalized_input, key_mat)
    value_low = matmul(normalized_input, value_mat).astype(jnp.bfloat16)
    query_rot, query_pull = jax.vjp(
        lambda projected, gain_vec: head_prep(projected, gain_vec, cosine, sine_table),
        query_pre,
        gain_query,
    )
    key_rot, key_pull = jax.vjp(
        lambda projected, gain_vec: head_prep(projected, gain_vec, cosine, sine_table),
        key_pre,
        gain_key,
    )
    query_low = query_rot.astype(jnp.bfloat16)
    key_heads = key_rot.astype(jnp.bfloat16).transpose(1, 0, 2)
    value_heads = value_low.reshape(token_count, kv_heads, head_size).transpose(1, 0, 2)
    gathered = (
        lax.all_gather(key_heads, "ctx", axis=1, tiled=True),
        lax.all_gather(value_heads, "ctx", axis=1, tiled=True),
    )
    query_groups = query_low.reshape(
        token_count, kv_heads, group_repeat_count, head_size
    ).transpose(1, 0, 2, 3)
    mixture, log_total = lax.map(
        attend_head(query_pos, key_pos), (query_groups, gathered[0], gathered[1])
    )
    mixed_low = mixture.transpose(1, 0, 2, 3).reshape(token_count, -1).astype(jnp.bfloat16)
    middle = tokens_f + matmul(mixed_low, output_mat)
    normed_two_f, norm_two_pull = jax.vjp(rms_norm, middle, gain_mlp)
    normed_two = normed_two_f.astype(jnp.bfloat16)
    gate_act = matmul(normed_two, gate_mat)
    upward = matmul(normed_two, up_mat)
    active_f, swiglu_pull = jax.vjp(
        lambda gate_in, up_in: jax.nn.silu(gate_in) * up_in, gate_act, upward
    )
    active = active_f.astype(jnp.bfloat16)
    layer_out = (middle + matmul(active, down_mat)).astype(jnp.bfloat16)[None]
    grad_out = cotangent[0]
    grad_down = contract_rows(active, grad_out)
    grad_active = contract_cols(grad_out, down_mat)
    grad_gate_f, grad_up_f = swiglu_pull(grad_active)
    grad_gate = grad_gate_f.astype(jnp.bfloat16)
    grad_upward = grad_up_f.astype(jnp.bfloat16)
    grad_gate_mat = contract_rows(normed_two, grad_gate)
    grad_up_mat = contract_rows(normed_two, grad_upward)
    grad_normed_two = contract_cols(grad_gate, gate_mat) + contract_cols(grad_upward, up_mat)
    grad_middle_norm, grad_gain_mlp = norm_two_pull(grad_normed_two)
    grad_middle = grad_out.astype(jnp.float32) + grad_middle_norm
    grad_branch = grad_middle.astype(jnp.bfloat16)
    grad_output_mat = contract_rows(mixed_low, grad_branch)
    grad_mixed = contract_cols(grad_branch, output_mat).astype(jnp.bfloat16)
    grad_groups = grad_mixed.reshape(
        token_count, kv_heads, group_repeat_count, head_size
    ).transpose(1, 0, 2, 3)
    grad_query_groups, grad_key_all, grad_value_all = lax.map(
        attend_back(query_pos, key_pos),
        (query_groups, gathered[0], gathered[1], grad_groups, log_total),
    )
    grad_key_own, grad_value_own = (
        lax.psum_scatter(
            grad_key_all.astype(jnp.bfloat16), "ctx", scatter_dimension=1, tiled=True
        ).astype(jnp.float32),
        lax.psum_scatter(
            grad_value_all.astype(jnp.bfloat16), "ctx", scatter_dimension=1, tiled=True
        ).astype(jnp.float32),
    )
    grad_query_rot = grad_query_groups.transpose(1, 0, 2, 3).reshape(
        token_count, query_heads, head_size
    )
    grad_query_pre, grad_gain_query = query_pull(grad_query_rot)
    grad_key_pre, grad_gain_key = key_pull(grad_key_own.transpose(1, 0, 2))
    grad_query_low = grad_query_pre.astype(jnp.bfloat16)
    grad_key_low = grad_key_pre.astype(jnp.bfloat16)
    grad_value_low = grad_value_own.transpose(1, 0, 2).reshape(token_count, -1).astype(jnp.bfloat16)
    grad_query_mat = contract_rows(normalized_input, grad_query_low)
    grad_key_mat = contract_rows(normalized_input, grad_key_low)
    grad_value_mat = contract_rows(normalized_input, grad_value_low)
    grad_normed = (
        contract_cols(grad_query_low, query_mat)
        + contract_cols(grad_key_low, key_mat)
        + contract_cols(grad_value_low, value_mat)
    )
    grad_tokens_norm, grad_gain_attn = norm_pull(grad_normed)
    input_grad = (grad_middle + grad_tokens_norm).astype(jnp.bfloat16)[None]
    grad_gains = jnp.concatenate([grad_gain_attn, grad_gain_mlp, grad_gain_query, grad_gain_key])
    masters = (w_query, key_weight, value_weight, w_output, w_gate, w_up, w_down, norm_gains)
    moments = (
        momentum_query,
        key_momentum,
        value_momentum,
        momentum_output,
        momentum_gate,
        momentum_up,
        momentum_down,
        momentum_gains,
    )
    token_total = lax.axis_size("dp") * key_pos.shape[0]
    norm_scale = lax.rsqrt(jnp.float32(token_total))
    shares = (
        lax.psum_scatter(
            grad_query_mat.astype(jnp.bfloat16), "dp", scatter_dimension=0, tiled=True
        ).astype(jnp.float32),
        lax.psum_scatter(
            grad_key_mat.astype(jnp.bfloat16), "dp", scatter_dimension=0, tiled=True
        ).astype(jnp.float32),
        lax.psum_scatter(
            grad_value_mat.astype(jnp.bfloat16), "dp", scatter_dimension=0, tiled=True
        ).astype(jnp.float32),
        lax.psum_scatter(
            grad_output_mat.astype(jnp.bfloat16), "dp", scatter_dimension=0, tiled=True
        ).astype(jnp.float32),
        lax.psum_scatter(
            grad_gate_mat.astype(jnp.bfloat16), "dp", scatter_dimension=0, tiled=True
        ).astype(jnp.float32),
        lax.psum_scatter(
            grad_up_mat.astype(jnp.bfloat16), "dp", scatter_dimension=0, tiled=True
        ).astype(jnp.float32),
        lax.psum_scatter(
            grad_down.astype(jnp.bfloat16), "dp", scatter_dimension=0, tiled=True
        ).astype(jnp.float32),
        lax.psum_scatter(
            grad_gains.astype(jnp.bfloat16), "dp", scatter_dimension=0, tiled=True
        ).astype(jnp.float32),
    )
    summed = (
        lax.psum(shares[0].astype(jnp.bfloat16), "ctx").astype(jnp.float32),
        lax.psum(shares[1].astype(jnp.bfloat16), "ctx").astype(jnp.float32),
        lax.psum(shares[2].astype(jnp.bfloat16), "ctx").astype(jnp.float32),
        lax.psum(shares[3].astype(jnp.bfloat16), "ctx").astype(jnp.float32),
        lax.psum(shares[4].astype(jnp.bfloat16), "ctx").astype(jnp.float32),
        lax.psum(shares[5].astype(jnp.bfloat16), "ctx").astype(jnp.float32),
        lax.psum(shares[6].astype(jnp.bfloat16), "ctx").astype(jnp.float32),
        lax.psum(shares[7].astype(jnp.bfloat16), "ctx").astype(jnp.float32),
    )
    updates, new_moments = lion_step(masters, moments, summed, norm_scale)
    return (layer_out, input_grad) + tuple(updates) + tuple(new_moments)


X_BIT, Y_BIT, P_BIT, H_BIT = 1, 2, 4, 8
LOW = jnp.bfloat16


def swap(values, bit):
    return lax.ppermute(values, "dp", [(i, i ^ bit) for i in range(16)])


def swap_core(values):
    return lax.ppermute(values, "ctx", [(0, 1), (1, 0)])


def h_of(index):
    return (index // H_BIT) % 2


def row_cross(values, to_owner):
    pairs = []
    for index in range(16):
        for core in range(2):
            if (core == h_of(index)) != to_owner:
                pairs.append((index * 2 + core, (index ^ H_BIT) * 2 + core))
    return lax.ppermute(values, ("dp", "ctx"), pairs)


def gather_column_slices(own, give):
    rows = own.shape[0]
    got = swap(give, P_BIT)
    far = swap(jnp.concatenate([own, got]), H_BIT)
    first = jnp.concatenate([own, far[:rows]])
    second = jnp.concatenate([got, far[rows:]])
    first = jnp.concatenate([first, swap(first, Y_BIT)])
    second = jnp.concatenate([second, swap(second, X_BIT)])
    first_x = swap(first, X_BIT)
    second_y = swap(second, Y_BIT)
    pieces = {}
    for place in range(4):
        outer, r_h = place // 2, place % 2
        cut = slice(place * rows, (place + 1) * rows)
        pieces[outer * Y_BIT + r_h * H_BIT] = first[cut]
        pieces[X_BIT + outer * Y_BIT + r_h * H_BIT] = first_x[cut]
        pieces[P_BIT + outer * X_BIT + r_h * H_BIT] = second[cut]
        pieces[P_BIT + Y_BIT + outer * X_BIT + r_h * H_BIT] = second_y[cut]
    return pieces


def gather_row_slices(own, mine):
    rows = own.shape[0] // 2
    crossed = row_cross(own, False)
    held = jnp.where(mine, own, crossed)
    first, second = held[:rows], held[rows:]
    first = jnp.concatenate([first, swap(first, Y_BIT)])
    second = jnp.concatenate([second, swap(second, X_BIT)])
    first_x = swap(first, X_BIT)
    second_y = swap(second, Y_BIT)
    pieces = {}
    for outer in range(2):
        cut = slice(outer * rows, (outer + 1) * rows)
        pieces[(outer * Y_BIT, 0)] = first[cut]
        pieces[(X_BIT + outer * Y_BIT, 0)] = first_x[cut]
        pieces[(outer * X_BIT, 1)] = second[cut]
        pieces[(Y_BIT + outer * X_BIT, 1)] = second_y[cut]
    return pieces


def lay_columns(pieces, index):
    rows, width = pieces[0].shape
    whole = jnp.zeros((16 * rows, width), LOW)
    for relative, piece in pieces.items():
        whole = lax.dynamic_update_slice(whole, piece, (rows * (index ^ relative), 0))
    return whole


def lay_rows(pieces, index):
    rows, width = pieces[(0, 0)].shape
    whole = jnp.zeros((8 * rows, width), LOW)
    for (relative, half), piece in pieces.items():
        place = ((index ^ relative) % 4) * 2 + half
        whole = lax.dynamic_update_slice(whole, piece, (rows * place, 0))
    return whole


def add_low(left, right):
    return (left.astype(jnp.float32) + right.astype(jnp.float32)).astype(LOW)


def scatter_column_slices(grad_low, index):
    rows = grad_low.shape[0] // 16

    def piece(relative):
        return lax.dynamic_slice_in_dim(grad_low, rows * (index ^ relative), rows)

    def four(base, outer):
        return jnp.concatenate(
            [piece(base + o * outer + r_h * H_BIT) for o in range(2) for r_h in range(2)]
        )

    first = add_low(four(0, Y_BIT), swap(four(X_BIT, Y_BIT), X_BIT))
    second = add_low(four(P_BIT, X_BIT), swap(four(P_BIT + Y_BIT, X_BIT), Y_BIT))
    first = add_low(first[: 2 * rows], swap(first[2 * rows :], Y_BIT))
    second = add_low(second[: 2 * rows], swap(second[2 * rows :], X_BIT))
    near = jnp.concatenate([first[:rows], second[:rows]])
    far = jnp.concatenate([first[rows:], second[rows:]])
    near = add_low(near, swap(far, H_BIT))
    return near[:rows], swap(near[rows:], P_BIT)


def scatter_row_slices(grad_low, index, mine):
    rows = grad_low.shape[0] // 8

    def piece(relative, half):
        place = ((index ^ relative) % 4) * 2 + half
        return lax.dynamic_slice_in_dim(grad_low, rows * place, rows)

    def two(base, outer, half):
        return jnp.concatenate([piece(base, half), piece(base + outer, half)])

    first = add_low(two(0, Y_BIT, 0), swap(two(X_BIT, Y_BIT, 0), X_BIT))
    second = add_low(two(0, X_BIT, 1), swap(two(Y_BIT, X_BIT, 1), Y_BIT))
    first = add_low(first[:rows], swap(first[rows:], Y_BIT))
    second = add_low(second[:rows], swap(second[rows:], X_BIT))
    held = jnp.concatenate([first, second])
    crossed = row_cross(held, True)
    summed = add_low(held, crossed)
    pairs = [(i * 2 + h_of(i), i * 2 + 1 - h_of(i)) for i in range(16)]
    return jnp.where(mine, summed, lax.ppermute(summed, ("dp", "ctx"), pairs))


def join_column_slices(own, partner, p_index, core):
    low_pair = jnp.where(p_index == 0, own, partner)
    high_pair = jnp.where(p_index == 0, partner, own)
    pair = jnp.stack([low_pair, high_pair])
    other = swap_core(pair)
    lower = jnp.where(core == 0, pair, other)
    upper = jnp.where(core == 0, other, pair)
    return [lower[0], lower[1], upper[0], upper[1]]


def gather_tokens(own):
    same = jnp.stack([own, swap(own, P_BIT)])
    return same, swap_core(same)


def sum_tokens(same, sibling):
    pair = same + swap_core(sibling.astype(LOW)).astype(jnp.float32)
    return pair[0] + swap(pair[1].astype(LOW), P_BIT).astype(jnp.float32)


def sequences(same, sibling):
    return jnp.stack([same, sibling], axis=1).reshape(2, 2 * same.shape[1], same.shape[2])


def halves(values):
    shaped = values.reshape(2, 2, -1, values.shape[-1])
    return shaped[:, 0], shaped[:, 1]


def fast_body(
    hidden_in,
    cotangent,
    block_order,
    w_query,
    key_weight,
    value_weight,
    w_output,
    w_gate,
    w_up,
    w_down,
    norm_gains,
    momentum_query,
    key_momentum,
    value_momentum,
    momentum_output,
    momentum_gate,
    momentum_up,
    momentum_down,
    momentum_gains,
):
    index = lax.axis_index("dp")
    core = lax.axis_index("ctx")
    p_index = (index // P_BIT) % 2
    mine = h_of(index) == core
    slice_own = 2 * core + p_index
    slice_give = 2 * core + 1 - p_index

    def column_slice(weight, which):
        size = weight.shape[1] // 4
        return lax.dynamic_slice_in_dim(weight, which * size, size, axis=1).astype(LOW)

    def column_pack(weights, which):
        return jnp.concatenate([column_slice(weight, which) for weight in weights], axis=1)

    gains = norm_gains.astype(LOW)[None]
    for bit in (P_BIT, H_BIT, Y_BIT, X_BIT):
        gains = jnp.concatenate([gains, swap(gains, bit)])
    order = [0]
    for bit in (P_BIT, H_BIT, Y_BIT, X_BIT):
        order = order + [o ^ bit for o in order]
    place = jnp.zeros((16,), jnp.int32)
    inverse = [0] * 16
    for at, relative in enumerate(order):
        inverse[relative] = at
    lookup = jnp.array(inverse, jnp.int32)[index ^ jnp.arange(16)]
    gains_all = jnp.take(gains, lookup, axis=0).reshape(-1).astype(jnp.float32)

    width = hidden_in.shape[2]
    head_size = (gains_all.shape[0] - 2 * width) // 2
    gain_attn = gains_all[:width]
    gain_mlp = gains_all[width : 2 * width]
    gain_query = gains_all[2 * width : 2 * width + head_size]
    gain_key = gains_all[2 * width + head_size :]

    qkv = (w_query, key_weight, value_weight)
    qkv_mat = lay_columns(
        gather_column_slices(column_pack(qkv, slice_own), column_pack(qkv, slice_give)), index
    )
    output_mat = lay_rows(gather_row_slices(w_output.astype(LOW), mine), index)
    gate_up = (w_gate, w_up)
    gate_up_mat = lay_columns(
        gather_column_slices(column_pack(gate_up, slice_own), column_pack(gate_up, slice_give)),
        index,
    )
    down_mat = lay_rows(gather_row_slices(w_down.astype(LOW), mine), index)

    tokens_own = hidden_in[0]
    count = tokens_own.shape[0]
    block = count // 2
    orders = jnp.concatenate([block_order, swap(block_order, P_BIT)])
    orders = jnp.where(core == 0, orders, jnp.roll(orders, 2, axis=1))
    positions = (orders[:, :, None] * block + jnp.arange(block, dtype=jnp.int32)).reshape(2, -1)
    cosine, sine_table = rotary_tables(positions.reshape(-1), head_size)

    tokens_f = tokens_own.astype(jnp.float32)
    normed_f, norm_pull = jax.vjp(rms_norm, tokens_f, gain_attn)
    normed = sequences(*gather_tokens(normed_f.astype(LOW))).reshape(-1, width)
    grad_out = sequences(*gather_tokens(cotangent[0])).reshape(-1, width)

    query_width = w_query.shape[1] // 4
    kv_width = key_weight.shape[1] // 4
    projected = matmul(normed, qkv_mat)
    query_pre = projected[:, :query_width]
    key_pre = projected[:, query_width : query_width + kv_width]
    value_low = projected[:, query_width + kv_width :].astype(LOW)

    def prep(projected_part, gain_vec):
        return head_prep(projected_part, gain_vec, cosine, sine_table)

    query_rot, query_pull = jax.vjp(prep, query_pre, gain_query)
    key_rot, key_pull = jax.vjp(prep, key_pre, gain_key)
    kv_heads = kv_width // head_size
    query_low = query_rot.astype(LOW).reshape(2, 2 * count, kv_heads, 2, head_size)
    key_low = key_rot.astype(LOW).reshape(2, 2 * count, kv_heads, head_size)
    value_low = value_low.reshape(2, 2 * count, kv_heads, head_size)
    scaling = head_size ** (-0.5)
    scores = scaling * jnp.einsum(
        "sqgrd,skgd->sgrqk", query_low, key_low, preferred_element_type=jnp.float32
    )
    allowed = positions[:, :, None] >= positions[:, None, :]
    scores = jnp.where(allowed[:, None, None], scores, -1e30)
    weights = jnp.exp(scores - jnp.max(scores, axis=-1, keepdims=True))
    probs = weights / jnp.sum(weights, axis=-1, keepdims=True)
    probs_low = probs.astype(LOW)
    mixture = jnp.einsum(
        "sgrqk,skgd->sqgrd", probs_low, value_low, preferred_element_type=jnp.float32
    )
    mixed_low = mixture.reshape(2 * 2 * count, -1).astype(LOW)
    attended = sum_tokens(*halves(matmul(mixed_low, output_mat)))
    middle = tokens_f + attended
    normed_two_f, norm_two_pull = jax.vjp(rms_norm, middle, gain_mlp)
    normed_two = sequences(*gather_tokens(normed_two_f.astype(LOW))).reshape(-1, width)
    gate_up_act = matmul(normed_two, gate_up_mat)
    hidden_units = gate_up_act.shape[1] // 2
    active_f, swiglu_pull = jax.vjp(
        lambda gate_in, up_in: jax.nn.silu(gate_in) * up_in,
        gate_up_act[:, :hidden_units],
        gate_up_act[:, hidden_units:],
    )
    active = active_f.astype(LOW)
    grad_down = contract_rows(active, grad_out).astype(LOW)
    grad_active = contract_cols(grad_out, down_mat)
    grad_gate_up = jnp.concatenate(
        [part.astype(LOW) for part in swiglu_pull(grad_active)], axis=1
    )
    grad_gate_up_mat = contract_rows(normed_two, grad_gate_up).astype(LOW)
    grad_normed_two = sum_tokens(*halves(contract_cols(grad_gate_up, gate_up_mat)))
    layer_sum = sum_tokens(*halves(matmul(active, down_mat)))
    layer_out = (middle + layer_sum).astype(LOW)[None]

    grad_middle_norm, grad_gain_mlp = norm_two_pull(grad_normed_two)
    grad_middle = cotangent[0].astype(jnp.float32) + grad_middle_norm
    grad_branch = sequences(*gather_tokens(grad_middle.astype(LOW))).reshape(-1, width)
    grad_output_mat = contract_rows(mixed_low, grad_branch).astype(LOW)
    grad_mixed = contract_cols(grad_branch, output_mat).astype(LOW)
    grad_mixed = grad_mixed.reshape(2, 2 * count, kv_heads, 2, head_size)
    grad_values = jnp.einsum(
        "sgrqk,sqgrd->skgd", probs_low, grad_mixed, preferred_element_type=jnp.float32
    )
    grad_probs = jnp.einsum(
        "sqgrd,skgd->sgrqk", grad_mixed, value_low, preferred_element_type=jnp.float32
    )
    inner = jnp.sum(probs * grad_probs, axis=-1, keepdims=True)
    grad_scores = (probs * (grad_probs - inner)).astype(LOW)
    grad_query_rot = scaling * jnp.einsum(
        "sgrqk,skgd->sqgrd", grad_scores, key_low, preferred_element_type=jnp.float32
    )
    grad_key_rot = scaling * jnp.einsum(
        "sgrqk,sqgrd->skgd", grad_scores, query_low, preferred_element_type=jnp.float32
    )
    grad_query_pre, grad_gain_query = query_pull(grad_query_rot.reshape(query_rot.shape))
    grad_key_pre, grad_gain_key = key_pull(grad_key_rot.reshape(key_rot.shape))
    grad_qkv = jnp.concatenate(
        [
            grad_query_pre.astype(LOW),
            grad_key_pre.astype(LOW),
            grad_values.reshape(-1, kv_width).astype(LOW),
        ],
        axis=1,
    )
    grad_qkv_mat = contract_rows(normed, grad_qkv).astype(LOW)
    grad_normed = sum_tokens(*halves(contract_cols(grad_qkv, qkv_mat)))
    grad_tokens_norm, grad_gain_attn = norm_pull(grad_normed)
    input_grad = (grad_middle + grad_tokens_norm).astype(LOW)[None]

    grad_gains = jnp.concatenate([grad_gain_attn, grad_gain_mlp, grad_gain_query, grad_gain_key])
    grad_gains = grad_gains.reshape(16, -1)
    grad_gains = grad_gains + swap_core(grad_gains.astype(LOW)).astype(jnp.float32)
    for bit in (P_BIT, H_BIT, Y_BIT, X_BIT):
        grad_gains = grad_gains + swap(grad_gains.astype(LOW), bit).astype(jnp.float32)
    grad_gains = lax.dynamic_index_in_dim(grad_gains, index, keepdims=False)

    down_sum = scatter_row_slices(grad_down, index, mine)
    gate_up_sum = join_column_slices(
        *scatter_column_slices(grad_gate_up_mat, index), p_index, core
    )
    output_sum = scatter_row_slices(grad_output_mat, index, mine)
    qkv_sum = join_column_slices(*scatter_column_slices(grad_qkv_mat, index), p_index, core)

    def columns(parts, start, size):
        return jnp.concatenate([part[:, start : start + size] for part in parts], axis=1)

    sums = (
        columns(qkv_sum, 0, query_width),
        columns(qkv_sum, query_width, kv_width),
        columns(qkv_sum, query_width + kv_width, kv_width),
        output_sum,
        columns(gate_up_sum, 0, hidden_units),
        columns(gate_up_sum, hidden_units, hidden_units),
        down_sum,
        grad_gains,
    )
    masters = (w_query, key_weight, value_weight, w_output, w_gate, w_up, w_down, norm_gains)
    moments = (
        momentum_query,
        key_momentum,
        value_momentum,
        momentum_output,
        momentum_gate,
        momentum_up,
        momentum_down,
        momentum_gains,
    )
    norm_scale = lax.rsqrt(jnp.float32(16 * 2 * count))
    summed = tuple(part.astype(jnp.float32) for part in sums)
    updates, new_moments = lion_step(masters, moments, summed, norm_scale)
    return (layer_out, input_grad) + tuple(updates) + tuple(new_moments)


def solution(mesh):
    body = fast_body if dict(mesh.shape) == {"dp": 16, "ctx": 2} else general_body
    return jax.shard_map(
        body,
        mesh=mesh,
        in_specs=(
            P("dp", "ctx", None),
            P("dp", "ctx", None),
            P("dp", None),
            P("dp", None),
            P("dp", None),
            P("dp", None),
            P("dp", None),
            P("dp", None),
            P("dp", None),
            P("dp", None),
            P("dp"),
            P("dp", None),
            P("dp", None),
            P("dp", None),
            P("dp", None),
            P("dp", None),
            P("dp", None),
            P("dp", None),
            P("dp"),
        ),
        out_specs=(
            P("dp", "ctx", None),
            P("dp", "ctx", None),
            P("dp", None),
            P("dp", None),
            P("dp", None),
            P("dp", None),
            P("dp", None),
            P("dp", None),
            P("dp", None),
            P("dp"),
            P("dp", None),
            P("dp", None),
            P("dp", None),
            P("dp", None),
            P("dp", None),
            P("dp", None),
            P("dp", None),
            P("dp"),
        ),
        check_vma=False,
    )
```

```python
import jax
import jax.numpy as jnp
from jax import lax
from jax.experimental import pallas as pl
from jax.experimental.pallas import tpu as pltpu
from jax.sharding import PartitionSpec as P

EPSILON = 1e-06
THETA = 1000000.0
BETA_ONE = 0.9
BETA_TWO = 0.5
SOFTEN = 0.005
DECAY_FACTOR = 1.0


def rms_norm(values, gain_vec):
    return (
        values * lax.rsqrt(jnp.mean(values * values, axis=-1, keepdims=True) + EPSILON) * gain_vec
    )


def rotary_tables(positions, head_size):
    half_size = head_size // 2
    frequency = THETA ** (-(jnp.arange(half_size, dtype=jnp.float32) * 2.0 / head_size))
    angles = positions.astype(jnp.float32)[:, None] * frequency[None, :]
    angles = jnp.concatenate([angles, angles], axis=1)
    return (jnp.cos(angles), jnp.sin(angles))


def rotate(values, cosine, sine_table):
    half_size = values.shape[-1] // 2
    turned = jnp.concatenate([-values[..., half_size:], values[..., :half_size]], axis=-1)
    return values * cosine[:, None, :] + turned * sine_table[:, None, :]


def head_prep(projected, gain_vec, cosine, sine_table):
    shaped = projected.reshape(projected.shape[0], -1, gain_vec.shape[0])
    return rotate(rms_norm(shaped, gain_vec), cosine, sine_table)


def matmul(left, right):
    return jnp.dot(left, right, preferred_element_type=jnp.float32)


def contract_rows(left, right):
    return lax.dot_general(
        left, right, (((0,), (0,)), ((), ())), preferred_element_type=jnp.float32
    )


def contract_cols(left, right):
    return lax.dot_general(
        left, right, (((1,), (1,)), ((), ())), preferred_element_type=jnp.float32
    )


def head_scores(queries, key_row_block, query_pos, key_pos):
    scaling = queries.shape[-1] ** (-0.5)
    scores = (
        jnp.einsum("trd,kd->rtk", queries, key_row_block, preferred_element_type=jnp.float32)
        * scaling
    )
    allowed = query_pos[:, None] >= key_pos[None, :]
    return jnp.where(allowed[None], scores, -1e30)


def attend_head(query_pos, key_pos):

    def attend(group_item):
        queries, key_row_block, value_row_block = group_item
        scores = head_scores(queries, key_row_block, query_pos, key_pos)
        row_top = jnp.max(scores, axis=-1, keepdims=True)
        weights = jnp.exp(scores - row_top)
        row_total = jnp.sum(weights, axis=-1, keepdims=True)
        probs_low = (weights / row_total).astype(jnp.bfloat16)
        mixture = jnp.einsum(
            "rtk,kd->trd", probs_low, value_row_block, preferred_element_type=jnp.float32
        )
        return (mixture, (row_top + jnp.log(row_total))[..., 0])

    return attend


def attend_back(query_pos, key_pos):

    def backward(group_item):
        queries, key_row_block, value_row_block, grad_mix, log_total = group_item
        scaling = queries.shape[-1] ** (-0.5)
        scores = head_scores(queries, key_row_block, query_pos, key_pos)
        probs = jnp.exp(scores - log_total[..., None])
        grad_values = jnp.einsum(
            "rtk,trd->kd", probs.astype(jnp.bfloat16), grad_mix, preferred_element_type=jnp.float32
        )
        grad_probs = jnp.einsum(
            "trd,kd->rtk", grad_mix, value_row_block, preferred_element_type=jnp.float32
        )
        inner = jnp.sum(probs * grad_probs, axis=-1, keepdims=True)
        grad_scores = (probs * (grad_probs - inner)).astype(jnp.bfloat16)
        grad_queries = (
            jnp.einsum(
                "rtk,kd->trd", grad_scores, key_row_block, preferred_element_type=jnp.float32
            )
            * scaling
        )
        grad_keys = (
            jnp.einsum("rtk,trd->kd", grad_scores, queries, preferred_element_type=jnp.float32)
            * scaling
        )
        return (grad_queries, grad_keys, grad_values)

    return backward


def lion_step(masters, moments, gradients, norm_scale):
    updates = []
    new_moments = []
    for tensor_index in range(8):
        scaled = gradients[tensor_index] * norm_scale
        moment_arr = moments[tensor_index]
        blend_arr = BETA_ONE * moment_arr + (1.0 - BETA_ONE) * scaled
        direction = blend_arr / jnp.sqrt(blend_arr * blend_arr + SOFTEN)
        decay_here = DECAY_FACTOR if tensor_index < 7 else 0.0
        updates.append(direction + decay_here * masters[tensor_index])
        new_moments.append(BETA_TWO * moment_arr + (1.0 - BETA_TWO) * scaled)
    return (updates, new_moments)


def general_body(
    hidden_in,
    cotangent,
    block_order,
    w_query,
    key_weight,
    value_weight,
    w_output,
    w_gate,
    w_up,
    w_down,
    norm_gains,
    momentum_query,
    key_momentum,
    value_momentum,
    momentum_output,
    momentum_gate,
    momentum_up,
    momentum_down,
    momentum_gains,
):
    copies = (
        lax.all_gather(w_query.astype(jnp.bfloat16), "dp", axis=0, tiled=True),
        lax.all_gather(key_weight.astype(jnp.bfloat16), "dp", axis=0, tiled=True),
        lax.all_gather(value_weight.astype(jnp.bfloat16), "dp", axis=0, tiled=True),
        lax.all_gather(w_output.astype(jnp.bfloat16), "dp", axis=0, tiled=True),
        lax.all_gather(w_gate.astype(jnp.bfloat16), "dp", axis=0, tiled=True),
        lax.all_gather(w_up.astype(jnp.bfloat16), "dp", axis=0, tiled=True),
        lax.all_gather(w_down.astype(jnp.bfloat16), "dp", axis=0, tiled=True),
        lax.all_gather(norm_gains.astype(jnp.bfloat16), "dp", axis=0, tiled=True),
    )
    query_mat, key_mat, value_mat, output_mat, gate_mat, up_mat, down_mat, gains_low = copies
    gains_all = gains_low.astype(jnp.float32)
    width = hidden_in.shape[2]
    head_size = (gains_all.shape[0] - 2 * width) // 2
    kv_heads = key_mat.shape[1] // head_size
    query_heads = query_mat.shape[1] // head_size
    group_repeat_count = query_heads // kv_heads
    gain_attn = gains_all[:width]
    gain_mlp = gains_all[width : 2 * width]
    gain_query = gains_all[2 * width : 2 * width + head_size]
    gain_key = gains_all[2 * width + head_size :]
    tokens_in = hidden_in[0]
    token_count = tokens_in.shape[0]
    block_size = token_count // 2
    slot_order = block_order[0]
    key_pos = (
        slot_order[:, None] * block_size + jnp.arange(block_size, dtype=jnp.int32)[None, :]
    ).reshape(-1)
    query_pos = lax.dynamic_slice_in_dim(key_pos, lax.axis_index("ctx") * token_count, token_count)
    cosine, sine_table = rotary_tables(query_pos, head_size)
    tokens_f = tokens_in.astype(jnp.float32)
    normed_f, norm_pull = jax.vjp(rms_norm, tokens_f, gain_attn)
    normalized_input = normed_f.astype(jnp.bfloat16)
    query_pre = matmul(normalized_input, query_mat)
    key_pre = matmul(normalized_input, key_mat)
    value_low = matmul(normalized_input, value_mat).astype(jnp.bfloat16)
    query_rot, query_pull = jax.vjp(
        lambda projected, gain_vec: head_prep(projected, gain_vec, cosine, sine_table),
        query_pre,
        gain_query,
    )
    key_rot, key_pull = jax.vjp(
        lambda projected, gain_vec: head_prep(projected, gain_vec, cosine, sine_table),
        key_pre,
        gain_key,
    )
    query_low = query_rot.astype(jnp.bfloat16)
    key_heads = key_rot.astype(jnp.bfloat16).transpose(1, 0, 2)
    value_heads = value_low.reshape(token_count, kv_heads, head_size).transpose(1, 0, 2)
    gathered = (
        lax.all_gather(key_heads, "ctx", axis=1, tiled=True),
        lax.all_gather(value_heads, "ctx", axis=1, tiled=True),
    )
    query_groups = query_low.reshape(
        token_count, kv_heads, group_repeat_count, head_size
    ).transpose(1, 0, 2, 3)
    mixture, log_total = lax.map(
        attend_head(query_pos, key_pos), (query_groups, gathered[0], gathered[1])
    )
    mixed_low = mixture.transpose(1, 0, 2, 3).reshape(token_count, -1).astype(jnp.bfloat16)
    middle = tokens_f + matmul(mixed_low, output_mat)
    normed_two_f, norm_two_pull = jax.vjp(rms_norm, middle, gain_mlp)
    normed_two = normed_two_f.astype(jnp.bfloat16)
    gate_act = matmul(normed_two, gate_mat)
    upward = matmul(normed_two, up_mat)
    active_f, swiglu_pull = jax.vjp(
        lambda gate_in, up_in: jax.nn.silu(gate_in) * up_in, gate_act, upward
    )
    active = active_f.astype(jnp.bfloat16)
    layer_out = (middle + matmul(active, down_mat)).astype(jnp.bfloat16)[None]
    grad_out = cotangent[0]
    grad_down = contract_rows(active, grad_out)
    grad_active = contract_cols(grad_out, down_mat)
    grad_gate_f, grad_up_f = swiglu_pull(grad_active)
    grad_gate = grad_gate_f.astype(jnp.bfloat16)
    grad_upward = grad_up_f.astype(jnp.bfloat16)
    grad_gate_mat = contract_rows(normed_two, grad_gate)
    grad_up_mat = contract_rows(normed_two, grad_upward)
    grad_normed_two = contract_cols(grad_gate, gate_mat) + contract_cols(grad_upward, up_mat)
    grad_middle_norm, grad_gain_mlp = norm_two_pull(grad_normed_two)
    grad_middle = grad_out.astype(jnp.float32) + grad_middle_norm
    grad_branch = grad_middle.astype(jnp.bfloat16)
    grad_output_mat = contract_rows(mixed_low, grad_branch)
    grad_mixed = contract_cols(grad_branch, output_mat).astype(jnp.bfloat16)
    grad_groups = grad_mixed.reshape(
        token_count, kv_heads, group_repeat_count, head_size
    ).transpose(1, 0, 2, 3)
    grad_query_groups, grad_key_all, grad_value_all = lax.map(
        attend_back(query_pos, key_pos),
        (query_groups, gathered[0], gathered[1], grad_groups, log_total),
    )
    grad_key_own, grad_value_own = (
        lax.psum_scatter(
            grad_key_all.astype(jnp.bfloat16), "ctx", scatter_dimension=1, tiled=True
        ).astype(jnp.float32),
        lax.psum_scatter(
            grad_value_all.astype(jnp.bfloat16), "ctx", scatter_dimension=1, tiled=True
        ).astype(jnp.float32),
    )
    grad_query_rot = grad_query_groups.transpose(1, 0, 2, 3).reshape(
        token_count, query_heads, head_size
    )
    grad_query_pre, grad_gain_query = query_pull(grad_query_rot)
    grad_key_pre, grad_gain_key = key_pull(grad_key_own.transpose(1, 0, 2))
    grad_query_low = grad_query_pre.astype(jnp.bfloat16)
    grad_key_low = grad_key_pre.astype(jnp.bfloat16)
    grad_value_low = grad_value_own.transpose(1, 0, 2).reshape(token_count, -1).astype(jnp.bfloat16)
    grad_query_mat = contract_rows(normalized_input, grad_query_low)
    grad_key_mat = contract_rows(normalized_input, grad_key_low)
    grad_value_mat = contract_rows(normalized_input, grad_value_low)
    grad_normed = (
        contract_cols(grad_query_low, query_mat)
        + contract_cols(grad_key_low, key_mat)
        + contract_cols(grad_value_low, value_mat)
    )
    grad_tokens_norm, grad_gain_attn = norm_pull(grad_normed)
    input_grad = (grad_middle + grad_tokens_norm).astype(jnp.bfloat16)[None]
    grad_gains = jnp.concatenate([grad_gain_attn, grad_gain_mlp, grad_gain_query, grad_gain_key])
    masters = (w_query, key_weight, value_weight, w_output, w_gate, w_up, w_down, norm_gains)
    moments = (
        momentum_query,
        key_momentum,
        value_momentum,
        momentum_output,
        momentum_gate,
        momentum_up,
        momentum_down,
        momentum_gains,
    )
    token_total = lax.axis_size("dp") * key_pos.shape[0]
    norm_scale = lax.rsqrt(jnp.float32(token_total))
    shares = (
        lax.psum_scatter(
            grad_query_mat.astype(jnp.bfloat16), "dp", scatter_dimension=0, tiled=True
        ).astype(jnp.float32),
        lax.psum_scatter(
            grad_key_mat.astype(jnp.bfloat16), "dp", scatter_dimension=0, tiled=True
        ).astype(jnp.float32),
        lax.psum_scatter(
            grad_value_mat.astype(jnp.bfloat16), "dp", scatter_dimension=0, tiled=True
        ).astype(jnp.float32),
        lax.psum_scatter(
            grad_output_mat.astype(jnp.bfloat16), "dp", scatter_dimension=0, tiled=True
        ).astype(jnp.float32),
        lax.psum_scatter(
            grad_gate_mat.astype(jnp.bfloat16), "dp", scatter_dimension=0, tiled=True
        ).astype(jnp.float32),
        lax.psum_scatter(
            grad_up_mat.astype(jnp.bfloat16), "dp", scatter_dimension=0, tiled=True
        ).astype(jnp.float32),
        lax.psum_scatter(
            grad_down.astype(jnp.bfloat16), "dp", scatter_dimension=0, tiled=True
        ).astype(jnp.float32),
        lax.psum_scatter(
            grad_gains.astype(jnp.bfloat16), "dp", scatter_dimension=0, tiled=True
        ).astype(jnp.float32),
    )
    summed = (
        lax.psum(shares[0].astype(jnp.bfloat16), "ctx").astype(jnp.float32),
        lax.psum(shares[1].astype(jnp.bfloat16), "ctx").astype(jnp.float32),
        lax.psum(shares[2].astype(jnp.bfloat16), "ctx").astype(jnp.float32),
        lax.psum(shares[3].astype(jnp.bfloat16), "ctx").astype(jnp.float32),
        lax.psum(shares[4].astype(jnp.bfloat16), "ctx").astype(jnp.float32),
        lax.psum(shares[5].astype(jnp.bfloat16), "ctx").astype(jnp.float32),
        lax.psum(shares[6].astype(jnp.bfloat16), "ctx").astype(jnp.float32),
        lax.psum(shares[7].astype(jnp.bfloat16), "ctx").astype(jnp.float32),
    )
    updates, new_moments = lion_step(masters, moments, summed, norm_scale)
    return (layer_out, input_grad) + tuple(updates) + tuple(new_moments)


X_BIT, Y_BIT, P_BIT, H_BIT = 1, 2, 4, 8
LOW = jnp.bfloat16
WIDE = jnp.float32
VMEM_BYTES = 48 * 1024 * 1024
COLUMN_GROUPS = ((0, Y_BIT), (X_BIT, Y_BIT), (P_BIT, X_BIT), (P_BIT + Y_BIT, X_BIT))
ROW_GROUPS = ((0, Y_BIT, 0), (X_BIT, Y_BIT, 0), (0, X_BIT, 1), (Y_BIT, X_BIT, 1))


def swap(values, bit):
    return lax.ppermute(values, "dp", [(i, i ^ bit) for i in range(16)])


def swap_core(values):
    return lax.ppermute(values, "ctx", [(0, 1), (1, 0)])


def h_of(index):
    return (index // H_BIT) % 2


def row_cross(values, to_owner):
    pairs = []
    for index in range(16):
        for core in range(2):
            if (core == h_of(index)) != to_owner:
                pairs.append((index * 2 + core, (index ^ H_BIT) * 2 + core))
    return lax.ppermute(values, ("dp", "ctx"), pairs)


def gather_column_slices(own, give):
    rows = own.shape[0]
    got = swap(give, P_BIT)
    far = swap(jnp.concatenate([own, got]), H_BIT)
    first = jnp.concatenate([own, far[:rows]])
    second = jnp.concatenate([got, far[rows:]])
    first = jnp.concatenate([first, swap(first, Y_BIT)])
    second = jnp.concatenate([second, swap(second, X_BIT)])
    return first, swap(first, X_BIT), second, swap(second, Y_BIT)


def gather_row_slices(own, mine):
    rows = own.shape[0] // 2
    held = jnp.where(mine, own, row_cross(own, False))
    first, second = held[:rows], held[rows:]
    first = jnp.concatenate([first, swap(first, Y_BIT)])
    second = jnp.concatenate([second, swap(second, X_BIT)])
    return first, swap(first, X_BIT), second, swap(second, Y_BIT)


def add_low(left, right):
    return (left.astype(WIDE) + right.astype(WIDE)).astype(LOW)


def scatter_column_slices(keep_one, send_one, keep_two, send_two):
    rows = keep_one.shape[0] // 4
    first = add_low(keep_one, swap(send_one, X_BIT))
    second = add_low(keep_two, swap(send_two, Y_BIT))
    first = add_low(first[: 2 * rows], swap(first[2 * rows :], Y_BIT))
    second = add_low(second[: 2 * rows], swap(second[2 * rows :], X_BIT))
    near = jnp.concatenate([first[:rows], second[:rows]])
    far = jnp.concatenate([first[rows:], second[rows:]])
    near = add_low(near, swap(far, H_BIT))
    return near[:rows], swap(near[rows:], P_BIT)


def scatter_row_slices(keep_one, send_one, keep_two, send_two, mine):
    rows = keep_one.shape[0] // 2
    first = add_low(keep_one, swap(send_one, X_BIT))
    second = add_low(keep_two, swap(send_two, Y_BIT))
    first = add_low(first[:rows], swap(first[rows:], Y_BIT))
    second = add_low(second[:rows], swap(second[rows:], X_BIT))
    held = jnp.concatenate([first, second])
    summed = add_low(held, row_cross(held, True))
    pairs = [(i * 2 + h_of(i), i * 2 + 1 - h_of(i)) for i in range(16)]
    return jnp.where(mine, summed, lax.ppermute(summed, ("dp", "ctx"), pairs))


def join_column_slices(own, partner, p_index, core):
    low_pair = jnp.where(p_index == 0, own, partner)
    high_pair = jnp.where(p_index == 0, partner, own)
    pair = jnp.stack([low_pair, high_pair])
    other = swap_core(pair)
    lower = jnp.where(core == 0, pair, other)
    upper = jnp.where(core == 0, other, pair)
    return [lower[0], lower[1], upper[0], upper[1]]


def gather_tokens(own):
    same = jnp.stack([own, swap(own, P_BIT)])
    return same, swap_core(same)


def sum_tokens(same, sibling):
    pair = same.astype(WIDE) + swap_core(sibling).astype(WIDE)
    return pair[0] + swap(pair[1].astype(LOW), P_BIT).astype(WIDE)


VM = pl.BlockSpec(memory_space=pltpu.VMEM)
SM = pl.BlockSpec(memory_space=pltpu.SMEM)
HB = pl.BlockSpec(memory_space=pl.ANY)


def call(kernel, in_specs, outs, out_specs, scratch, flops, moved):
    return pl.pallas_call(
        kernel,
        in_specs=in_specs,
        out_specs=out_specs,
        out_shape=[jax.ShapeDtypeStruct(shape, dtype) for shape, dtype in outs],
        scratch_shapes=scratch,
        compiler_params=pltpu.CompilerParams(vmem_limit_bytes=VMEM_BYTES),
        cost_estimate=pl.CostEstimate(flops=flops, bytes_accessed=moved, transcendentals=0),
    )


def column_copies(index, parts, whole, sems, outward):
    copies = []
    rows = whole.shape[0] // 16
    for part, (base, outer) in zip(parts, COLUMN_GROUPS):
        for place in range(4):
            relative = base + (place // 2) * outer + (place % 2) * H_BIT
            start = pl.multiple_of((index ^ relative) * rows, rows)
            block = part.at[pl.ds(place * rows, rows)]
            inside = whole.at[pl.ds(start, rows)]
            ends = (inside, block) if outward else (block, inside)
            copies.append(pltpu.make_async_copy(*ends, sems.at[len(copies)]))
    return copies


def row_copies(index, parts, whole, sems, outward):
    copies = []
    rows = whole.shape[0] // 8
    for part, (base, outer, half) in zip(parts, ROW_GROUPS):
        for place in range(2):
            relative = base + place * outer
            start = pl.multiple_of((((index ^ relative) % 4) * 2 + half) * rows, rows)
            block = part.at[pl.ds(place * rows, rows)]
            inside = whole.at[pl.ds(start, rows)]
            ends = (inside, block) if outward else (block, inside)
            copies.append(pltpu.make_async_copy(*ends, sems.at[len(copies)]))
    return copies


def start_all(copies):
    for copy in copies:
        copy.start()


def wait_all(copies):
    for copy in copies:
        copy.wait()


def load_tokens(same, sibling):
    return jnp.concatenate([same[0], sibling[0], same[1], sibling[1]])


def store_tokens(values, same, sibling):
    count = same.shape[1]
    for sequence in range(2):
        at = 2 * count * sequence
        same[sequence] = values[at : at + count].astype(same.dtype)
        sibling[sequence] = values[at + count : at + 2 * count].astype(sibling.dtype)


def place_of(scalars, sequence, at):
    block = jnp.where(
        at < 128,
        jnp.where(at < 64, scalars[1 + 4 * sequence], scalars[2 + 4 * sequence]),
        jnp.where(at < 192, scalars[3 + 4 * sequence], scalars[4 + 4 * sequence]),
    )
    return block * 64 + at % 64


def allowed_of(scalars, sequence):
    rows = place_of(scalars, sequence, lax.broadcasted_iota(jnp.int32, (256, 1), 0))
    cols = place_of(scalars, sequence, lax.broadcasted_iota(jnp.int32, (1, 256), 1))
    return rows >= cols


def fill_tables(scalars, cosine, sine, cos_rows, sin_rows):
    for slot in range(8):
        start = pl.multiple_of(scalars[1 + slot] * 64, 64)
        cos_rows[slot * 64 : slot * 64 + 64] = cosine[pl.ds(start, 64)]
        sin_rows[slot * 64 : slot * 64 + 64] = sine[pl.ds(start, 64)]


def attend_kernel(
    scalars, same, sibling, part_a, part_b, part_c, part_d, cosine, sine, gains,
    mixture, pre, rotated, values_out, log_total, whole, cos_rows, sin_rows, sems,
):
    copies = column_copies(scalars[0], (part_a, part_b, part_c, part_d), whole, sems, False)
    start_all(copies)
    fill_tables(scalars, cosine, sine, cos_rows, sin_rows)
    tokens = load_tokens(same, sibling)
    wait_all(copies)
    projected = matmul(tokens, whole[...])
    pre[...] = projected[:, :768]
    values_out[...] = projected[:, 768:].astype(LOW)
    for head in range(6):
        cut = slice(head * 128, head * 128 + 128)
        raw = pre[:, cut]
        gain = gains[0:1] if head < 4 else gains[1:2]
        scale = lax.rsqrt(jnp.mean(raw * raw, axis=-1, keepdims=True) + EPSILON)
        unit = raw * scale * gain
        turned = pltpu.roll(unit, 64, 1)
        rotated[:, cut] = (unit * cos_rows[...] + turned * sin_rows[...]).astype(LOW)
    for sequence in range(2):
        rows = slice(sequence * 256, sequence * 256 + 256)
        allowed = allowed_of(scalars, sequence)
        tops = []
        for head in range(4):
            group = head // 2
            queries = rotated[rows, head * 128 : head * 128 + 128]
            keys = rotated[rows, 512 + group * 128 : 640 + group * 128]
            scores = jnp.where(allowed, contract_cols(queries, keys) * (128**-0.5), -1e30)
            top = jnp.max(scores, axis=-1, keepdims=True)
            weights = jnp.exp(scores - top)
            total = jnp.sum(weights, axis=-1, keepdims=True)
            probs = (weights / total).astype(LOW)
            mixed = matmul(probs, values_out[rows, group * 128 : group * 128 + 128])
            mixture[rows, head * 128 : head * 128 + 128] = mixed.astype(LOW)
            tops.append(jnp.broadcast_to(top + jnp.log(total), (256, 128)))
        lane = lax.broadcasted_iota(jnp.int32, (256, 128), 1)
        log_total[rows] = jnp.where(
            lane < 2, jnp.where(lane < 1, tops[0], tops[1]), jnp.where(lane < 3, tops[2], tops[3])
        )


def attend(scalars, tokens, parts, tables, gains):
    return call(
        attend_kernel,
        [SM, VM, VM, HB, HB, HB, HB, VM, VM, VM],
        [((512, 512), LOW), ((512, 768), WIDE), ((512, 768), LOW), ((512, 256), LOW), ((512, 128), WIDE)],
        [VM] * 5,
        [
            pltpu.VMEM((1024, 1024), LOW),
            pltpu.VMEM((512, 128), WIDE),
            pltpu.VMEM((512, 128), WIDE),
            pltpu.SemaphoreType.DMA((16,)),
        ],
        2 * 10**9,
        8 * 10**6,
    )(scalars, *tokens, *parts, *tables, gains)


def output_kernel(scalars, mixture, part_a, part_b, part_c, part_d, same, sibling, whole, sems):
    copies = row_copies(scalars[0], (part_a, part_b, part_c, part_d), whole, sems, False)
    start_all(copies)
    wait_all(copies)
    store_tokens(matmul(mixture[...], whole[...]), same, sibling)


def row_product(scalars, left, parts):
    depth = left.shape[1]
    return call(
        output_kernel,
        [SM, VM, HB, HB, HB, HB],
        [((2, 128, 1024), LOW)] * 2,
        [VM] * 2,
        [pltpu.VMEM((depth, 1024), LOW), pltpu.SemaphoreType.DMA((8,))],
        2 * 512 * 1024 * depth,
        4 * 10**6,
    )(scalars, left, *parts)


def gate_kernel(
    scalars, same, sibling, part_a, part_b, part_c, part_d, gate_up, active, whole, sems
):
    copies = column_copies(scalars[0], (part_a, part_b, part_c, part_d), whole, sems, False)
    start_all(copies)
    tokens = load_tokens(same, sibling)
    wait_all(copies)
    for at in range(0, 768, 256):
        gate = matmul(tokens, whole[:, at : at + 256])
        upward = matmul(tokens, whole[:, 768 + at : 1024 + at])
        gate_up[:, at : at + 256] = gate
        gate_up[:, 768 + at : 1024 + at] = upward
        active[:, at : at + 256] = (gate * jax.nn.sigmoid(gate) * upward).astype(LOW)


def gate_product(scalars, tokens, parts):
    return call(
        gate_kernel,
        [SM, VM, VM, HB, HB, HB, HB],
        [((512, 1536), WIDE), ((512, 768), LOW)],
        [VM] * 2,
        [pltpu.VMEM((1024, 1536), LOW), pltpu.SemaphoreType.DMA((16,))],
        2 * 512 * 1024 * 1536,
        10 * 10**6,
    )(scalars, *tokens, *parts)


def swiglu_back_kernel(
    scalars, same, sibling, gate_up, row_a, row_b, row_c, row_d, col_a, col_b, col_c, col_d,
    grad_gate_up, grad_same, grad_sibling, down, both, row_sems, col_sems,
):
    down_copies = row_copies(scalars[0], (row_a, row_b, row_c, row_d), down, row_sems, False)
    both_copies = column_copies(scalars[0], (col_a, col_b, col_c, col_d), both, col_sems, False)
    start_all(down_copies)
    start_all(both_copies)
    grad_out = load_tokens(same, sibling)
    wait_all(down_copies)
    for at in range(0, 768, 256):
        grad_active = contract_cols(grad_out, down[at : at + 256])
        gate = gate_up[:, at : at + 256]
        upward = gate_up[:, 768 + at : 1024 + at]
        sigmoid = jax.nn.sigmoid(gate)
        grad_gate_up[:, at : at + 256] = (
            grad_active * upward * (sigmoid * (1.0 + gate * (1.0 - sigmoid)))
        ).astype(LOW)
        grad_gate_up[:, 768 + at : 1024 + at] = (grad_active * (gate * sigmoid)).astype(LOW)
    wait_all(both_copies)
    store_tokens(contract_cols(grad_gate_up[...], both[...]), grad_same, grad_sibling)


def swiglu_back(scalars, grad_out, gate_up, down_parts, gate_up_parts):
    return call(
        swiglu_back_kernel,
        [SM, VM, VM, VM] + [HB] * 8,
        [((512, 1536), LOW), ((2, 128, 1024), LOW), ((2, 128, 1024), LOW)],
        [VM] * 3,
        [
            pltpu.VMEM((768, 1024), LOW),
            pltpu.VMEM((1024, 1536), LOW),
            pltpu.SemaphoreType.DMA((8,)),
            pltpu.SemaphoreType.DMA((16,)),
        ],
        2 * 512 * 1024 * 2304,
        12 * 10**6,
    )(scalars, *grad_out, gate_up, *down_parts, *gate_up_parts)


def attend_back_kernel(
    scalars, same, sibling, part_a, part_b, part_c, part_d, pre, rotated, values, log_total,
    cosine, sine, gains, grad_all, grad_gains, whole, cos_rows, sin_rows, grad_rot, sems,
):
    copies = row_copies(scalars[0], (part_a, part_b, part_c, part_d), whole, sems, False)
    start_all(copies)
    fill_tables(scalars, cosine, sine, cos_rows, sin_rows)
    branch = load_tokens(same, sibling)
    wait_all(copies)
    grad_mixed = contract_cols(branch, whole[...]).astype(LOW)
    scaling = 128**-0.5
    for sequence in range(2):
        rows = slice(sequence * 256, sequence * 256 + 256)
        allowed = allowed_of(scalars, sequence)
        for group in range(2):
            keys = rotated[rows, 512 + group * 128 : 640 + group * 128]
            value_rows = values[rows, group * 128 : group * 128 + 128]
            grad_keys = jnp.zeros((256, 128), WIDE)
            grad_values = jnp.zeros((256, 128), WIDE)
            for head in (2 * group, 2 * group + 1):
                cut = slice(head * 128, head * 128 + 128)
                queries = rotated[rows, cut]
                grad_mix = grad_mixed[rows, cut]
                scores = jnp.where(allowed, contract_cols(queries, keys) * scaling, -1e30)
                probs = jnp.exp(scores - log_total[rows, head : head + 1])
                grad_values += contract_rows(probs.astype(LOW), grad_mix)
                grad_probs = contract_cols(grad_mix, value_rows)
                inner = jnp.sum(probs * grad_probs, axis=-1, keepdims=True)
                grad_scores = (probs * (grad_probs - inner)).astype(LOW)
                grad_rot[rows, cut] = matmul(grad_scores, keys) * scaling
                grad_keys += contract_rows(grad_scores, queries)
            grad_rot[rows, 512 + group * 128 : 640 + group * 128] = grad_keys * scaling
            grad_all[rows, 768 + group * 128 : 896 + group * 128] = grad_values.astype(LOW)
    gain_sums = [jnp.zeros((1, 128), WIDE), jnp.zeros((1, 128), WIDE)]
    for head in range(6):
        cut = slice(head * 128, head * 128 + 128)
        which = 0 if head < 4 else 1
        raw = pre[:, cut]
        scale = lax.rsqrt(jnp.mean(raw * raw, axis=-1, keepdims=True) + EPSILON)
        unit = raw * scale
        coming = grad_rot[:, cut]
        back = coming * cos_rows[...] - pltpu.roll(coming, 64, 1) * sin_rows[...]
        gain_sums[which] += jnp.sum(back * unit, axis=0, keepdims=True)
        back = back * gains[which : which + 1]
        along = jnp.mean(back * unit, axis=-1, keepdims=True)
        grad_all[:, cut] = (scale * (back - unit * along)).astype(LOW)
    grad_gains[...] = jnp.zeros((8, 128), WIDE)
    grad_gains[0:1] = gain_sums[0]
    grad_gains[1:2] = gain_sums[1]


def attend_back_call(scalars, branch, parts, pre, rotated, values, log_total, tables, gains):
    return call(
        attend_back_kernel,
        [SM, VM, VM, HB, HB, HB, HB] + [VM] * 7,
        [((512, 1024), LOW), ((8, 128), WIDE)],
        [VM] * 2,
        [
            pltpu.VMEM((512, 1024), LOW),
            pltpu.VMEM((512, 128), WIDE),
            pltpu.VMEM((512, 128), WIDE),
            pltpu.VMEM((512, 768), WIDE),
            pltpu.SemaphoreType.DMA((8,)),
        ],
        2 * 10**9,
        8 * 10**6,
    )(scalars, *branch, *parts, pre, rotated, values, log_total, *tables, gains)


def column_back_kernel(scalars, grads, part_a, part_b, part_c, part_d, same, sibling, whole, sems):
    copies = column_copies(scalars[0], (part_a, part_b, part_c, part_d), whole, sems, False)
    start_all(copies)
    wait_all(copies)
    store_tokens(contract_cols(grads[...], whole[...]), same, sibling)


def column_back(scalars, grads, parts):
    width = grads.shape[1]
    return call(
        column_back_kernel,
        [SM, VM, HB, HB, HB, HB],
        [((2, 128, 1024), LOW)] * 2,
        [VM] * 2,
        [pltpu.VMEM((1024, width), LOW), pltpu.SemaphoreType.DMA((16,))],
        2 * 512 * 1024 * width,
        5 * 10**6,
    )(scalars, grads, *parts)


def column_grad_kernel(
    scalars, same, sibling, grads, keep_one, send_one, keep_two, send_two, whole, sems
):
    for at in range(0, 1024, 256):
        cut = slice(at, at + 256)
        left = jnp.concatenate(
            [same[0, :, cut], sibling[0, :, cut], same[1, :, cut], sibling[1, :, cut]]
        )
        whole[cut] = contract_rows(left, grads[...]).astype(LOW)
    copies = column_copies(
        scalars[0], (keep_one, send_one, keep_two, send_two), whole, sems, True
    )
    start_all(copies)
    wait_all(copies)


def column_grad(scalars, tokens, grads):
    width = grads.shape[1]
    return call(
        column_grad_kernel,
        [SM, VM, VM, VM],
        [((256, width), LOW)] * 4,
        [HB] * 4,
        [pltpu.VMEM((1024, width), LOW), pltpu.SemaphoreType.DMA((16,))],
        2 * 512 * 1024 * width,
        6 * 10**6,
    )(scalars, *tokens, grads)


def row_grad_kernel(
    scalars, left, same, sibling, keep_one, send_one, keep_two, send_two, whole, sems
):
    right = load_tokens(same, sibling)
    for at in range(0, whole.shape[0], 256):
        cut = slice(at, at + 256)
        whole[cut] = contract_rows(left[:, cut], right).astype(LOW)
    copies = row_copies(scalars[0], (keep_one, send_one, keep_two, send_two), whole, sems, True)
    start_all(copies)
    wait_all(copies)


def row_grad(scalars, left, tokens):
    depth = left.shape[1]
    return call(
        row_grad_kernel,
        [SM, VM, VM, VM],
        [((depth // 4, 1024), LOW)] * 4,
        [HB] * 4,
        [pltpu.VMEM((depth, 1024), LOW), pltpu.SemaphoreType.DMA((8,))],
        2 * 512 * 1024 * depth,
        4 * 10**6,
    )(scalars, left, *tokens)


def fast_body(
    hidden_in,
    cotangent,
    block_order,
    w_query,
    key_weight,
    value_weight,
    w_output,
    w_gate,
    w_up,
    w_down,
    norm_gains,
    momentum_query,
    key_momentum,
    value_momentum,
    momentum_output,
    momentum_gate,
    momentum_up,
    momentum_down,
    momentum_gains,
):
    index = lax.axis_index("dp")
    core = lax.axis_index("ctx")
    p_index = (index // P_BIT) % 2
    mine = h_of(index) == core
    slice_own = 2 * core + p_index
    slice_give = 2 * core + 1 - p_index

    def column_slice(weight, which):
        size = weight.shape[1] // 4
        return lax.dynamic_slice_in_dim(weight, which * size, size, axis=1).astype(LOW)

    def column_pack(weights, which):
        return jnp.concatenate([column_slice(weight, which) for weight in weights], axis=1)

    gains_low = norm_gains.astype(LOW)[None]
    for bit in (P_BIT, H_BIT, Y_BIT, X_BIT):
        gains_low = jnp.concatenate([gains_low, swap(gains_low, bit)])
    order = [0]
    for bit in (P_BIT, H_BIT, Y_BIT, X_BIT):
        order = order + [o ^ bit for o in order]
    inverse = [0] * 16
    for at, relative in enumerate(order):
        inverse[relative] = at
    lookup = jnp.array(inverse, jnp.int32)[index ^ jnp.arange(16)]
    gains_all = jnp.take(gains_low, lookup, axis=0).reshape(-1).astype(WIDE)

    width = hidden_in.shape[2]
    head_size = 128
    gain_attn = gains_all[:width]
    gain_mlp = gains_all[width : 2 * width]
    head_gains = gains_all[2 * width :].reshape(2, head_size)

    qkv = (w_query, key_weight, value_weight)
    qkv_parts = gather_column_slices(column_pack(qkv, slice_own), column_pack(qkv, slice_give))
    output_parts = gather_row_slices(w_output.astype(LOW), mine)
    gate_up = (w_gate, w_up)
    gate_up_parts = gather_column_slices(
        column_pack(gate_up, slice_own), column_pack(gate_up, slice_give)
    )
    down_parts = gather_row_slices(w_down.astype(LOW), mine)

    tokens_own = hidden_in[0]
    count = tokens_own.shape[0]
    orders = jnp.concatenate([block_order, swap(block_order, P_BIT)])
    orders = jnp.where(core == 0, orders, jnp.roll(orders, 2, axis=1))
    scalars = jnp.concatenate([index[None], orders.reshape(-1)]).astype(jnp.int32)
    cosine, sine_table = rotary_tables(jnp.arange(2 * count, dtype=jnp.int32), head_size)
    sign = jnp.where(jnp.arange(head_size) < head_size // 2, -1.0, 1.0)
    tables = (cosine, sine_table * sign)

    tokens_f = tokens_own.astype(WIDE)
    normed_f, norm_pull = jax.vjp(rms_norm, tokens_f, gain_attn)
    normed = gather_tokens(normed_f.astype(LOW))
    grad_out = gather_tokens(cotangent[0])

    mixed_low, pre, rotated, value_low, log_total = attend(
        scalars, normed, qkv_parts, tables, head_gains
    )
    attended = sum_tokens(*row_product(scalars, mixed_low, output_parts))
    middle = tokens_f + attended
    normed_two_f, norm_two_pull = jax.vjp(rms_norm, middle, gain_mlp)
    normed_two = gather_tokens(normed_two_f.astype(LOW))
    gate_up_act, active = gate_product(scalars, normed_two, gate_up_parts)
    grad_down = row_grad(scalars, active, grad_out)
    grad_gate_up, back_same, back_sibling = swiglu_back(
        scalars, grad_out, gate_up_act, down_parts, gate_up_parts
    )
    grad_normed_two = sum_tokens(back_same, back_sibling)
    grad_gate_up_mat = column_grad(scalars, normed_two, grad_gate_up)
    layer_sum = sum_tokens(*row_product(scalars, active, down_parts))
    layer_out = (middle + layer_sum).astype(LOW)[None]

    grad_middle_norm, grad_gain_mlp = norm_two_pull(grad_normed_two)
    grad_middle = cotangent[0].astype(WIDE) + grad_middle_norm
    grad_branch = gather_tokens(grad_middle.astype(LOW))
    grad_output_mat = row_grad(scalars, mixed_low, grad_branch)
    grad_qkv, grad_head_gains = attend_back_call(
        scalars, grad_branch, output_parts, pre, rotated, value_low, log_total, tables, head_gains
    )
    grad_qkv_mat = column_grad(scalars, normed, grad_qkv)
    grad_normed = sum_tokens(*column_back(scalars, grad_qkv, qkv_parts))
    grad_tokens_norm, grad_gain_attn = norm_pull(grad_normed)
    input_grad = (grad_middle + grad_tokens_norm).astype(LOW)[None]

    grad_gains = jnp.concatenate([grad_gain_attn, grad_gain_mlp, grad_head_gains[:2].reshape(-1)])
    grad_gains = grad_gains.reshape(16, -1)
    grad_gains = grad_gains + swap_core(grad_gains.astype(LOW)).astype(WIDE)
    for bit in (P_BIT, H_BIT, Y_BIT, X_BIT):
        grad_gains = grad_gains + swap(grad_gains.astype(LOW), bit).astype(WIDE)
    grad_gains = lax.dynamic_index_in_dim(grad_gains, index, keepdims=False)

    down_sum = scatter_row_slices(*grad_down, mine)
    gate_up_sum = join_column_slices(*scatter_column_slices(*grad_gate_up_mat), p_index, core)
    output_sum = scatter_row_slices(*grad_output_mat, mine)
    qkv_sum = join_column_slices(*scatter_column_slices(*grad_qkv_mat), p_index, core)

    def columns(parts, start, size):
        return jnp.concatenate([part[:, start : start + size] for part in parts], axis=1)

    query_width = w_query.shape[1] // 4
    kv_width = key_weight.shape[1] // 4
    hidden_units = w_gate.shape[1] // 4
    sums = (
        columns(qkv_sum, 0, query_width),
        columns(qkv_sum, query_width, kv_width),
        columns(qkv_sum, query_width + kv_width, kv_width),
        output_sum,
        columns(gate_up_sum, 0, hidden_units),
        columns(gate_up_sum, hidden_units, hidden_units),
        down_sum,
        grad_gains,
    )
    masters = (w_query, key_weight, value_weight, w_output, w_gate, w_up, w_down, norm_gains)
    moments = (
        momentum_query,
        key_momentum,
        value_momentum,
        momentum_output,
        momentum_gate,
        momentum_up,
        momentum_down,
        momentum_gains,
    )
    norm_scale = lax.rsqrt(jnp.float32(16 * 2 * count))
    summed = tuple(part.astype(WIDE) for part in sums)
    updates, new_moments = lion_step(masters, moments, summed, norm_scale)
    return (layer_out, input_grad) + tuple(updates) + tuple(new_moments)


def solution(mesh):
    body = fast_body if dict(mesh.shape) == {"dp": 16, "ctx": 2} else general_body
    return jax.shard_map(
        body,
        mesh=mesh,
        in_specs=(
            P("dp", "ctx", None),
            P("dp", "ctx", None),
            P("dp", None),
            P("dp", None),
            P("dp", None),
            P("dp", None),
            P("dp", None),
            P("dp", None),
            P("dp", None),
            P("dp", None),
            P("dp"),
            P("dp", None),
            P("dp", None),
            P("dp", None),
            P("dp", None),
            P("dp", None),
            P("dp", None),
            P("dp", None),
            P("dp"),
        ),
        out_specs=(
            P("dp", "ctx", None),
            P("dp", "ctx", None),
            P("dp", None),
            P("dp", None),
            P("dp", None),
            P("dp", None),
            P("dp", None),
            P("dp", None),
            P("dp", None),
            P("dp"),
            P("dp", None),
            P("dp", None),
            P("dp", None),
            P("dp", None),
            P("dp", None),
            P("dp", None),
            P("dp", None),
            P("dp"),
        ),
        check_vma=False,
    )
```

```python
import jax
import jax.numpy as jnp
from jax import lax
from jax.experimental import pallas as pl
from jax.experimental.pallas import tpu as pltpu
from jax.sharding import PartitionSpec as P

EPSILON = 1e-06
THETA = 1000000.0
BETA_ONE = 0.9
BETA_TWO = 0.5
SOFTEN = 0.005
DECAY_FACTOR = 1.0


def rms_norm(values, gain_vec):
    return (
        values * lax.rsqrt(jnp.mean(values * values, axis=-1, keepdims=True) + EPSILON) * gain_vec
    )


def rotary_tables(positions, head_size):
    half_size = head_size // 2
    frequency = THETA ** (-(jnp.arange(half_size, dtype=jnp.float32) * 2.0 / head_size))
    angles = positions.astype(jnp.float32)[:, None] * frequency[None, :]
    angles = jnp.concatenate([angles, angles], axis=1)
    return (jnp.cos(angles), jnp.sin(angles))


def rotate(values, cosine, sine_table):
    half_size = values.shape[-1] // 2
    turned = jnp.concatenate([-values[..., half_size:], values[..., :half_size]], axis=-1)
    return values * cosine[:, None, :] + turned * sine_table[:, None, :]


def head_prep(projected, gain_vec, cosine, sine_table):
    shaped = projected.reshape(projected.shape[0], -1, gain_vec.shape[0])
    return rotate(rms_norm(shaped, gain_vec), cosine, sine_table)


def matmul(left, right):
    return jnp.dot(left, right, preferred_element_type=jnp.float32)


def contract_rows(left, right):
    return lax.dot_general(
        left, right, (((0,), (0,)), ((), ())), preferred_element_type=jnp.float32
    )


def contract_cols(left, right):
    return lax.dot_general(
        left, right, (((1,), (1,)), ((), ())), preferred_element_type=jnp.float32
    )


def head_scores(queries, key_row_block, query_pos, key_pos):
    scaling = queries.shape[-1] ** (-0.5)
    scores = (
        jnp.einsum("trd,kd->rtk", queries, key_row_block, preferred_element_type=jnp.float32)
        * scaling
    )
    allowed = query_pos[:, None] >= key_pos[None, :]
    return jnp.where(allowed[None], scores, -1e30)


def attend_head(query_pos, key_pos):

    def attend(group_item):
        queries, key_row_block, value_row_block = group_item
        scores = head_scores(queries, key_row_block, query_pos, key_pos)
        row_top = jnp.max(scores, axis=-1, keepdims=True)
        weights = jnp.exp(scores - row_top)
        row_total = jnp.sum(weights, axis=-1, keepdims=True)
        probs_low = (weights / row_total).astype(jnp.bfloat16)
        mixture = jnp.einsum(
            "rtk,kd->trd", probs_low, value_row_block, preferred_element_type=jnp.float32
        )
        return (mixture, (row_top + jnp.log(row_total))[..., 0])

    return attend


def attend_back(query_pos, key_pos):

    def backward(group_item):
        queries, key_row_block, value_row_block, grad_mix, log_total = group_item
        scaling = queries.shape[-1] ** (-0.5)
        scores = head_scores(queries, key_row_block, query_pos, key_pos)
        probs = jnp.exp(scores - log_total[..., None])
        grad_values = jnp.einsum(
            "rtk,trd->kd", probs.astype(jnp.bfloat16), grad_mix, preferred_element_type=jnp.float32
        )
        grad_probs = jnp.einsum(
            "trd,kd->rtk", grad_mix, value_row_block, preferred_element_type=jnp.float32
        )
        inner = jnp.sum(probs * grad_probs, axis=-1, keepdims=True)
        grad_scores = (probs * (grad_probs - inner)).astype(jnp.bfloat16)
        grad_queries = (
            jnp.einsum(
                "rtk,kd->trd", grad_scores, key_row_block, preferred_element_type=jnp.float32
            )
            * scaling
        )
        grad_keys = (
            jnp.einsum("rtk,trd->kd", grad_scores, queries, preferred_element_type=jnp.float32)
            * scaling
        )
        return (grad_queries, grad_keys, grad_values)

    return backward


def lion_step(masters, moments, gradients, norm_scale):
    updates = []
    new_moments = []
    for tensor_index in range(8):
        scaled = gradients[tensor_index] * norm_scale
        moment_arr = moments[tensor_index]
        blend_arr = BETA_ONE * moment_arr + (1.0 - BETA_ONE) * scaled
        direction = blend_arr / jnp.sqrt(blend_arr * blend_arr + SOFTEN)
        decay_here = DECAY_FACTOR if tensor_index < 7 else 0.0
        updates.append(direction + decay_here * masters[tensor_index])
        new_moments.append(BETA_TWO * moment_arr + (1.0 - BETA_TWO) * scaled)
    return (updates, new_moments)


def general_body(
    hidden_in,
    cotangent,
    block_order,
    w_query,
    key_weight,
    value_weight,
    w_output,
    w_gate,
    w_up,
    w_down,
    norm_gains,
    momentum_query,
    key_momentum,
    value_momentum,
    momentum_output,
    momentum_gate,
    momentum_up,
    momentum_down,
    momentum_gains,
):
    copies = (
        lax.all_gather(w_query.astype(jnp.bfloat16), "dp", axis=0, tiled=True),
        lax.all_gather(key_weight.astype(jnp.bfloat16), "dp", axis=0, tiled=True),
        lax.all_gather(value_weight.astype(jnp.bfloat16), "dp", axis=0, tiled=True),
        lax.all_gather(w_output.astype(jnp.bfloat16), "dp", axis=0, tiled=True),
        lax.all_gather(w_gate.astype(jnp.bfloat16), "dp", axis=0, tiled=True),
        lax.all_gather(w_up.astype(jnp.bfloat16), "dp", axis=0, tiled=True),
        lax.all_gather(w_down.astype(jnp.bfloat16), "dp", axis=0, tiled=True),
        lax.all_gather(norm_gains.astype(jnp.bfloat16), "dp", axis=0, tiled=True),
    )
    query_mat, key_mat, value_mat, output_mat, gate_mat, up_mat, down_mat, gains_low = copies
    gains_all = gains_low.astype(jnp.float32)
    width = hidden_in.shape[2]
    head_size = (gains_all.shape[0] - 2 * width) // 2
    kv_heads = key_mat.shape[1] // head_size
    query_heads = query_mat.shape[1] // head_size
    group_repeat_count = query_heads // kv_heads
    gain_attn = gains_all[:width]
    gain_mlp = gains_all[width : 2 * width]
    gain_query = gains_all[2 * width : 2 * width + head_size]
    gain_key = gains_all[2 * width + head_size :]
    tokens_in = hidden_in[0]
    token_count = tokens_in.shape[0]
    block_size = token_count // 2
    slot_order = block_order[0]
    key_pos = (
        slot_order[:, None] * block_size + jnp.arange(block_size, dtype=jnp.int32)[None, :]
    ).reshape(-1)
    query_pos = lax.dynamic_slice_in_dim(key_pos, lax.axis_index("ctx") * token_count, token_count)
    cosine, sine_table = rotary_tables(query_pos, head_size)
    tokens_f = tokens_in.astype(jnp.float32)
    normed_f, norm_pull = jax.vjp(rms_norm, tokens_f, gain_attn)
    normalized_input = normed_f.astype(jnp.bfloat16)
    query_pre = matmul(normalized_input, query_mat)
    key_pre = matmul(normalized_input, key_mat)
    value_low = matmul(normalized_input, value_mat).astype(jnp.bfloat16)
    query_rot, query_pull = jax.vjp(
        lambda projected, gain_vec: head_prep(projected, gain_vec, cosine, sine_table),
        query_pre,
        gain_query,
    )
    key_rot, key_pull = jax.vjp(
        lambda projected, gain_vec: head_prep(projected, gain_vec, cosine, sine_table),
        key_pre,
        gain_key,
    )
    query_low = query_rot.astype(jnp.bfloat16)
    key_heads = key_rot.astype(jnp.bfloat16).transpose(1, 0, 2)
    value_heads = value_low.reshape(token_count, kv_heads, head_size).transpose(1, 0, 2)
    gathered = (
        lax.all_gather(key_heads, "ctx", axis=1, tiled=True),
        lax.all_gather(value_heads, "ctx", axis=1, tiled=True),
    )
    query_groups = query_low.reshape(
        token_count, kv_heads, group_repeat_count, head_size
    ).transpose(1, 0, 2, 3)
    mixture, log_total = lax.map(
        attend_head(query_pos, key_pos), (query_groups, gathered[0], gathered[1])
    )
    mixed_low = mixture.transpose(1, 0, 2, 3).reshape(token_count, -1).astype(jnp.bfloat16)
    middle = tokens_f + matmul(mixed_low, output_mat)
    normed_two_f, norm_two_pull = jax.vjp(rms_norm, middle, gain_mlp)
    normed_two = normed_two_f.astype(jnp.bfloat16)
    gate_act = matmul(normed_two, gate_mat)
    upward = matmul(normed_two, up_mat)
    active_f, swiglu_pull = jax.vjp(
        lambda gate_in, up_in: jax.nn.silu(gate_in) * up_in, gate_act, upward
    )
    active = active_f.astype(jnp.bfloat16)
    layer_out = (middle + matmul(active, down_mat)).astype(jnp.bfloat16)[None]
    grad_out = cotangent[0]
    grad_down = contract_rows(active, grad_out)
    grad_active = contract_cols(grad_out, down_mat)
    grad_gate_f, grad_up_f = swiglu_pull(grad_active)
    grad_gate = grad_gate_f.astype(jnp.bfloat16)
    grad_upward = grad_up_f.astype(jnp.bfloat16)
    grad_gate_mat = contract_rows(normed_two, grad_gate)
    grad_up_mat = contract_rows(normed_two, grad_upward)
    grad_normed_two = contract_cols(grad_gate, gate_mat) + contract_cols(grad_upward, up_mat)
    grad_middle_norm, grad_gain_mlp = norm_two_pull(grad_normed_two)
    grad_middle = grad_out.astype(jnp.float32) + grad_middle_norm
    grad_branch = grad_middle.astype(jnp.bfloat16)
    grad_output_mat = contract_rows(mixed_low, grad_branch)
    grad_mixed = contract_cols(grad_branch, output_mat).astype(jnp.bfloat16)
    grad_groups = grad_mixed.reshape(
        token_count, kv_heads, group_repeat_count, head_size
    ).transpose(1, 0, 2, 3)
    grad_query_groups, grad_key_all, grad_value_all = lax.map(
        attend_back(query_pos, key_pos),
        (query_groups, gathered[0], gathered[1], grad_groups, log_total),
    )
    grad_key_own, grad_value_own = (
        lax.psum_scatter(
            grad_key_all.astype(jnp.bfloat16), "ctx", scatter_dimension=1, tiled=True
        ).astype(jnp.float32),
        lax.psum_scatter(
            grad_value_all.astype(jnp.bfloat16), "ctx", scatter_dimension=1, tiled=True
        ).astype(jnp.float32),
    )
    grad_query_rot = grad_query_groups.transpose(1, 0, 2, 3).reshape(
        token_count, query_heads, head_size
    )
    grad_query_pre, grad_gain_query = query_pull(grad_query_rot)
    grad_key_pre, grad_gain_key = key_pull(grad_key_own.transpose(1, 0, 2))
    grad_query_low = grad_query_pre.astype(jnp.bfloat16)
    grad_key_low = grad_key_pre.astype(jnp.bfloat16)
    grad_value_low = grad_value_own.transpose(1, 0, 2).reshape(token_count, -1).astype(jnp.bfloat16)
    grad_query_mat = contract_rows(normalized_input, grad_query_low)
    grad_key_mat = contract_rows(normalized_input, grad_key_low)
    grad_value_mat = contract_rows(normalized_input, grad_value_low)
    grad_normed = (
        contract_cols(grad_query_low, query_mat)
        + contract_cols(grad_key_low, key_mat)
        + contract_cols(grad_value_low, value_mat)
    )
    grad_tokens_norm, grad_gain_attn = norm_pull(grad_normed)
    input_grad = (grad_middle + grad_tokens_norm).astype(jnp.bfloat16)[None]
    grad_gains = jnp.concatenate([grad_gain_attn, grad_gain_mlp, grad_gain_query, grad_gain_key])
    masters = (w_query, key_weight, value_weight, w_output, w_gate, w_up, w_down, norm_gains)
    moments = (
        momentum_query,
        key_momentum,
        value_momentum,
        momentum_output,
        momentum_gate,
        momentum_up,
        momentum_down,
        momentum_gains,
    )
    token_total = lax.axis_size("dp") * key_pos.shape[0]
    norm_scale = lax.rsqrt(jnp.float32(token_total))
    shares = (
        lax.psum_scatter(
            grad_query_mat.astype(jnp.bfloat16), "dp", scatter_dimension=0, tiled=True
        ).astype(jnp.float32),
        lax.psum_scatter(
            grad_key_mat.astype(jnp.bfloat16), "dp", scatter_dimension=0, tiled=True
        ).astype(jnp.float32),
        lax.psum_scatter(
            grad_value_mat.astype(jnp.bfloat16), "dp", scatter_dimension=0, tiled=True
        ).astype(jnp.float32),
        lax.psum_scatter(
            grad_output_mat.astype(jnp.bfloat16), "dp", scatter_dimension=0, tiled=True
        ).astype(jnp.float32),
        lax.psum_scatter(
            grad_gate_mat.astype(jnp.bfloat16), "dp", scatter_dimension=0, tiled=True
        ).astype(jnp.float32),
        lax.psum_scatter(
            grad_up_mat.astype(jnp.bfloat16), "dp", scatter_dimension=0, tiled=True
        ).astype(jnp.float32),
        lax.psum_scatter(
            grad_down.astype(jnp.bfloat16), "dp", scatter_dimension=0, tiled=True
        ).astype(jnp.float32),
        lax.psum_scatter(
            grad_gains.astype(jnp.bfloat16), "dp", scatter_dimension=0, tiled=True
        ).astype(jnp.float32),
    )
    summed = (
        lax.psum(shares[0].astype(jnp.bfloat16), "ctx").astype(jnp.float32),
        lax.psum(shares[1].astype(jnp.bfloat16), "ctx").astype(jnp.float32),
        lax.psum(shares[2].astype(jnp.bfloat16), "ctx").astype(jnp.float32),
        lax.psum(shares[3].astype(jnp.bfloat16), "ctx").astype(jnp.float32),
        lax.psum(shares[4].astype(jnp.bfloat16), "ctx").astype(jnp.float32),
        lax.psum(shares[5].astype(jnp.bfloat16), "ctx").astype(jnp.float32),
        lax.psum(shares[6].astype(jnp.bfloat16), "ctx").astype(jnp.float32),
        lax.psum(shares[7].astype(jnp.bfloat16), "ctx").astype(jnp.float32),
    )
    updates, new_moments = lion_step(masters, moments, summed, norm_scale)
    return (layer_out, input_grad) + tuple(updates) + tuple(new_moments)


X_BIT, Y_BIT, P_BIT, H_BIT = 1, 2, 4, 8
LOW = jnp.bfloat16
WIDE = jnp.float32
VMEM_BYTES = 48 * 1024 * 1024
COLUMN_GROUPS = ((0, Y_BIT), (X_BIT, Y_BIT), (P_BIT, X_BIT), (P_BIT + Y_BIT, X_BIT))
ROW_GROUPS = ((0, Y_BIT, 0), (X_BIT, Y_BIT, 0), (0, X_BIT, 1), (Y_BIT, X_BIT, 1))


def swap(values, bit):
    return lax.ppermute(values, "dp", [(i, i ^ bit) for i in range(16)])


def swap_core(values):
    return lax.ppermute(values, "ctx", [(0, 1), (1, 0)])


def h_of(index):
    return (index // H_BIT) % 2


def row_cross(values, to_owner):
    pairs = []
    for index in range(16):
        for core in range(2):
            if (core == h_of(index)) != to_owner:
                pairs.append((index * 2 + core, (index ^ H_BIT) * 2 + core))
    return lax.ppermute(values, ("dp", "ctx"), pairs)


def gather_column_slices(own, give):
    rows = own.shape[0]
    got = swap(give, P_BIT)
    far = swap(jnp.concatenate([own, got]), H_BIT)
    first = jnp.concatenate([own, far[:rows]])
    second = jnp.concatenate([got, far[rows:]])
    first = jnp.concatenate([first, swap(first, Y_BIT)])
    second = jnp.concatenate([second, swap(second, X_BIT)])
    return first, swap(first, X_BIT), second, swap(second, Y_BIT)


def gather_row_slices(own, mine, stages=False):
    rows = own.shape[0] // 2
    far = row_cross(own, False)
    held = jnp.where(mine, own, far)
    first, second = held[:rows], held[rows:]
    came_y, came_x = swap(first, Y_BIT), swap(second, X_BIT)
    first = jnp.concatenate([first, came_y])
    second = jnp.concatenate([second, came_x])
    parts = first, swap(first, X_BIT), second, swap(second, Y_BIT)
    return (parts, [far], [came_y, came_x]) if stages else parts


def add_low(left, right):
    return (left.astype(WIDE) + right.astype(WIDE)).astype(LOW)


def scatter_column_slices(keep_one, send_one, keep_two, send_two):
    rows = keep_one.shape[0] // 4
    first = add_low(keep_one, swap(send_one, X_BIT))
    second = add_low(keep_two, swap(send_two, Y_BIT))
    first = add_low(first[: 2 * rows], swap(first[2 * rows :], Y_BIT))
    second = add_low(second[: 2 * rows], swap(second[2 * rows :], X_BIT))
    near = jnp.concatenate([first[:rows], second[:rows]])
    far = jnp.concatenate([first[rows:], second[rows:]])
    near = add_low(near, swap(far, H_BIT))
    return near[:rows], swap(near[rows:], P_BIT)


def scatter_row_slices(keep_one, send_one, keep_two, send_two, mine):
    rows = keep_one.shape[0] // 2
    first = add_low(keep_one, swap(send_one, X_BIT))
    second = add_low(keep_two, swap(send_two, Y_BIT))
    first = add_low(first[:rows], swap(first[rows:], Y_BIT))
    second = add_low(second[:rows], swap(second[rows:], X_BIT))
    held = jnp.concatenate([first, second])
    summed = add_low(held, row_cross(held, True))
    pairs = [(i * 2 + h_of(i), i * 2 + 1 - h_of(i)) for i in range(16)]
    return jnp.where(mine, summed, lax.ppermute(summed, ("dp", "ctx"), pairs))


def join_column_slices(own, partner, p_index, core):
    low_pair = jnp.where(p_index == 0, own, partner)
    high_pair = jnp.where(p_index == 0, partner, own)
    pair = jnp.stack([low_pair, high_pair])
    other = swap_core(pair)
    lower = jnp.where(core == 0, pair, other)
    upper = jnp.where(core == 0, other, pair)
    return [lower[0], lower[1], upper[0], upper[1]]


def gather_tokens(own):
    same = jnp.stack([own, swap(own, P_BIT)])
    return same, swap_core(same)


def sum_tokens(same, sibling):
    pair = same.astype(WIDE) + swap_core(sibling).astype(WIDE)
    return pair[0] + swap(pair[1].astype(LOW), P_BIT).astype(WIDE)


VM = pl.BlockSpec(memory_space=pltpu.VMEM)
SM = pl.BlockSpec(memory_space=pltpu.SMEM)
HB = pl.BlockSpec(memory_space=pl.ANY)


def call(kernel, in_specs, outs, out_specs, scratch, flops, moved, after=()):
    held, late = len(in_specs), len(after)

    def body(*refs):
        kernel(*refs[:held], *refs[held + late :])

    made = pl.pallas_call(
        body,
        in_specs=in_specs + [HB] * late,
        out_specs=out_specs,
        out_shape=[jax.ShapeDtypeStruct(shape, dtype) for shape, dtype in outs],
        scratch_shapes=scratch,
        compiler_params=pltpu.CompilerParams(vmem_limit_bytes=VMEM_BYTES),
        cost_estimate=pl.CostEstimate(flops=flops, bytes_accessed=moved, transcendentals=0),
    )
    return lambda *operands: made(*operands, *after)


def column_copies(index, parts, whole, sems, outward):
    copies = []
    rows = whole.shape[0] // 16
    for part, (base, outer) in zip(parts, COLUMN_GROUPS):
        for place in range(4):
            relative = base + (place // 2) * outer + (place % 2) * H_BIT
            start = pl.multiple_of((index ^ relative) * rows, rows)
            block = part.at[pl.ds(place * rows, rows)]
            inside = whole.at[pl.ds(start, rows)]
            ends = (inside, block) if outward else (block, inside)
            copies.append(pltpu.make_async_copy(*ends, sems.at[len(copies)]))
    return copies


def row_copies(index, parts, whole, sems, outward):
    copies = []
    rows = whole.shape[0] // 8
    for part, (base, outer, half) in zip(parts, ROW_GROUPS):
        for place in range(2):
            relative = base + place * outer
            start = pl.multiple_of((((index ^ relative) % 4) * 2 + half) * rows, rows)
            block = part.at[pl.ds(place * rows, rows)]
            inside = whole.at[pl.ds(start, rows)]
            ends = (inside, block) if outward else (block, inside)
            copies.append(pltpu.make_async_copy(*ends, sems.at[len(copies)]))
    return copies


def start_all(copies):
    for copy in copies:
        copy.start()


def wait_all(copies):
    for copy in copies:
        copy.wait()


def load_tokens(same, sibling):
    return jnp.concatenate([same[0], sibling[0], same[1], sibling[1]])


def store_tokens(values, same, sibling):
    count = same.shape[1]
    for sequence in range(2):
        at = 2 * count * sequence
        same[sequence] = values[at : at + count].astype(same.dtype)
        sibling[sequence] = values[at + count : at + 2 * count].astype(sibling.dtype)


def place_of(scalars, sequence, at):
    block = jnp.where(
        at < 128,
        jnp.where(at < 64, scalars[1 + 4 * sequence], scalars[2 + 4 * sequence]),
        jnp.where(at < 192, scalars[3 + 4 * sequence], scalars[4 + 4 * sequence]),
    )
    return block * 64 + at % 64


def allowed_of(scalars, sequence):
    rows = place_of(scalars, sequence, lax.broadcasted_iota(jnp.int32, (256, 1), 0))
    cols = place_of(scalars, sequence, lax.broadcasted_iota(jnp.int32, (1, 256), 1))
    return rows >= cols


def fill_tables(scalars, cosine, sine, cos_rows, sin_rows):
    for slot in range(8):
        start = pl.multiple_of(scalars[1 + slot] * 64, 64)
        cos_rows[slot * 64 : slot * 64 + 64] = cosine[pl.ds(start, 64)]
        sin_rows[slot * 64 : slot * 64 + 64] = sine[pl.ds(start, 64)]


def attend_kernel(
    scalars, same, sibling, part_a, part_b, part_c, part_d, cosine, sine, gains,
    mixture, pre, rotated, values_out, log_total, whole, cos_rows, sin_rows, sems,
):
    copies = column_copies(scalars[0], (part_a, part_b, part_c, part_d), whole, sems, False)
    start_all(copies)
    fill_tables(scalars, cosine, sine, cos_rows, sin_rows)
    tokens = load_tokens(same, sibling)
    wait_all(copies)
    projected = matmul(tokens, whole[...])
    pre[...] = projected[:, :768]
    values_out[...] = projected[:, 768:].astype(LOW)
    for head in range(6):
        cut = slice(head * 128, head * 128 + 128)
        raw = pre[:, cut]
        gain = gains[0:1] if head < 4 else gains[1:2]
        scale = lax.rsqrt(jnp.mean(raw * raw, axis=-1, keepdims=True) + EPSILON)
        unit = raw * scale * gain
        turned = pltpu.roll(unit, 64, 1)
        rotated[:, cut] = (unit * cos_rows[...] + turned * sin_rows[...]).astype(LOW)
    for sequence in range(2):
        rows = slice(sequence * 256, sequence * 256 + 256)
        allowed = allowed_of(scalars, sequence)
        tops = []
        for head in range(4):
            group = head // 2
            queries = rotated[rows, head * 128 : head * 128 + 128]
            keys = rotated[rows, 512 + group * 128 : 640 + group * 128]
            scores = jnp.where(allowed, contract_cols(queries, keys) * (128**-0.5), -1e30)
            top = jnp.max(scores, axis=-1, keepdims=True)
            weights = jnp.exp(scores - top)
            total = jnp.sum(weights, axis=-1, keepdims=True)
            probs = (weights / total).astype(LOW)
            mixed = matmul(probs, values_out[rows, group * 128 : group * 128 + 128])
            mixture[rows, head * 128 : head * 128 + 128] = mixed.astype(LOW)
            tops.append(jnp.broadcast_to(top + jnp.log(total), (256, 128)))
        lane = lax.broadcasted_iota(jnp.int32, (256, 128), 1)
        log_total[rows] = jnp.where(
            lane < 2, jnp.where(lane < 1, tops[0], tops[1]), jnp.where(lane < 3, tops[2], tops[3])
        )


def attend(scalars, tokens, parts, tables, gains, after=()):
    return call(
        attend_kernel,
        [SM, VM, VM, HB, HB, HB, HB, VM, VM, VM],
        [((512, 512), LOW), ((512, 768), WIDE), ((512, 768), LOW), ((512, 256), LOW), ((512, 128), WIDE)],
        [VM] * 5,
        [
            pltpu.VMEM((1024, 1024), LOW),
            pltpu.VMEM((512, 128), WIDE),
            pltpu.VMEM((512, 128), WIDE),
            pltpu.SemaphoreType.DMA((16,)),
        ],
        2 * 10**9,
        8 * 10**6,
        after,
    )(scalars, *tokens, *parts, *tables, gains)


def output_kernel(scalars, mixture, part_a, part_b, part_c, part_d, same, sibling, whole, sems):
    copies = row_copies(scalars[0], (part_a, part_b, part_c, part_d), whole, sems, False)
    start_all(copies)
    wait_all(copies)
    store_tokens(matmul(mixture[...], whole[...]), same, sibling)


def row_product(scalars, left, parts, after=()):
    depth = left.shape[1]
    return call(
        output_kernel,
        [SM, VM, HB, HB, HB, HB],
        [((2, 128, 1024), LOW)] * 2,
        [VM] * 2,
        [pltpu.VMEM((depth, 1024), LOW), pltpu.SemaphoreType.DMA((8,))],
        2 * 512 * 1024 * depth,
        4 * 10**6,
        after,
    )(scalars, left, *parts)


def gate_kernel(
    scalars, same, sibling, part_a, part_b, part_c, part_d, gate_up, active, whole, sems
):
    copies = column_copies(scalars[0], (part_a, part_b, part_c, part_d), whole, sems, False)
    start_all(copies)
    tokens = load_tokens(same, sibling)
    wait_all(copies)
    for at in range(0, 768, 256):
        gate = matmul(tokens, whole[:, at : at + 256])
        upward = matmul(tokens, whole[:, 768 + at : 1024 + at])
        gate_up[:, at : at + 256] = gate
        gate_up[:, 768 + at : 1024 + at] = upward
        active[:, at : at + 256] = (gate * jax.nn.sigmoid(gate) * upward).astype(LOW)


def gate_product(scalars, tokens, parts, after=()):
    return call(
        gate_kernel,
        [SM, VM, VM, HB, HB, HB, HB],
        [((512, 1536), WIDE), ((512, 768), LOW)],
        [VM] * 2,
        [pltpu.VMEM((1024, 1536), LOW), pltpu.SemaphoreType.DMA((16,))],
        2 * 512 * 1024 * 1536,
        10 * 10**6,
        after,
    )(scalars, *tokens, *parts)


def swiglu_back_kernel(
    scalars, same, sibling, gate_up, row_a, row_b, row_c, row_d, col_a, col_b, col_c, col_d,
    grad_gate_up, grad_same, grad_sibling, down, both, row_sems, col_sems,
):
    down_copies = row_copies(scalars[0], (row_a, row_b, row_c, row_d), down, row_sems, False)
    both_copies = column_copies(scalars[0], (col_a, col_b, col_c, col_d), both, col_sems, False)
    start_all(down_copies)
    start_all(both_copies)
    grad_out = load_tokens(same, sibling)
    wait_all(down_copies)
    for at in range(0, 768, 256):
        grad_active = contract_cols(grad_out, down[at : at + 256])
        gate = gate_up[:, at : at + 256]
        upward = gate_up[:, 768 + at : 1024 + at]
        sigmoid = jax.nn.sigmoid(gate)
        grad_gate_up[:, at : at + 256] = (
            grad_active * upward * (sigmoid * (1.0 + gate * (1.0 - sigmoid)))
        ).astype(LOW)
        grad_gate_up[:, 768 + at : 1024 + at] = (grad_active * (gate * sigmoid)).astype(LOW)
    wait_all(both_copies)
    store_tokens(contract_cols(grad_gate_up[...], both[...]), grad_same, grad_sibling)


def swiglu_back(scalars, grad_out, gate_up, down_parts, gate_up_parts, after=()):
    return call(
        swiglu_back_kernel,
        [SM, VM, VM, VM] + [HB] * 8,
        [((512, 1536), LOW), ((2, 128, 1024), LOW), ((2, 128, 1024), LOW)],
        [VM] * 3,
        [
            pltpu.VMEM((768, 1024), LOW),
            pltpu.VMEM((1024, 1536), LOW),
            pltpu.SemaphoreType.DMA((8,)),
            pltpu.SemaphoreType.DMA((16,)),
        ],
        2 * 512 * 1024 * 2304,
        12 * 10**6,
        after,
    )(scalars, *grad_out, gate_up, *down_parts, *gate_up_parts)


def attend_back_kernel(
    scalars, same, sibling, part_a, part_b, part_c, part_d, pre, rotated, values, log_total,
    cosine, sine, gains, grad_all, grad_gains, whole, cos_rows, sin_rows, grad_rot, sems,
):
    copies = row_copies(scalars[0], (part_a, part_b, part_c, part_d), whole, sems, False)
    start_all(copies)
    fill_tables(scalars, cosine, sine, cos_rows, sin_rows)
    branch = load_tokens(same, sibling)
    wait_all(copies)
    grad_mixed = contract_cols(branch, whole[...]).astype(LOW)
    scaling = 128**-0.5
    for sequence in range(2):
        rows = slice(sequence * 256, sequence * 256 + 256)
        allowed = allowed_of(scalars, sequence)
        for group in range(2):
            keys = rotated[rows, 512 + group * 128 : 640 + group * 128]
            value_rows = values[rows, group * 128 : group * 128 + 128]
            grad_keys = jnp.zeros((256, 128), WIDE)
            grad_values = jnp.zeros((256, 128), WIDE)
            for head in (2 * group, 2 * group + 1):
                cut = slice(head * 128, head * 128 + 128)
                queries = rotated[rows, cut]
                grad_mix = grad_mixed[rows, cut]
                scores = jnp.where(allowed, contract_cols(queries, keys) * scaling, -1e30)
                probs = jnp.exp(scores - log_total[rows, head : head + 1])
                grad_values += contract_rows(probs.astype(LOW), grad_mix)
                grad_probs = contract_cols(grad_mix, value_rows)
                inner = jnp.sum(probs * grad_probs, axis=-1, keepdims=True)
                grad_scores = (probs * (grad_probs - inner)).astype(LOW)
                grad_rot[rows, cut] = matmul(grad_scores, keys) * scaling
                grad_keys += contract_rows(grad_scores, queries)
            grad_rot[rows, 512 + group * 128 : 640 + group * 128] = grad_keys * scaling
            grad_all[rows, 768 + group * 128 : 896 + group * 128] = grad_values.astype(LOW)
    gain_sums = [jnp.zeros((1, 128), WIDE), jnp.zeros((1, 128), WIDE)]
    for head in range(6):
        cut = slice(head * 128, head * 128 + 128)
        which = 0 if head < 4 else 1
        raw = pre[:, cut]
        scale = lax.rsqrt(jnp.mean(raw * raw, axis=-1, keepdims=True) + EPSILON)
        unit = raw * scale
        coming = grad_rot[:, cut]
        back = coming * cos_rows[...] - pltpu.roll(coming, 64, 1) * sin_rows[...]
        gain_sums[which] += jnp.sum(back * unit, axis=0, keepdims=True)
        back = back * gains[which : which + 1]
        along = jnp.mean(back * unit, axis=-1, keepdims=True)
        grad_all[:, cut] = (scale * (back - unit * along)).astype(LOW)
    grad_gains[...] = jnp.zeros((8, 128), WIDE)
    grad_gains[0:1] = gain_sums[0]
    grad_gains[1:2] = gain_sums[1]


def attend_back_call(scalars, branch, parts, pre, rotated, values, log_total, tables, gains, after=()):
    return call(
        attend_back_kernel,
        [SM, VM, VM, HB, HB, HB, HB] + [VM] * 7,
        [((512, 1024), LOW), ((8, 128), WIDE)],
        [VM] * 2,
        [
            pltpu.VMEM((512, 1024), LOW),
            pltpu.VMEM((512, 128), WIDE),
            pltpu.VMEM((512, 128), WIDE),
            pltpu.VMEM((512, 768), WIDE),
            pltpu.SemaphoreType.DMA((8,)),
        ],
        2 * 10**9,
        8 * 10**6,
        after,
    )(scalars, *branch, *parts, pre, rotated, values, log_total, *tables, gains)


def column_back_kernel(scalars, grads, part_a, part_b, part_c, part_d, same, sibling, whole, sems):
    copies = column_copies(scalars[0], (part_a, part_b, part_c, part_d), whole, sems, False)
    start_all(copies)
    wait_all(copies)
    store_tokens(contract_cols(grads[...], whole[...]), same, sibling)


def column_back(scalars, grads, parts, after=()):
    width = grads.shape[1]
    return call(
        column_back_kernel,
        [SM, VM, HB, HB, HB, HB],
        [((2, 128, 1024), LOW)] * 2,
        [VM] * 2,
        [pltpu.VMEM((1024, width), LOW), pltpu.SemaphoreType.DMA((16,))],
        2 * 512 * 1024 * width,
        5 * 10**6,
        after,
    )(scalars, grads, *parts)


def column_grad_kernel(
    scalars, same, sibling, grads, keep_one, send_one, keep_two, send_two, whole, sems
):
    for at in range(0, 1024, 256):
        cut = slice(at, at + 256)
        left = jnp.concatenate(
            [same[0, :, cut], sibling[0, :, cut], same[1, :, cut], sibling[1, :, cut]]
        )
        whole[cut] = contract_rows(left, grads[...]).astype(LOW)
    copies = column_copies(
        scalars[0], (keep_one, send_one, keep_two, send_two), whole, sems, True
    )
    start_all(copies)
    wait_all(copies)


def column_grad(scalars, tokens, grads, after=()):
    width = grads.shape[1]
    return call(
        column_grad_kernel,
        [SM, VM, VM, VM],
        [((256, width), LOW)] * 4,
        [HB] * 4,
        [pltpu.VMEM((1024, width), LOW), pltpu.SemaphoreType.DMA((16,))],
        2 * 512 * 1024 * width,
        6 * 10**6,
        after,
    )(scalars, *tokens, grads)


def row_grad_kernel(
    scalars, left, same, sibling, keep_one, send_one, keep_two, send_two, whole, sems
):
    right = load_tokens(same, sibling)
    for at in range(0, whole.shape[0], 256):
        cut = slice(at, at + 256)
        whole[cut] = contract_rows(left[:, cut], right).astype(LOW)
    copies = row_copies(scalars[0], (keep_one, send_one, keep_two, send_two), whole, sems, True)
    start_all(copies)
    wait_all(copies)


def row_grad(scalars, left, tokens, after=()):
    depth = left.shape[1]
    return call(
        row_grad_kernel,
        [SM, VM, VM, VM],
        [((depth // 4, 1024), LOW)] * 4,
        [HB] * 4,
        [pltpu.VMEM((depth, 1024), LOW), pltpu.SemaphoreType.DMA((8,))],
        2 * 512 * 1024 * depth,
        4 * 10**6,
        after,
    )(scalars, left, *tokens)


def fast_body(
    hidden_in,
    cotangent,
    block_order,
    w_query,
    key_weight,
    value_weight,
    w_output,
    w_gate,
    w_up,
    w_down,
    norm_gains,
    momentum_query,
    key_momentum,
    value_momentum,
    momentum_output,
    momentum_gate,
    momentum_up,
    momentum_down,
    momentum_gains,
):
    index = lax.axis_index("dp")
    core = lax.axis_index("ctx")
    p_index = (index // P_BIT) % 2
    mine = h_of(index) == core
    slice_own = 2 * core + p_index
    slice_give = 2 * core + 1 - p_index

    def column_slice(weight, which):
        size = weight.shape[1] // 4
        return lax.dynamic_slice_in_dim(weight, which * size, size, axis=1).astype(LOW)

    def column_pack(weights, which):
        return jnp.concatenate([column_slice(weight, which) for weight in weights], axis=1)

    gains_low = norm_gains.astype(LOW)[None]
    for bit in (P_BIT, H_BIT, Y_BIT, X_BIT):
        gains_low = jnp.concatenate([gains_low, swap(gains_low, bit)])
    order = [0]
    for bit in (P_BIT, H_BIT, Y_BIT, X_BIT):
        order = order + [o ^ bit for o in order]
    inverse = [0] * 16
    for at, relative in enumerate(order):
        inverse[relative] = at
    lookup = jnp.array(inverse, jnp.int32)[index ^ jnp.arange(16)]
    gains_all = jnp.take(gains_low, lookup, axis=0).reshape(-1).astype(WIDE)

    width = hidden_in.shape[2]
    head_size = 128
    gain_attn = gains_all[:width]
    gain_mlp = gains_all[width : 2 * width]
    head_gains = gains_all[2 * width :].reshape(2, head_size)

    qkv = (w_query, key_weight, value_weight)
    qkv_parts = gather_column_slices(column_pack(qkv, slice_own), column_pack(qkv, slice_give))
    output_parts = gather_row_slices(w_output.astype(LOW), mine)
    gate_up = (w_gate, w_up)
    gate_up_parts = gather_column_slices(
        column_pack(gate_up, slice_own), column_pack(gate_up, slice_give)
    )
    down_parts, _, down_first = gather_row_slices(w_down.astype(LOW), mine, True)

    tokens_own = hidden_in[0]
    count = tokens_own.shape[0]
    orders = jnp.concatenate([block_order, swap(block_order, P_BIT)])
    orders = jnp.where(core == 0, orders, jnp.roll(orders, 2, axis=1))
    scalars = jnp.concatenate([index[None], orders.reshape(-1)]).astype(jnp.int32)
    cosine, sine_table = rotary_tables(jnp.arange(2 * count, dtype=jnp.int32), head_size)
    sign = jnp.where(jnp.arange(head_size) < head_size // 2, -1.0, 1.0)
    tables = (cosine, sine_table * sign)

    tokens_f = tokens_own.astype(WIDE)
    normed_f, norm_pull = jax.vjp(rms_norm, tokens_f, gain_attn)
    normed = gather_tokens(normed_f.astype(LOW))
    grad_out = gather_tokens(cotangent[0])

    mixed_low, pre, rotated, value_low, log_total = attend(
        scalars, normed, qkv_parts, tables, head_gains
    )
    attended = sum_tokens(*row_product(scalars, mixed_low, output_parts, down_first))
    middle = tokens_f + attended
    normed_two_f, norm_two_pull = jax.vjp(rms_norm, middle, gain_mlp)
    normed_two = gather_tokens(normed_two_f.astype(LOW))
    gate_up_act, active = gate_product(scalars, normed_two, gate_up_parts, down_parts)
    grad_gate_up, back_same, back_sibling = swiglu_back(
        scalars, grad_out, gate_up_act, down_parts, gate_up_parts
    )
    grad_down = row_grad(scalars, active, grad_out, [back_same])
    grad_normed_two = sum_tokens(back_same, back_sibling)
    grad_gate_up_mat = column_grad(scalars, normed_two, grad_gate_up, [back_same])

    grad_middle_norm, grad_gain_mlp = norm_two_pull(grad_normed_two)
    grad_middle = cotangent[0].astype(WIDE) + grad_middle_norm
    grad_branch = gather_tokens(grad_middle.astype(LOW))
    grad_qkv, grad_head_gains = attend_back_call(
        scalars, grad_branch, output_parts, pre, rotated, value_low, log_total, tables, head_gains
    )
    grad_qkv_mat = column_grad(scalars, normed, grad_qkv, ())
    grad_output_mat = row_grad(scalars, mixed_low, grad_branch, [grad_qkv_mat[0]])
    grad_normed = sum_tokens(*column_back(scalars, grad_qkv, qkv_parts, [grad_qkv_mat[0]]))
    grad_tokens_norm, grad_gain_attn = norm_pull(grad_normed)
    input_grad = (grad_middle + grad_tokens_norm).astype(LOW)[None]

    layer_sum = sum_tokens(*row_product(scalars, active, down_parts, [grad_qkv_mat[0]]))
    layer_out = (middle + layer_sum).astype(LOW)[None]
    grad_gains = jnp.concatenate([grad_gain_attn, grad_gain_mlp, grad_head_gains[:2].reshape(-1)])
    grad_gains = grad_gains.reshape(16, -1)
    grad_gains = grad_gains + swap_core(grad_gains.astype(LOW)).astype(WIDE)
    for bit in (P_BIT, H_BIT, Y_BIT, X_BIT):
        grad_gains = grad_gains + swap(grad_gains.astype(LOW), bit).astype(WIDE)
    grad_gains = lax.dynamic_index_in_dim(grad_gains, index, keepdims=False)

    down_sum = scatter_row_slices(*grad_down, mine)
    gate_up_sum = join_column_slices(*scatter_column_slices(*grad_gate_up_mat), p_index, core)
    output_sum = scatter_row_slices(*grad_output_mat, mine)
    qkv_sum = join_column_slices(*scatter_column_slices(*grad_qkv_mat), p_index, core)

    def columns(parts, start, size):
        return jnp.concatenate([part[:, start : start + size] for part in parts], axis=1)

    query_width = w_query.shape[1] // 4
    kv_width = key_weight.shape[1] // 4
    hidden_units = w_gate.shape[1] // 4
    sums = (
        columns(qkv_sum, 0, query_width),
        columns(qkv_sum, query_width, kv_width),
        columns(qkv_sum, query_width + kv_width, kv_width),
        output_sum,
        columns(gate_up_sum, 0, hidden_units),
        columns(gate_up_sum, hidden_units, hidden_units),
        down_sum,
        grad_gains,
    )
    masters = (w_query, key_weight, value_weight, w_output, w_gate, w_up, w_down, norm_gains)
    moments = (
        momentum_query,
        key_momentum,
        value_momentum,
        momentum_output,
        momentum_gate,
        momentum_up,
        momentum_down,
        momentum_gains,
    )
    norm_scale = lax.rsqrt(jnp.float32(16 * 2 * count))
    summed = tuple(part.astype(WIDE) for part in sums)
    updates, new_moments = lion_step(masters, moments, summed, norm_scale)
    return (layer_out, input_grad) + tuple(updates) + tuple(new_moments)


def solution(mesh):
    body = fast_body if dict(mesh.shape) == {"dp": 16, "ctx": 2} else general_body
    return jax.shard_map(
        body,
        mesh=mesh,
        in_specs=(
            P("dp", "ctx", None),
            P("dp", "ctx", None),
            P("dp", None),
            P("dp", None),
            P("dp", None),
            P("dp", None),
            P("dp", None),
            P("dp", None),
            P("dp", None),
            P("dp", None),
            P("dp"),
            P("dp", None),
            P("dp", None),
            P("dp", None),
            P("dp", None),
            P("dp", None),
            P("dp", None),
            P("dp", None),
            P("dp"),
        ),
        out_specs=(
            P("dp", "ctx", None),
            P("dp", "ctx", None),
            P("dp", None),
            P("dp", None),
            P("dp", None),
            P("dp", None),
            P("dp", None),
            P("dp", None),
            P("dp", None),
            P("dp"),
            P("dp", None),
            P("dp", None),
            P("dp", None),
            P("dp", None),
            P("dp", None),
            P("dp", None),
            P("dp", None),
            P("dp"),
        ),
        check_vma=False,
    )
```

```python
import jax
import jax.numpy as jnp
from jax import lax
from jax.experimental import pallas as pl
from jax.experimental.pallas import tpu as pltpu
from jax.sharding import PartitionSpec as P

EPSILON = 1e-06
THETA = 1000000.0
BETA_ONE = 0.9
BETA_TWO = 0.5
SOFTEN = 0.005
DECAY_FACTOR = 1.0


def rms_norm(values, gain_vec):
    return (
        values * lax.rsqrt(jnp.mean(values * values, axis=-1, keepdims=True) + EPSILON) * gain_vec
    )


def rotary_tables(positions, head_size):
    half_size = head_size // 2
    frequency = THETA ** (-(jnp.arange(half_size, dtype=jnp.float32) * 2.0 / head_size))
    angles = positions.astype(jnp.float32)[:, None] * frequency[None, :]
    angles = jnp.concatenate([angles, angles], axis=1)
    return (jnp.cos(angles), jnp.sin(angles))


def rotate(values, cosine, sine_table):
    half_size = values.shape[-1] // 2
    turned = jnp.concatenate([-values[..., half_size:], values[..., :half_size]], axis=-1)
    return values * cosine[:, None, :] + turned * sine_table[:, None, :]


def head_prep(projected, gain_vec, cosine, sine_table):
    shaped = projected.reshape(projected.shape[0], -1, gain_vec.shape[0])
    return rotate(rms_norm(shaped, gain_vec), cosine, sine_table)


def matmul(left, right):
    return jnp.dot(left, right, preferred_element_type=jnp.float32)


def contract_rows(left, right):
    return lax.dot_general(
        left, right, (((0,), (0,)), ((), ())), preferred_element_type=jnp.float32
    )


def contract_cols(left, right):
    return lax.dot_general(
        left, right, (((1,), (1,)), ((), ())), preferred_element_type=jnp.float32
    )


def head_scores(queries, key_row_block, query_pos, key_pos):
    scaling = queries.shape[-1] ** (-0.5)
    scores = (
        jnp.einsum("trd,kd->rtk", queries, key_row_block, preferred_element_type=jnp.float32)
        * scaling
    )
    allowed = query_pos[:, None] >= key_pos[None, :]
    return jnp.where(allowed[None], scores, -1e30)


def attend_head(query_pos, key_pos):

    def attend(group_item):
        queries, key_row_block, value_row_block = group_item
        scores = head_scores(queries, key_row_block, query_pos, key_pos)
        row_top = jnp.max(scores, axis=-1, keepdims=True)
        weights = jnp.exp(scores - row_top)
        row_total = jnp.sum(weights, axis=-1, keepdims=True)
        probs_low = (weights / row_total).astype(jnp.bfloat16)
        mixture = jnp.einsum(
            "rtk,kd->trd", probs_low, value_row_block, preferred_element_type=jnp.float32
        )
        return (mixture, (row_top + jnp.log(row_total))[..., 0])

    return attend


def attend_back(query_pos, key_pos):

    def backward(group_item):
        queries, key_row_block, value_row_block, grad_mix, log_total = group_item
        scaling = queries.shape[-1] ** (-0.5)
        scores = head_scores(queries, key_row_block, query_pos, key_pos)
        probs = jnp.exp(scores - log_total[..., None])
        grad_values = jnp.einsum(
            "rtk,trd->kd", probs.astype(jnp.bfloat16), grad_mix, preferred_element_type=jnp.float32
        )
        grad_probs = jnp.einsum(
            "trd,kd->rtk", grad_mix, value_row_block, preferred_element_type=jnp.float32
        )
        inner = jnp.sum(probs * grad_probs, axis=-1, keepdims=True)
        grad_scores = (probs * (grad_probs - inner)).astype(jnp.bfloat16)
        grad_queries = (
            jnp.einsum(
                "rtk,kd->trd", grad_scores, key_row_block, preferred_element_type=jnp.float32
            )
            * scaling
        )
        grad_keys = (
            jnp.einsum("rtk,trd->kd", grad_scores, queries, preferred_element_type=jnp.float32)
            * scaling
        )
        return (grad_queries, grad_keys, grad_values)

    return backward


def lion_step(masters, moments, gradients, norm_scale):
    updates = []
    new_moments = []
    for tensor_index in range(8):
        scaled = gradients[tensor_index] * norm_scale
        moment_arr = moments[tensor_index]
        blend_arr = BETA_ONE * moment_arr + (1.0 - BETA_ONE) * scaled
        direction = blend_arr / jnp.sqrt(blend_arr * blend_arr + SOFTEN)
        decay_here = DECAY_FACTOR if tensor_index < 7 else 0.0
        updates.append(direction + decay_here * masters[tensor_index])
        new_moments.append(BETA_TWO * moment_arr + (1.0 - BETA_TWO) * scaled)
    return (updates, new_moments)


def general_body(
    hidden_in,
    cotangent,
    block_order,
    w_query,
    key_weight,
    value_weight,
    w_output,
    w_gate,
    w_up,
    w_down,
    norm_gains,
    momentum_query,
    key_momentum,
    value_momentum,
    momentum_output,
    momentum_gate,
    momentum_up,
    momentum_down,
    momentum_gains,
):
    copies = (
        lax.all_gather(w_query.astype(jnp.bfloat16), "dp", axis=0, tiled=True),
        lax.all_gather(key_weight.astype(jnp.bfloat16), "dp", axis=0, tiled=True),
        lax.all_gather(value_weight.astype(jnp.bfloat16), "dp", axis=0, tiled=True),
        lax.all_gather(w_output.astype(jnp.bfloat16), "dp", axis=0, tiled=True),
        lax.all_gather(w_gate.astype(jnp.bfloat16), "dp", axis=0, tiled=True),
        lax.all_gather(w_up.astype(jnp.bfloat16), "dp", axis=0, tiled=True),
        lax.all_gather(w_down.astype(jnp.bfloat16), "dp", axis=0, tiled=True),
        lax.all_gather(norm_gains.astype(jnp.bfloat16), "dp", axis=0, tiled=True),
    )
    query_mat, key_mat, value_mat, output_mat, gate_mat, up_mat, down_mat, gains_low = copies
    gains_all = gains_low.astype(jnp.float32)
    width = hidden_in.shape[2]
    head_size = (gains_all.shape[0] - 2 * width) // 2
    kv_heads = key_mat.shape[1] // head_size
    query_heads = query_mat.shape[1] // head_size
    group_repeat_count = query_heads // kv_heads
    gain_attn = gains_all[:width]
    gain_mlp = gains_all[width : 2 * width]
    gain_query = gains_all[2 * width : 2 * width + head_size]
    gain_key = gains_all[2 * width + head_size :]
    tokens_in = hidden_in[0]
    token_count = tokens_in.shape[0]
    block_size = token_count // 2
    slot_order = block_order[0]
    key_pos = (
        slot_order[:, None] * block_size + jnp.arange(block_size, dtype=jnp.int32)[None, :]
    ).reshape(-1)
    query_pos = lax.dynamic_slice_in_dim(key_pos, lax.axis_index("ctx") * token_count, token_count)
    cosine, sine_table = rotary_tables(query_pos, head_size)
    tokens_f = tokens_in.astype(jnp.float32)
    normed_f, norm_pull = jax.vjp(rms_norm, tokens_f, gain_attn)
    normalized_input = normed_f.astype(jnp.bfloat16)
    query_pre = matmul(normalized_input, query_mat)
    key_pre = matmul(normalized_input, key_mat)
    value_low = matmul(normalized_input, value_mat).astype(jnp.bfloat16)
    query_rot, query_pull = jax.vjp(
        lambda projected, gain_vec: head_prep(projected, gain_vec, cosine, sine_table),
        query_pre,
        gain_query,
    )
    key_rot, key_pull = jax.vjp(
        lambda projected, gain_vec: head_prep(projected, gain_vec, cosine, sine_table),
        key_pre,
        gain_key,
    )
    query_low = query_rot.astype(jnp.bfloat16)
    key_heads = key_rot.astype(jnp.bfloat16).transpose(1, 0, 2)
    value_heads = value_low.reshape(token_count, kv_heads, head_size).transpose(1, 0, 2)
    gathered = (
        lax.all_gather(key_heads, "ctx", axis=1, tiled=True),
        lax.all_gather(value_heads, "ctx", axis=1, tiled=True),
    )
    query_groups = query_low.reshape(
        token_count, kv_heads, group_repeat_count, head_size
    ).transpose(1, 0, 2, 3)
    mixture, log_total = lax.map(
        attend_head(query_pos, key_pos), (query_groups, gathered[0], gathered[1])
    )
    mixed_low = mixture.transpose(1, 0, 2, 3).reshape(token_count, -1).astype(jnp.bfloat16)
    middle = tokens_f + matmul(mixed_low, output_mat)
    normed_two_f, norm_two_pull = jax.vjp(rms_norm, middle, gain_mlp)
    normed_two = normed_two_f.astype(jnp.bfloat16)
    gate_act = matmul(normed_two, gate_mat)
    upward = matmul(normed_two, up_mat)
    active_f, swiglu_pull = jax.vjp(
        lambda gate_in, up_in: jax.nn.silu(gate_in) * up_in, gate_act, upward
    )
    active = active_f.astype(jnp.bfloat16)
    layer_out = (middle + matmul(active, down_mat)).astype(jnp.bfloat16)[None]
    grad_out = cotangent[0]
    grad_down = contract_rows(active, grad_out)
    grad_active = contract_cols(grad_out, down_mat)
    grad_gate_f, grad_up_f = swiglu_pull(grad_active)
    grad_gate = grad_gate_f.astype(jnp.bfloat16)
    grad_upward = grad_up_f.astype(jnp.bfloat16)
    grad_gate_mat = contract_rows(normed_two, grad_gate)
    grad_up_mat = contract_rows(normed_two, grad_upward)
    grad_normed_two = contract_cols(grad_gate, gate_mat) + contract_cols(grad_upward, up_mat)
    grad_middle_norm, grad_gain_mlp = norm_two_pull(grad_normed_two)
    grad_middle = grad_out.astype(jnp.float32) + grad_middle_norm
    grad_branch = grad_middle.astype(jnp.bfloat16)
    grad_output_mat = contract_rows(mixed_low, grad_branch)
    grad_mixed = contract_cols(grad_branch, output_mat).astype(jnp.bfloat16)
    grad_groups = grad_mixed.reshape(
        token_count, kv_heads, group_repeat_count, head_size
    ).transpose(1, 0, 2, 3)
    grad_query_groups, grad_key_all, grad_value_all = lax.map(
        attend_back(query_pos, key_pos),
        (query_groups, gathered[0], gathered[1], grad_groups, log_total),
    )
    grad_key_own, grad_value_own = (
        lax.psum_scatter(
            grad_key_all.astype(jnp.bfloat16), "ctx", scatter_dimension=1, tiled=True
        ).astype(jnp.float32),
        lax.psum_scatter(
            grad_value_all.astype(jnp.bfloat16), "ctx", scatter_dimension=1, tiled=True
        ).astype(jnp.float32),
    )
    grad_query_rot = grad_query_groups.transpose(1, 0, 2, 3).reshape(
        token_count, query_heads, head_size
    )
    grad_query_pre, grad_gain_query = query_pull(grad_query_rot)
    grad_key_pre, grad_gain_key = key_pull(grad_key_own.transpose(1, 0, 2))
    grad_query_low = grad_query_pre.astype(jnp.bfloat16)
    grad_key_low = grad_key_pre.astype(jnp.bfloat16)
    grad_value_low = grad_value_own.transpose(1, 0, 2).reshape(token_count, -1).astype(jnp.bfloat16)
    grad_query_mat = contract_rows(normalized_input, grad_query_low)
    grad_key_mat = contract_rows(normalized_input, grad_key_low)
    grad_value_mat = contract_rows(normalized_input, grad_value_low)
    grad_normed = (
        contract_cols(grad_query_low, query_mat)
        + contract_cols(grad_key_low, key_mat)
        + contract_cols(grad_value_low, value_mat)
    )
    grad_tokens_norm, grad_gain_attn = norm_pull(grad_normed)
    input_grad = (grad_middle + grad_tokens_norm).astype(jnp.bfloat16)[None]
    grad_gains = jnp.concatenate([grad_gain_attn, grad_gain_mlp, grad_gain_query, grad_gain_key])
    masters = (w_query, key_weight, value_weight, w_output, w_gate, w_up, w_down, norm_gains)
    moments = (
        momentum_query,
        key_momentum,
        value_momentum,
        momentum_output,
        momentum_gate,
        momentum_up,
        momentum_down,
        momentum_gains,
    )
    token_total = lax.axis_size("dp") * key_pos.shape[0]
    norm_scale = lax.rsqrt(jnp.float32(token_total))
    shares = (
        lax.psum_scatter(
            grad_query_mat.astype(jnp.bfloat16), "dp", scatter_dimension=0, tiled=True
        ).astype(jnp.float32),
        lax.psum_scatter(
            grad_key_mat.astype(jnp.bfloat16), "dp", scatter_dimension=0, tiled=True
        ).astype(jnp.float32),
        lax.psum_scatter(
            grad_value_mat.astype(jnp.bfloat16), "dp", scatter_dimension=0, tiled=True
        ).astype(jnp.float32),
        lax.psum_scatter(
            grad_output_mat.astype(jnp.bfloat16), "dp", scatter_dimension=0, tiled=True
        ).astype(jnp.float32),
        lax.psum_scatter(
            grad_gate_mat.astype(jnp.bfloat16), "dp", scatter_dimension=0, tiled=True
        ).astype(jnp.float32),
        lax.psum_scatter(
            grad_up_mat.astype(jnp.bfloat16), "dp", scatter_dimension=0, tiled=True
        ).astype(jnp.float32),
        lax.psum_scatter(
            grad_down.astype(jnp.bfloat16), "dp", scatter_dimension=0, tiled=True
        ).astype(jnp.float32),
        lax.psum_scatter(
            grad_gains.astype(jnp.bfloat16), "dp", scatter_dimension=0, tiled=True
        ).astype(jnp.float32),
    )
    summed = (
        lax.psum(shares[0].astype(jnp.bfloat16), "ctx").astype(jnp.float32),
        lax.psum(shares[1].astype(jnp.bfloat16), "ctx").astype(jnp.float32),
        lax.psum(shares[2].astype(jnp.bfloat16), "ctx").astype(jnp.float32),
        lax.psum(shares[3].astype(jnp.bfloat16), "ctx").astype(jnp.float32),
        lax.psum(shares[4].astype(jnp.bfloat16), "ctx").astype(jnp.float32),
        lax.psum(shares[5].astype(jnp.bfloat16), "ctx").astype(jnp.float32),
        lax.psum(shares[6].astype(jnp.bfloat16), "ctx").astype(jnp.float32),
        lax.psum(shares[7].astype(jnp.bfloat16), "ctx").astype(jnp.float32),
    )
    updates, new_moments = lion_step(masters, moments, summed, norm_scale)
    return (layer_out, input_grad) + tuple(updates) + tuple(new_moments)


X_BIT, Y_BIT, P_BIT, H_BIT = 1, 2, 4, 8
LOW = jnp.bfloat16
WIDE = jnp.float32
VMEM_BYTES = 32 * 1024 * 1024
COLUMN_GROUPS = ((0, Y_BIT), (X_BIT, Y_BIT), (P_BIT, X_BIT), (P_BIT + Y_BIT, X_BIT))
ROW_GROUPS = ((0, Y_BIT, 0), (X_BIT, Y_BIT, 0), (0, X_BIT, 1), (Y_BIT, X_BIT, 1))


def swap(values, bit):
    return lax.ppermute(values, "dp", [(i, i ^ bit) for i in range(16)])


def swap_core(values):
    return lax.ppermute(values, "ctx", [(0, 1), (1, 0)])


def h_of(index):
    return (index // H_BIT) % 2


def row_cross(values, to_owner):
    pairs = []
    for index in range(16):
        for core in range(2):
            if (core == h_of(index)) != to_owner:
                pairs.append((index * 2 + core, (index ^ H_BIT) * 2 + core))
    return lax.ppermute(values, ("dp", "ctx"), pairs)


def gather_column_slices(own, give):
    rows = own.shape[0]
    got = swap(give, P_BIT)
    far = swap(jnp.concatenate([own, got]), H_BIT)
    first = jnp.concatenate([own, far[:rows]])
    second = jnp.concatenate([got, far[rows:]])
    first = jnp.concatenate([first, swap(first, Y_BIT)])
    second = jnp.concatenate([second, swap(second, X_BIT)])
    return first, swap(first, X_BIT), second, swap(second, Y_BIT)


def gather_row_slices(own, mine, stages=False):
    rows = own.shape[0] // 2
    far = row_cross(own, False)
    held = jnp.where(mine, own, far)
    first, second = held[:rows], held[rows:]
    came_y, came_x = swap(first, Y_BIT), swap(second, X_BIT)
    first = jnp.concatenate([first, came_y])
    second = jnp.concatenate([second, came_x])
    parts = first, swap(first, X_BIT), second, swap(second, Y_BIT)
    return (parts, [far], [came_y, came_x]) if stages else parts


def add_low(left, right):
    return (left.astype(WIDE) + right.astype(WIDE)).astype(LOW)


def scatter_column_slices(keep_one, send_one, keep_two, send_two):
    rows = keep_one.shape[0] // 4
    first = add_low(keep_one, swap(send_one, X_BIT))
    second = add_low(keep_two, swap(send_two, Y_BIT))
    first = add_low(first[: 2 * rows], swap(first[2 * rows :], Y_BIT))
    second = add_low(second[: 2 * rows], swap(second[2 * rows :], X_BIT))
    near = jnp.concatenate([first[:rows], second[:rows]])
    far = jnp.concatenate([first[rows:], second[rows:]])
    near = add_low(near, swap(far, H_BIT))
    return near[:rows], swap(near[rows:], P_BIT)


def scatter_row_slices(keep_one, send_one, keep_two, send_two, mine):
    rows = keep_one.shape[0] // 2
    first = add_low(keep_one, swap(send_one, X_BIT))
    second = add_low(keep_two, swap(send_two, Y_BIT))
    first = add_low(first[:rows], swap(first[rows:], Y_BIT))
    second = add_low(second[:rows], swap(second[rows:], X_BIT))
    held = jnp.concatenate([first, second])
    summed = add_low(held, row_cross(held, True))
    pairs = [(i * 2 + h_of(i), i * 2 + 1 - h_of(i)) for i in range(16)]
    return jnp.where(mine, summed, lax.ppermute(summed, ("dp", "ctx"), pairs))


def join_column_slices(own, partner, p_index, core):
    low_pair = jnp.where(p_index == 0, own, partner)
    high_pair = jnp.where(p_index == 0, partner, own)
    pair = jnp.stack([low_pair, high_pair])
    other = swap_core(pair)
    lower = jnp.where(core == 0, pair, other)
    upper = jnp.where(core == 0, other, pair)
    return [lower[0], lower[1], upper[0], upper[1]]


def gather_tokens(own):
    same = jnp.stack([own, swap(own, P_BIT)])
    return same, swap_core(same)


def sum_tokens(same, sibling):
    pair = same.astype(WIDE) + swap_core(sibling).astype(WIDE)
    return pair[0] + swap(pair[1].astype(LOW), P_BIT).astype(WIDE)


VM = pl.BlockSpec(memory_space=pltpu.VMEM)
SM = pl.BlockSpec(memory_space=pltpu.SMEM)
HB = pl.BlockSpec(memory_space=pl.ANY)


def call(kernel, in_specs, outs, out_specs, scratch, flops, moved, after=()):
    held, late = len(in_specs), len(after)

    def body(*refs):
        kernel(*refs[:held], *refs[held + late :])

    made = pl.pallas_call(
        body,
        in_specs=in_specs + [HB] * late,
        out_specs=out_specs,
        out_shape=[jax.ShapeDtypeStruct(shape, dtype) for shape, dtype in outs],
        scratch_shapes=scratch,
        compiler_params=pltpu.CompilerParams(vmem_limit_bytes=VMEM_BYTES),
        cost_estimate=pl.CostEstimate(flops=flops, bytes_accessed=moved, transcendentals=0),
    )
    return lambda *operands: made(*operands, *after)


def column_copies(index, parts, whole, sems, outward):
    copies = []
    rows = whole.shape[0] // 16
    for part, (base, outer) in zip(parts, COLUMN_GROUPS):
        for place in range(4):
            relative = base + (place // 2) * outer + (place % 2) * H_BIT
            start = pl.multiple_of((index ^ relative) * rows, rows)
            block = part.at[pl.ds(place * rows, rows)]
            inside = whole.at[pl.ds(start, rows)]
            ends = (inside, block) if outward else (block, inside)
            copies.append(pltpu.make_async_copy(*ends, sems.at[len(copies)]))
    return copies


def row_copies(index, parts, whole, sems, outward):
    copies = []
    rows = whole.shape[0] // 8
    for part, (base, outer, half) in zip(parts, ROW_GROUPS):
        for place in range(2):
            relative = base + place * outer
            start = pl.multiple_of((((index ^ relative) % 4) * 2 + half) * rows, rows)
            block = part.at[pl.ds(place * rows, rows)]
            inside = whole.at[pl.ds(start, rows)]
            ends = (inside, block) if outward else (block, inside)
            copies.append(pltpu.make_async_copy(*ends, sems.at[len(copies)]))
    return copies


def start_all(copies):
    for copy in copies:
        copy.start()


def wait_all(copies):
    for copy in copies:
        copy.wait()


def load_tokens(same, sibling):
    return jnp.concatenate([same[0], sibling[0], same[1], sibling[1]])


def store_tokens(values, same, sibling):
    count = same.shape[1]
    for sequence in range(2):
        at = 2 * count * sequence
        same[sequence] = values[at : at + count].astype(same.dtype)
        sibling[sequence] = values[at + count : at + 2 * count].astype(sibling.dtype)


def place_of(scalars, sequence, at):
    block = jnp.where(
        at < 128,
        jnp.where(at < 64, scalars[1 + 4 * sequence], scalars[2 + 4 * sequence]),
        jnp.where(at < 192, scalars[3 + 4 * sequence], scalars[4 + 4 * sequence]),
    )
    return block * 64 + at % 64


def allowed_of(scalars, sequence):
    rows = place_of(scalars, sequence, lax.broadcasted_iota(jnp.int32, (256, 1), 0))
    cols = place_of(scalars, sequence, lax.broadcasted_iota(jnp.int32, (1, 256), 1))
    return rows >= cols


def fill_tables(scalars, cosine, sine, cos_rows, sin_rows):
    for slot in range(8):
        start = pl.multiple_of(scalars[1 + slot] * 64, 64)
        cos_rows[slot * 64 : slot * 64 + 64] = cosine[pl.ds(start, 64)]
        sin_rows[slot * 64 : slot * 64 + 64] = sine[pl.ds(start, 64)]


def attend_kernel(
    scalars, same, sibling, part_a, part_b, part_c, part_d, cosine, sine, gains,
    mixture, pre, rotated, values_out, log_total, whole, cos_rows, sin_rows, sems,
):
    copies = column_copies(scalars[0], (part_a, part_b, part_c, part_d), whole, sems, False)
    start_all(copies)
    fill_tables(scalars, cosine, sine, cos_rows, sin_rows)
    tokens = load_tokens(same, sibling)
    wait_all(copies)
    projected = matmul(tokens, whole[...])
    pre[...] = projected[:, :768]
    values_out[...] = projected[:, 768:].astype(LOW)
    for head in range(6):
        cut = slice(head * 128, head * 128 + 128)
        raw = pre[:, cut]
        gain = gains[0:1] if head < 4 else gains[1:2]
        scale = lax.rsqrt(jnp.mean(raw * raw, axis=-1, keepdims=True) + EPSILON)
        unit = raw * scale * gain
        turned = pltpu.roll(unit, 64, 1)
        rotated[:, cut] = (unit * cos_rows[...] + turned * sin_rows[...]).astype(LOW)
    for sequence in range(2):
        rows = slice(sequence * 256, sequence * 256 + 256)
        allowed = allowed_of(scalars, sequence)
        tops = []
        for head in range(4):
            group = head // 2
            queries = rotated[rows, head * 128 : head * 128 + 128]
            keys = rotated[rows, 512 + group * 128 : 640 + group * 128]
            scores = jnp.where(allowed, contract_cols(queries, keys) * (128**-0.5), -1e30)
            top = jnp.max(scores, axis=-1, keepdims=True)
            weights = jnp.exp(scores - top)
            total = jnp.sum(weights, axis=-1, keepdims=True)
            probs = (weights / total).astype(LOW)
            mixed = matmul(probs, values_out[rows, group * 128 : group * 128 + 128])
            mixture[rows, head * 128 : head * 128 + 128] = mixed.astype(LOW)
            tops.append(jnp.broadcast_to(top + jnp.log(total), (256, 128)))
        lane = lax.broadcasted_iota(jnp.int32, (256, 128), 1)
        log_total[rows] = jnp.where(
            lane < 2, jnp.where(lane < 1, tops[0], tops[1]), jnp.where(lane < 3, tops[2], tops[3])
        )


def attend(scalars, tokens, parts, tables, gains, after=()):
    return call(
        attend_kernel,
        [SM, VM, VM, HB, HB, HB, HB, VM, VM, VM],
        [((512, 512), LOW), ((512, 768), WIDE), ((512, 768), LOW), ((512, 256), LOW), ((512, 128), WIDE)],
        [VM] * 5,
        [
            pltpu.VMEM((1024, 1024), LOW),
            pltpu.VMEM((512, 128), WIDE),
            pltpu.VMEM((512, 128), WIDE),
            pltpu.SemaphoreType.DMA((16,)),
        ],
        2 * 10**9,
        8 * 10**6,
        after,
    )(scalars, *tokens, *parts, *tables, gains)


def output_kernel(scalars, mixture, part_a, part_b, part_c, part_d, same, sibling, whole, sems):
    copies = row_copies(scalars[0], (part_a, part_b, part_c, part_d), whole, sems, False)
    start_all(copies)
    wait_all(copies)
    store_tokens(matmul(mixture[...], whole[...]), same, sibling)


def row_product(scalars, left, parts, after=()):
    depth = left.shape[1]
    return call(
        output_kernel,
        [SM, VM, HB, HB, HB, HB],
        [((2, 128, 1024), LOW)] * 2,
        [VM] * 2,
        [pltpu.VMEM((depth, 1024), LOW), pltpu.SemaphoreType.DMA((8,))],
        2 * 512 * 1024 * depth,
        4 * 10**6,
        after,
    )(scalars, left, *parts)


def gate_kernel(
    scalars, same, sibling, part_a, part_b, part_c, part_d, gate_up, active, whole, sems
):
    copies = column_copies(scalars[0], (part_a, part_b, part_c, part_d), whole, sems, False)
    start_all(copies)
    tokens = load_tokens(same, sibling)
    wait_all(copies)
    for at in range(0, 768, 256):
        gate = matmul(tokens, whole[:, at : at + 256])
        upward = matmul(tokens, whole[:, 768 + at : 1024 + at])
        gate_up[:, at : at + 256] = gate
        gate_up[:, 768 + at : 1024 + at] = upward
        active[:, at : at + 256] = (gate * jax.nn.sigmoid(gate) * upward).astype(LOW)


def gate_product(scalars, tokens, parts, after=()):
    return call(
        gate_kernel,
        [SM, VM, VM, HB, HB, HB, HB],
        [((512, 1536), WIDE), ((512, 768), LOW)],
        [VM] * 2,
        [pltpu.VMEM((1024, 1536), LOW), pltpu.SemaphoreType.DMA((16,))],
        2 * 512 * 1024 * 1536,
        10 * 10**6,
        after,
    )(scalars, *tokens, *parts)


def swiglu_back_kernel(
    scalars, same, sibling, gate_up, row_a, row_b, row_c, row_d, col_a, col_b, col_c, col_d,
    grad_gate_up, grad_same, grad_sibling, down, both, row_sems, col_sems,
):
    down_copies = row_copies(scalars[0], (row_a, row_b, row_c, row_d), down, row_sems, False)
    both_copies = column_copies(scalars[0], (col_a, col_b, col_c, col_d), both, col_sems, False)
    start_all(down_copies)
    start_all(both_copies)
    grad_out = load_tokens(same, sibling)
    wait_all(down_copies)
    for at in range(0, 768, 256):
        grad_active = contract_cols(grad_out, down[at : at + 256])
        gate = gate_up[:, at : at + 256]
        upward = gate_up[:, 768 + at : 1024 + at]
        sigmoid = jax.nn.sigmoid(gate)
        grad_gate_up[:, at : at + 256] = (
            grad_active * upward * (sigmoid * (1.0 + gate * (1.0 - sigmoid)))
        ).astype(LOW)
        grad_gate_up[:, 768 + at : 1024 + at] = (grad_active * (gate * sigmoid)).astype(LOW)
    wait_all(both_copies)
    store_tokens(contract_cols(grad_gate_up[...], both[...]), grad_same, grad_sibling)


def swiglu_back(scalars, grad_out, gate_up, down_parts, gate_up_parts, after=()):
    return call(
        swiglu_back_kernel,
        [SM, VM, VM, VM] + [HB] * 8,
        [((512, 1536), LOW), ((2, 128, 1024), LOW), ((2, 128, 1024), LOW)],
        [VM] * 3,
        [
            pltpu.VMEM((768, 1024), LOW),
            pltpu.VMEM((1024, 1536), LOW),
            pltpu.SemaphoreType.DMA((8,)),
            pltpu.SemaphoreType.DMA((16,)),
        ],
        2 * 512 * 1024 * 2304,
        12 * 10**6,
        after,
    )(scalars, *grad_out, gate_up, *down_parts, *gate_up_parts)


def attend_back_kernel(
    scalars, same, sibling, part_a, part_b, part_c, part_d, pre, rotated, values, log_total,
    cosine, sine, gains, grad_all, grad_gains, whole, cos_rows, sin_rows, grad_rot, sems,
):
    copies = row_copies(scalars[0], (part_a, part_b, part_c, part_d), whole, sems, False)
    start_all(copies)
    fill_tables(scalars, cosine, sine, cos_rows, sin_rows)
    branch = load_tokens(same, sibling)
    wait_all(copies)
    grad_mixed = contract_cols(branch, whole[...]).astype(LOW)
    scaling = 128**-0.5
    for sequence in range(2):
        rows = slice(sequence * 256, sequence * 256 + 256)
        allowed = allowed_of(scalars, sequence)
        for group in range(2):
            keys = rotated[rows, 512 + group * 128 : 640 + group * 128]
            value_rows = values[rows, group * 128 : group * 128 + 128]
            grad_keys = jnp.zeros((256, 128), WIDE)
            grad_values = jnp.zeros((256, 128), WIDE)
            for head in (2 * group, 2 * group + 1):
                cut = slice(head * 128, head * 128 + 128)
                queries = rotated[rows, cut]
                grad_mix = grad_mixed[rows, cut]
                scores = jnp.where(allowed, contract_cols(queries, keys) * scaling, -1e30)
                probs = jnp.exp(scores - log_total[rows, head : head + 1])
                grad_values += contract_rows(probs.astype(LOW), grad_mix)
                grad_probs = contract_cols(grad_mix, value_rows)
                inner = jnp.sum(probs * grad_probs, axis=-1, keepdims=True)
                grad_scores = (probs * (grad_probs - inner)).astype(LOW)
                grad_rot[rows, cut] = matmul(grad_scores, keys) * scaling
                grad_keys += contract_rows(grad_scores, queries)
            grad_rot[rows, 512 + group * 128 : 640 + group * 128] = grad_keys * scaling
            grad_all[rows, 768 + group * 128 : 896 + group * 128] = grad_values.astype(LOW)
    gain_sums = [jnp.zeros((1, 128), WIDE), jnp.zeros((1, 128), WIDE)]
    for head in range(6):
        cut = slice(head * 128, head * 128 + 128)
        which = 0 if head < 4 else 1
        raw = pre[:, cut]
        scale = lax.rsqrt(jnp.mean(raw * raw, axis=-1, keepdims=True) + EPSILON)
        unit = raw * scale
        coming = grad_rot[:, cut]
        back = coming * cos_rows[...] - pltpu.roll(coming, 64, 1) * sin_rows[...]
        gain_sums[which] += jnp.sum(back * unit, axis=0, keepdims=True)
        back = back * gains[which : which + 1]
        along = jnp.mean(back * unit, axis=-1, keepdims=True)
        grad_all[:, cut] = (scale * (back - unit * along)).astype(LOW)
    grad_gains[...] = jnp.zeros((8, 128), WIDE)
    grad_gains[0:1] = gain_sums[0]
    grad_gains[1:2] = gain_sums[1]


def attend_back_call(scalars, branch, parts, pre, rotated, values, log_total, tables, gains, after=()):
    return call(
        attend_back_kernel,
        [SM, VM, VM, HB, HB, HB, HB] + [VM] * 7,
        [((512, 1024), LOW), ((8, 128), WIDE)],
        [VM] * 2,
        [
            pltpu.VMEM((512, 1024), LOW),
            pltpu.VMEM((512, 128), WIDE),
            pltpu.VMEM((512, 128), WIDE),
            pltpu.VMEM((512, 768), WIDE),
            pltpu.SemaphoreType.DMA((8,)),
        ],
        2 * 10**9,
        8 * 10**6,
        after,
    )(scalars, *branch, *parts, pre, rotated, values, log_total, *tables, gains)


def column_back_kernel(scalars, grads, part_a, part_b, part_c, part_d, same, sibling, whole, sems):
    copies = column_copies(scalars[0], (part_a, part_b, part_c, part_d), whole, sems, False)
    start_all(copies)
    wait_all(copies)
    store_tokens(contract_cols(grads[...], whole[...]), same, sibling)


def column_back(scalars, grads, parts, after=()):
    width = grads.shape[1]
    return call(
        column_back_kernel,
        [SM, VM, HB, HB, HB, HB],
        [((2, 128, 1024), LOW)] * 2,
        [VM] * 2,
        [pltpu.VMEM((1024, width), LOW), pltpu.SemaphoreType.DMA((16,))],
        2 * 512 * 1024 * width,
        5 * 10**6,
        after,
    )(scalars, grads, *parts)


def column_grad_kernel(
    scalars, same, sibling, grads, keep_one, send_one, keep_two, send_two, whole, sems
):
    for at in range(0, 1024, 256):
        cut = slice(at, at + 256)
        left = jnp.concatenate(
            [same[0, :, cut], sibling[0, :, cut], same[1, :, cut], sibling[1, :, cut]]
        )
        whole[cut] = contract_rows(left, grads[...]).astype(LOW)
    copies = column_copies(
        scalars[0], (keep_one, send_one, keep_two, send_two), whole, sems, True
    )
    start_all(copies)
    wait_all(copies)


def column_grad(scalars, tokens, grads, after=()):
    width = grads.shape[1]
    return call(
        column_grad_kernel,
        [SM, VM, VM, VM],
        [((256, width), LOW)] * 4,
        [HB] * 4,
        [pltpu.VMEM((1024, width), LOW), pltpu.SemaphoreType.DMA((16,))],
        2 * 512 * 1024 * width,
        6 * 10**6,
        after,
    )(scalars, *tokens, grads)


def row_grad_kernel(
    scalars, left, same, sibling, keep_one, send_one, keep_two, send_two, whole, sems
):
    right = load_tokens(same, sibling)
    for at in range(0, whole.shape[0], 256):
        cut = slice(at, at + 256)
        whole[cut] = contract_rows(left[:, cut], right).astype(LOW)
    copies = row_copies(scalars[0], (keep_one, send_one, keep_two, send_two), whole, sems, True)
    start_all(copies)
    wait_all(copies)


def row_grad(scalars, left, tokens, after=()):
    depth = left.shape[1]
    return call(
        row_grad_kernel,
        [SM, VM, VM, VM],
        [((depth // 4, 1024), LOW)] * 4,
        [HB] * 4,
        [pltpu.VMEM((depth, 1024), LOW), pltpu.SemaphoreType.DMA((8,))],
        2 * 512 * 1024 * depth,
        4 * 10**6,
        after,
    )(scalars, left, *tokens)


def fast_body(
    hidden_in,
    cotangent,
    block_order,
    w_query,
    key_weight,
    value_weight,
    w_output,
    w_gate,
    w_up,
    w_down,
    norm_gains,
    momentum_query,
    key_momentum,
    value_momentum,
    momentum_output,
    momentum_gate,
    momentum_up,
    momentum_down,
    momentum_gains,
):
    index = lax.axis_index("dp")
    core = lax.axis_index("ctx")
    p_index = (index // P_BIT) % 2
    mine = h_of(index) == core
    slice_own = 2 * core + p_index
    slice_give = 2 * core + 1 - p_index

    def column_slice(weight, which):
        size = weight.shape[1] // 4
        return lax.dynamic_slice_in_dim(weight, which * size, size, axis=1).astype(LOW)

    def column_pack(weights, which):
        return jnp.concatenate([column_slice(weight, which) for weight in weights], axis=1)

    gains_low = norm_gains.astype(LOW)[None]
    for bit in (P_BIT, H_BIT, Y_BIT, X_BIT):
        gains_low = jnp.concatenate([gains_low, swap(gains_low, bit)])
    order = [0]
    for bit in (P_BIT, H_BIT, Y_BIT, X_BIT):
        order = order + [o ^ bit for o in order]
    inverse = [0] * 16
    for at, relative in enumerate(order):
        inverse[relative] = at
    lookup = jnp.array(inverse, jnp.int32)[index ^ jnp.arange(16)]
    gains_all = jnp.take(gains_low, lookup, axis=0).reshape(-1).astype(WIDE)

    width = hidden_in.shape[2]
    head_size = 128
    gain_attn = gains_all[:width]
    gain_mlp = gains_all[width : 2 * width]
    head_gains = gains_all[2 * width :].reshape(2, head_size)

    qkv = (w_query, key_weight, value_weight)
    qkv_parts = gather_column_slices(column_pack(qkv, slice_own), column_pack(qkv, slice_give))
    output_parts = gather_row_slices(w_output.astype(LOW), mine)
    gate_up = (w_gate, w_up)
    gate_up_parts = gather_column_slices(
        column_pack(gate_up, slice_own), column_pack(gate_up, slice_give)
    )
    down_parts, _, down_first = gather_row_slices(w_down.astype(LOW), mine, True)

    tokens_own = hidden_in[0]
    count = tokens_own.shape[0]
    orders = jnp.concatenate([block_order, swap(block_order, P_BIT)])
    orders = jnp.where(core == 0, orders, jnp.roll(orders, 2, axis=1))
    scalars = jnp.concatenate([index[None], orders.reshape(-1)]).astype(jnp.int32)
    cosine, sine_table = rotary_tables(jnp.arange(2 * count, dtype=jnp.int32), head_size)
    sign = jnp.where(jnp.arange(head_size) < head_size // 2, -1.0, 1.0)
    tables = (cosine, sine_table * sign)

    tokens_f = tokens_own.astype(WIDE)
    normed_f, norm_pull = jax.vjp(rms_norm, tokens_f, gain_attn)
    normed = gather_tokens(normed_f.astype(LOW))
    grad_out = gather_tokens(cotangent[0])

    mixed_low, pre, rotated, value_low, log_total = attend(
        scalars, normed, qkv_parts, tables, head_gains
    )
    attended = sum_tokens(*row_product(scalars, mixed_low, output_parts, down_first))
    middle = tokens_f + attended
    normed_two_f, norm_two_pull = jax.vjp(rms_norm, middle, gain_mlp)
    normed_two = gather_tokens(normed_two_f.astype(LOW))
    gate_up_act, active = gate_product(scalars, normed_two, gate_up_parts, down_parts)
    grad_gate_up, back_same, back_sibling = swiglu_back(
        scalars, grad_out, gate_up_act, down_parts, gate_up_parts
    )
    grad_down = row_grad(scalars, active, grad_out, [back_same])
    grad_normed_two = sum_tokens(back_same, back_sibling)
    grad_gate_up_mat = column_grad(scalars, normed_two, grad_gate_up, [back_same])

    grad_middle_norm, grad_gain_mlp = norm_two_pull(grad_normed_two)
    grad_middle = cotangent[0].astype(WIDE) + grad_middle_norm
    grad_branch = gather_tokens(grad_middle.astype(LOW))
    grad_qkv, grad_head_gains = attend_back_call(
        scalars, grad_branch, output_parts, pre, rotated, value_low, log_total, tables, head_gains
    )
    grad_qkv_mat = column_grad(scalars, normed, grad_qkv, ())
    grad_output_mat = row_grad(scalars, mixed_low, grad_branch, [grad_qkv_mat[0]])
    grad_normed = sum_tokens(*column_back(scalars, grad_qkv, qkv_parts, [grad_qkv_mat[0]]))
    grad_tokens_norm, grad_gain_attn = norm_pull(grad_normed)
    input_grad = (grad_middle + grad_tokens_norm).astype(LOW)[None]

    layer_sum = sum_tokens(*row_product(scalars, active, down_parts, [grad_qkv_mat[0]]))
    layer_out = (middle + layer_sum).astype(LOW)[None]
    grad_gains = jnp.concatenate([grad_gain_attn, grad_gain_mlp, grad_head_gains[:2].reshape(-1)])
    grad_gains = grad_gains.reshape(16, -1)
    grad_gains = grad_gains + swap_core(grad_gains.astype(LOW)).astype(WIDE)
    for bit in (P_BIT, H_BIT, Y_BIT, X_BIT):
        grad_gains = grad_gains + swap(grad_gains.astype(LOW), bit).astype(WIDE)
    grad_gains = lax.dynamic_index_in_dim(grad_gains, index, keepdims=False)

    down_sum = scatter_row_slices(*grad_down, mine)
    gate_up_sum = join_column_slices(*scatter_column_slices(*grad_gate_up_mat), p_index, core)
    output_sum = scatter_row_slices(*grad_output_mat, mine)
    qkv_sum = join_column_slices(*scatter_column_slices(*grad_qkv_mat), p_index, core)

    def columns(parts, start, size):
        return jnp.concatenate([part[:, start : start + size] for part in parts], axis=1)

    query_width = w_query.shape[1] // 4
    kv_width = key_weight.shape[1] // 4
    hidden_units = w_gate.shape[1] // 4
    sums = (
        columns(qkv_sum, 0, query_width),
        columns(qkv_sum, query_width, kv_width),
        columns(qkv_sum, query_width + kv_width, kv_width),
        output_sum,
        columns(gate_up_sum, 0, hidden_units),
        columns(gate_up_sum, hidden_units, hidden_units),
        down_sum,
        grad_gains,
    )
    masters = (w_query, key_weight, value_weight, w_output, w_gate, w_up, w_down, norm_gains)
    moments = (
        momentum_query,
        key_momentum,
        value_momentum,
        momentum_output,
        momentum_gate,
        momentum_up,
        momentum_down,
        momentum_gains,
    )
    norm_scale = lax.rsqrt(jnp.float32(16 * 2 * count))
    summed = tuple(part.astype(WIDE) for part in sums)
    updates, new_moments = lion_step(masters, moments, summed, norm_scale)
    return (layer_out, input_grad) + tuple(updates) + tuple(new_moments)


def solution(mesh):
    body = fast_body if dict(mesh.shape) == {"dp": 16, "ctx": 2} else general_body
    return jax.shard_map(
        body,
        mesh=mesh,
        in_specs=(
            P("dp", "ctx", None),
            P("dp", "ctx", None),
            P("dp", None),
            P("dp", None),
            P("dp", None),
            P("dp", None),
            P("dp", None),
            P("dp", None),
            P("dp", None),
            P("dp", None),
            P("dp"),
            P("dp", None),
            P("dp", None),
            P("dp", None),
            P("dp", None),
            P("dp", None),
            P("dp", None),
            P("dp", None),
            P("dp"),
        ),
        out_specs=(
            P("dp", "ctx", None),
            P("dp", "ctx", None),
            P("dp", None),
            P("dp", None),
            P("dp", None),
            P("dp", None),
            P("dp", None),
            P("dp", None),
            P("dp", None),
            P("dp"),
            P("dp", None),
            P("dp", None),
            P("dp", None),
            P("dp", None),
            P("dp", None),
            P("dp", None),
            P("dp", None),
            P("dp"),
        ),
        check_vma=False,
    )
```

```python
import jax
import jax.numpy as jnp
from jax import lax
from jax.experimental import pallas as pl
from jax.experimental.pallas import tpu as pltpu
from jax.sharding import PartitionSpec as P

EPSILON = 1e-06
THETA = 1000000.0
BETA_ONE = 0.9
BETA_TWO = 0.5
SOFTEN = 0.005
DECAY_FACTOR = 1.0


def rms_norm(values, gain_vec):
    return (
        values * lax.rsqrt(jnp.mean(values * values, axis=-1, keepdims=True) + EPSILON) * gain_vec
    )


def rotary_tables(positions, head_size):
    half_size = head_size // 2
    frequency = THETA ** (-(jnp.arange(half_size, dtype=jnp.float32) * 2.0 / head_size))
    angles = positions.astype(jnp.float32)[:, None] * frequency[None, :]
    angles = jnp.concatenate([angles, angles], axis=1)
    return (jnp.cos(angles), jnp.sin(angles))


def rotate(values, cosine, sine_table):
    half_size = values.shape[-1] // 2
    turned = jnp.concatenate([-values[..., half_size:], values[..., :half_size]], axis=-1)
    return values * cosine[:, None, :] + turned * sine_table[:, None, :]


def head_prep(projected, gain_vec, cosine, sine_table):
    shaped = projected.reshape(projected.shape[0], -1, gain_vec.shape[0])
    return rotate(rms_norm(shaped, gain_vec), cosine, sine_table)


def matmul(left, right):
    return jnp.dot(left, right, preferred_element_type=jnp.float32)


def contract_rows(left, right):
    return lax.dot_general(
        left, right, (((0,), (0,)), ((), ())), preferred_element_type=jnp.float32
    )


def contract_cols(left, right):
    return lax.dot_general(
        left, right, (((1,), (1,)), ((), ())), preferred_element_type=jnp.float32
    )


def head_scores(queries, key_row_block, query_pos, key_pos):
    scaling = queries.shape[-1] ** (-0.5)
    scores = (
        jnp.einsum("trd,kd->rtk", queries, key_row_block, preferred_element_type=jnp.float32)
        * scaling
    )
    allowed = query_pos[:, None] >= key_pos[None, :]
    return jnp.where(allowed[None], scores, -1e30)


def attend_head(query_pos, key_pos):

    def attend(group_item):
        queries, key_row_block, value_row_block = group_item
        scores = head_scores(queries, key_row_block, query_pos, key_pos)
        row_top = jnp.max(scores, axis=-1, keepdims=True)
        weights = jnp.exp(scores - row_top)
        row_total = jnp.sum(weights, axis=-1, keepdims=True)
        probs_low = (weights / row_total).astype(jnp.bfloat16)
        mixture = jnp.einsum(
            "rtk,kd->trd", probs_low, value_row_block, preferred_element_type=jnp.float32
        )
        return (mixture, (row_top + jnp.log(row_total))[..., 0])

    return attend


def attend_back(query_pos, key_pos):

    def backward(group_item):
        queries, key_row_block, value_row_block, grad_mix, log_total = group_item
        scaling = queries.shape[-1] ** (-0.5)
        scores = head_scores(queries, key_row_block, query_pos, key_pos)
        probs = jnp.exp(scores - log_total[..., None])
        grad_values = jnp.einsum(
            "rtk,trd->kd", probs.astype(jnp.bfloat16), grad_mix, preferred_element_type=jnp.float32
        )
        grad_probs = jnp.einsum(
            "trd,kd->rtk", grad_mix, value_row_block, preferred_element_type=jnp.float32
        )
        inner = jnp.sum(probs * grad_probs, axis=-1, keepdims=True)
        grad_scores = (probs * (grad_probs - inner)).astype(jnp.bfloat16)
        grad_queries = (
            jnp.einsum(
                "rtk,kd->trd", grad_scores, key_row_block, preferred_element_type=jnp.float32
            )
            * scaling
        )
        grad_keys = (
            jnp.einsum("rtk,trd->kd", grad_scores, queries, preferred_element_type=jnp.float32)
            * scaling
        )
        return (grad_queries, grad_keys, grad_values)

    return backward


def lion_step(masters, moments, gradients, norm_scale):
    updates = []
    new_moments = []
    for tensor_index in range(8):
        scaled = gradients[tensor_index] * norm_scale
        moment_arr = moments[tensor_index]
        blend_arr = BETA_ONE * moment_arr + (1.0 - BETA_ONE) * scaled
        direction = blend_arr / jnp.sqrt(blend_arr * blend_arr + SOFTEN)
        decay_here = DECAY_FACTOR if tensor_index < 7 else 0.0
        updates.append(direction + decay_here * masters[tensor_index])
        new_moments.append(BETA_TWO * moment_arr + (1.0 - BETA_TWO) * scaled)
    return (updates, new_moments)


def general_body(
    hidden_in,
    cotangent,
    block_order,
    w_query,
    key_weight,
    value_weight,
    w_output,
    w_gate,
    w_up,
    w_down,
    norm_gains,
    momentum_query,
    key_momentum,
    value_momentum,
    momentum_output,
    momentum_gate,
    momentum_up,
    momentum_down,
    momentum_gains,
):
    copies = (
        lax.all_gather(w_query.astype(jnp.bfloat16), "dp", axis=0, tiled=True),
        lax.all_gather(key_weight.astype(jnp.bfloat16), "dp", axis=0, tiled=True),
        lax.all_gather(value_weight.astype(jnp.bfloat16), "dp", axis=0, tiled=True),
        lax.all_gather(w_output.astype(jnp.bfloat16), "dp", axis=0, tiled=True),
        lax.all_gather(w_gate.astype(jnp.bfloat16), "dp", axis=0, tiled=True),
        lax.all_gather(w_up.astype(jnp.bfloat16), "dp", axis=0, tiled=True),
        lax.all_gather(w_down.astype(jnp.bfloat16), "dp", axis=0, tiled=True),
        lax.all_gather(norm_gains.astype(jnp.bfloat16), "dp", axis=0, tiled=True),
    )
    query_mat, key_mat, value_mat, output_mat, gate_mat, up_mat, down_mat, gains_low = copies
    gains_all = gains_low.astype(jnp.float32)
    width = hidden_in.shape[2]
    head_size = (gains_all.shape[0] - 2 * width) // 2
    kv_heads = key_mat.shape[1] // head_size
    query_heads = query_mat.shape[1] // head_size
    group_repeat_count = query_heads // kv_heads
    gain_attn = gains_all[:width]
    gain_mlp = gains_all[width : 2 * width]
    gain_query = gains_all[2 * width : 2 * width + head_size]
    gain_key = gains_all[2 * width + head_size :]
    tokens_in = hidden_in[0]
    token_count = tokens_in.shape[0]
    block_size = token_count // 2
    slot_order = block_order[0]
    key_pos = (
        slot_order[:, None] * block_size + jnp.arange(block_size, dtype=jnp.int32)[None, :]
    ).reshape(-1)
    query_pos = lax.dynamic_slice_in_dim(key_pos, lax.axis_index("ctx") * token_count, token_count)
    cosine, sine_table = rotary_tables(query_pos, head_size)
    tokens_f = tokens_in.astype(jnp.float32)
    normed_f, norm_pull = jax.vjp(rms_norm, tokens_f, gain_attn)
    normalized_input = normed_f.astype(jnp.bfloat16)
    query_pre = matmul(normalized_input, query_mat)
    key_pre = matmul(normalized_input, key_mat)
    value_low = matmul(normalized_input, value_mat).astype(jnp.bfloat16)
    query_rot, query_pull = jax.vjp(
        lambda projected, gain_vec: head_prep(projected, gain_vec, cosine, sine_table),
        query_pre,
        gain_query,
    )
    key_rot, key_pull = jax.vjp(
        lambda projected, gain_vec: head_prep(projected, gain_vec, cosine, sine_table),
        key_pre,
        gain_key,
    )
    query_low = query_rot.astype(jnp.bfloat16)
    key_heads = key_rot.astype(jnp.bfloat16).transpose(1, 0, 2)
    value_heads = value_low.reshape(token_count, kv_heads, head_size).transpose(1, 0, 2)
    gathered = (
        lax.all_gather(key_heads, "ctx", axis=1, tiled=True),
        lax.all_gather(value_heads, "ctx", axis=1, tiled=True),
    )
    query_groups = query_low.reshape(
        token_count, kv_heads, group_repeat_count, head_size
    ).transpose(1, 0, 2, 3)
    mixture, log_total = lax.map(
        attend_head(query_pos, key_pos), (query_groups, gathered[0], gathered[1])
    )
    mixed_low = mixture.transpose(1, 0, 2, 3).reshape(token_count, -1).astype(jnp.bfloat16)
    middle = tokens_f + matmul(mixed_low, output_mat)
    normed_two_f, norm_two_pull = jax.vjp(rms_norm, middle, gain_mlp)
    normed_two = normed_two_f.astype(jnp.bfloat16)
    gate_act = matmul(normed_two, gate_mat)
    upward = matmul(normed_two, up_mat)
    active_f, swiglu_pull = jax.vjp(
        lambda gate_in, up_in: jax.nn.silu(gate_in) * up_in, gate_act, upward
    )
    active = active_f.astype(jnp.bfloat16)
    layer_out = (middle + matmul(active, down_mat)).astype(jnp.bfloat16)[None]
    grad_out = cotangent[0]
    grad_down = contract_rows(active, grad_out)
    grad_active = contract_cols(grad_out, down_mat)
    grad_gate_f, grad_up_f = swiglu_pull(grad_active)
    grad_gate = grad_gate_f.astype(jnp.bfloat16)
    grad_upward = grad_up_f.astype(jnp.bfloat16)
    grad_gate_mat = contract_rows(normed_two, grad_gate)
    grad_up_mat = contract_rows(normed_two, grad_upward)
    grad_normed_two = contract_cols(grad_gate, gate_mat) + contract_cols(grad_upward, up_mat)
    grad_middle_norm, grad_gain_mlp = norm_two_pull(grad_normed_two)
    grad_middle = grad_out.astype(jnp.float32) + grad_middle_norm
    grad_branch = grad_middle.astype(jnp.bfloat16)
    grad_output_mat = contract_rows(mixed_low, grad_branch)
    grad_mixed = contract_cols(grad_branch, output_mat).astype(jnp.bfloat16)
    grad_groups = grad_mixed.reshape(
        token_count, kv_heads, group_repeat_count, head_size
    ).transpose(1, 0, 2, 3)
    grad_query_groups, grad_key_all, grad_value_all = lax.map(
        attend_back(query_pos, key_pos),
        (query_groups, gathered[0], gathered[1], grad_groups, log_total),
    )
    grad_key_own, grad_value_own = (
        lax.psum_scatter(
            grad_key_all.astype(jnp.bfloat16), "ctx", scatter_dimension=1, tiled=True
        ).astype(jnp.float32),
        lax.psum_scatter(
            grad_value_all.astype(jnp.bfloat16), "ctx", scatter_dimension=1, tiled=True
        ).astype(jnp.float32),
    )
    grad_query_rot = grad_query_groups.transpose(1, 0, 2, 3).reshape(
        token_count, query_heads, head_size
    )
    grad_query_pre, grad_gain_query = query_pull(grad_query_rot)
    grad_key_pre, grad_gain_key = key_pull(grad_key_own.transpose(1, 0, 2))
    grad_query_low = grad_query_pre.astype(jnp.bfloat16)
    grad_key_low = grad_key_pre.astype(jnp.bfloat16)
    grad_value_low = grad_value_own.transpose(1, 0, 2).reshape(token_count, -1).astype(jnp.bfloat16)
    grad_query_mat = contract_rows(normalized_input, grad_query_low)
    grad_key_mat = contract_rows(normalized_input, grad_key_low)
    grad_value_mat = contract_rows(normalized_input, grad_value_low)
    grad_normed = (
        contract_cols(grad_query_low, query_mat)
        + contract_cols(grad_key_low, key_mat)
        + contract_cols(grad_value_low, value_mat)
    )
    grad_tokens_norm, grad_gain_attn = norm_pull(grad_normed)
    input_grad = (grad_middle + grad_tokens_norm).astype(jnp.bfloat16)[None]
    grad_gains = jnp.concatenate([grad_gain_attn, grad_gain_mlp, grad_gain_query, grad_gain_key])
    masters = (w_query, key_weight, value_weight, w_output, w_gate, w_up, w_down, norm_gains)
    moments = (
        momentum_query,
        key_momentum,
        value_momentum,
        momentum_output,
        momentum_gate,
        momentum_up,
        momentum_down,
        momentum_gains,
    )
    token_total = lax.axis_size("dp") * key_pos.shape[0]
    norm_scale = lax.rsqrt(jnp.float32(token_total))
    shares = (
        lax.psum_scatter(
            grad_query_mat.astype(jnp.bfloat16), "dp", scatter_dimension=0, tiled=True
        ).astype(jnp.float32),
        lax.psum_scatter(
            grad_key_mat.astype(jnp.bfloat16), "dp", scatter_dimension=0, tiled=True
        ).astype(jnp.float32),
        lax.psum_scatter(
            grad_value_mat.astype(jnp.bfloat16), "dp", scatter_dimension=0, tiled=True
        ).astype(jnp.float32),
        lax.psum_scatter(
            grad_output_mat.astype(jnp.bfloat16), "dp", scatter_dimension=0, tiled=True
        ).astype(jnp.float32),
        lax.psum_scatter(
            grad_gate_mat.astype(jnp.bfloat16), "dp", scatter_dimension=0, tiled=True
        ).astype(jnp.float32),
        lax.psum_scatter(
            grad_up_mat.astype(jnp.bfloat16), "dp", scatter_dimension=0, tiled=True
        ).astype(jnp.float32),
        lax.psum_scatter(
            grad_down.astype(jnp.bfloat16), "dp", scatter_dimension=0, tiled=True
        ).astype(jnp.float32),
        lax.psum_scatter(
            grad_gains.astype(jnp.bfloat16), "dp", scatter_dimension=0, tiled=True
        ).astype(jnp.float32),
    )
    summed = (
        lax.psum(shares[0].astype(jnp.bfloat16), "ctx").astype(jnp.float32),
        lax.psum(shares[1].astype(jnp.bfloat16), "ctx").astype(jnp.float32),
        lax.psum(shares[2].astype(jnp.bfloat16), "ctx").astype(jnp.float32),
        lax.psum(shares[3].astype(jnp.bfloat16), "ctx").astype(jnp.float32),
        lax.psum(shares[4].astype(jnp.bfloat16), "ctx").astype(jnp.float32),
        lax.psum(shares[5].astype(jnp.bfloat16), "ctx").astype(jnp.float32),
        lax.psum(shares[6].astype(jnp.bfloat16), "ctx").astype(jnp.float32),
        lax.psum(shares[7].astype(jnp.bfloat16), "ctx").astype(jnp.float32),
    )
    updates, new_moments = lion_step(masters, moments, summed, norm_scale)
    return (layer_out, input_grad) + tuple(updates) + tuple(new_moments)


X_BIT, Y_BIT, P_BIT, H_BIT = 1, 2, 4, 8
LOW = jnp.bfloat16
WIDE = jnp.float32
VMEM_BYTES = 24 * 1024 * 1024
COLUMN_GROUPS = ((0, Y_BIT), (X_BIT, Y_BIT), (P_BIT, X_BIT), (P_BIT + Y_BIT, X_BIT))
ROW_GROUPS = ((0, Y_BIT, 0), (X_BIT, Y_BIT, 0), (0, X_BIT, 1), (Y_BIT, X_BIT, 1))


def swap(values, bit):
    return lax.ppermute(values, "dp", [(i, i ^ bit) for i in range(16)])


def swap_core(values):
    return lax.ppermute(values, "ctx", [(0, 1), (1, 0)])


def h_of(index):
    return (index // H_BIT) % 2


def row_cross(values, to_owner):
    pairs = []
    for index in range(16):
        for core in range(2):
            if (core == h_of(index)) != to_owner:
                pairs.append((index * 2 + core, (index ^ H_BIT) * 2 + core))
    return lax.ppermute(values, ("dp", "ctx"), pairs)


def gather_column_slices(own, give):
    rows = own.shape[0]
    got = swap(give, P_BIT)
    far = swap(jnp.concatenate([own, got]), H_BIT)
    first = jnp.concatenate([own, far[:rows]])
    second = jnp.concatenate([got, far[rows:]])
    first = jnp.concatenate([first, swap(first, Y_BIT)])
    second = jnp.concatenate([second, swap(second, X_BIT)])
    return first, swap(first, X_BIT), second, swap(second, Y_BIT)


def gather_row_slices(own, mine, stages=False):
    rows = own.shape[0] // 2
    far = row_cross(own, False)
    held = jnp.where(mine, own, far)
    first, second = held[:rows], held[rows:]
    came_y, came_x = swap(first, Y_BIT), swap(second, X_BIT)
    first = jnp.concatenate([first, came_y])
    second = jnp.concatenate([second, came_x])
    parts = first, swap(first, X_BIT), second, swap(second, Y_BIT)
    return (parts, [far], [came_y, came_x]) if stages else parts


def add_low(left, right):
    return (left.astype(WIDE) + right.astype(WIDE)).astype(LOW)


def scatter_column_slices(keep_one, send_one, keep_two, send_two):
    rows = keep_one.shape[0] // 4
    first = add_low(keep_one, swap(send_one, X_BIT))
    second = add_low(keep_two, swap(send_two, Y_BIT))
    first = add_low(first[: 2 * rows], swap(first[2 * rows :], Y_BIT))
    second = add_low(second[: 2 * rows], swap(second[2 * rows :], X_BIT))
    near = jnp.concatenate([first[:rows], second[:rows]])
    far = jnp.concatenate([first[rows:], second[rows:]])
    near = add_low(near, swap(far, H_BIT))
    return near[:rows], swap(near[rows:], P_BIT)


def scatter_row_slices(keep_one, send_one, keep_two, send_two, mine):
    rows = keep_one.shape[0] // 2
    first = add_low(keep_one, swap(send_one, X_BIT))
    second = add_low(keep_two, swap(send_two, Y_BIT))
    first = add_low(first[:rows], swap(first[rows:], Y_BIT))
    second = add_low(second[:rows], swap(second[rows:], X_BIT))
    held = jnp.concatenate([first, second])
    summed = add_low(held, row_cross(held, True))
    pairs = [(i * 2 + h_of(i), i * 2 + 1 - h_of(i)) for i in range(16)]
    return jnp.where(mine, summed, lax.ppermute(summed, ("dp", "ctx"), pairs))


def join_column_slices(own, partner, p_index, core):
    low_pair = jnp.where(p_index == 0, own, partner)
    high_pair = jnp.where(p_index == 0, partner, own)
    pair = jnp.stack([low_pair, high_pair])
    other = swap_core(pair)
    lower = jnp.where(core == 0, pair, other)
    upper = jnp.where(core == 0, other, pair)
    return [lower[0], lower[1], upper[0], upper[1]]


def gather_tokens(own):
    same = jnp.stack([own, swap(own, P_BIT)])
    return same, swap_core(same)


def sum_tokens(same, sibling):
    pair = same.astype(WIDE) + swap_core(sibling).astype(WIDE)
    return pair[0] + swap(pair[1].astype(LOW), P_BIT).astype(WIDE)


VM = pl.BlockSpec(memory_space=pltpu.VMEM)
SM = pl.BlockSpec(memory_space=pltpu.SMEM)
HB = pl.BlockSpec(memory_space=pl.ANY)


def call(kernel, in_specs, outs, out_specs, scratch, flops, moved, after=()):
    held, late = len(in_specs), len(after)

    def body(*refs):
        kernel(*refs[:held], *refs[held + late :])

    made = pl.pallas_call(
        body,
        in_specs=in_specs + [HB] * late,
        out_specs=out_specs,
        out_shape=[jax.ShapeDtypeStruct(shape, dtype) for shape, dtype in outs],
        scratch_shapes=scratch,
        compiler_params=pltpu.CompilerParams(vmem_limit_bytes=VMEM_BYTES),
        cost_estimate=pl.CostEstimate(flops=flops, bytes_accessed=moved, transcendentals=0),
    )
    return lambda *operands: made(*operands, *after)


def column_copies(index, parts, whole, sems, outward):
    copies = []
    rows = whole.shape[0] // 16
    for part, (base, outer) in zip(parts, COLUMN_GROUPS):
        for place in range(4):
            relative = base + (place // 2) * outer + (place % 2) * H_BIT
            start = pl.multiple_of((index ^ relative) * rows, rows)
            block = part.at[pl.ds(place * rows, rows)]
            inside = whole.at[pl.ds(start, rows)]
            ends = (inside, block) if outward else (block, inside)
            copies.append(pltpu.make_async_copy(*ends, sems.at[len(copies)]))
    return copies


def row_copies(index, parts, whole, sems, outward):
    copies = []
    rows = whole.shape[0] // 8
    for part, (base, outer, half) in zip(parts, ROW_GROUPS):
        for place in range(2):
            relative = base + place * outer
            start = pl.multiple_of((((index ^ relative) % 4) * 2 + half) * rows, rows)
            block = part.at[pl.ds(place * rows, rows)]
            inside = whole.at[pl.ds(start, rows)]
            ends = (inside, block) if outward else (block, inside)
            copies.append(pltpu.make_async_copy(*ends, sems.at[len(copies)]))
    return copies


def start_all(copies):
    for copy in copies:
        copy.start()


def wait_all(copies):
    for copy in copies:
        copy.wait()


def load_tokens(same, sibling):
    return jnp.concatenate([same[0], sibling[0], same[1], sibling[1]])


def store_tokens(values, same, sibling):
    count = same.shape[1]
    for sequence in range(2):
        at = 2 * count * sequence
        same[sequence] = values[at : at + count].astype(same.dtype)
        sibling[sequence] = values[at + count : at + 2 * count].astype(sibling.dtype)


def place_of(scalars, sequence, at):
    block = jnp.where(
        at < 128,
        jnp.where(at < 64, scalars[1 + 4 * sequence], scalars[2 + 4 * sequence]),
        jnp.where(at < 192, scalars[3 + 4 * sequence], scalars[4 + 4 * sequence]),
    )
    return block * 64 + at % 64


def allowed_of(scalars, sequence):
    rows = place_of(scalars, sequence, lax.broadcasted_iota(jnp.int32, (256, 1), 0))
    cols = place_of(scalars, sequence, lax.broadcasted_iota(jnp.int32, (1, 256), 1))
    return rows >= cols


def fill_tables(scalars, cosine, sine, cos_rows, sin_rows):
    for slot in range(8):
        start = pl.multiple_of(scalars[1 + slot] * 64, 64)
        cos_rows[slot * 64 : slot * 64 + 64] = cosine[pl.ds(start, 64)]
        sin_rows[slot * 64 : slot * 64 + 64] = sine[pl.ds(start, 64)]


def attend_kernel(
    scalars, same, sibling, part_a, part_b, part_c, part_d, cosine, sine, gains,
    mixture, pre, rotated, values_out, log_total, whole, cos_rows, sin_rows, sems,
):
    copies = column_copies(scalars[0], (part_a, part_b, part_c, part_d), whole, sems, False)
    start_all(copies)
    fill_tables(scalars, cosine, sine, cos_rows, sin_rows)
    tokens = load_tokens(same, sibling)
    wait_all(copies)
    projected = matmul(tokens, whole[...])
    pre[...] = projected[:, :768]
    values_out[...] = projected[:, 768:].astype(LOW)
    for head in range(6):
        cut = slice(head * 128, head * 128 + 128)
        raw = pre[:, cut]
        gain = gains[0:1] if head < 4 else gains[1:2]
        scale = lax.rsqrt(jnp.mean(raw * raw, axis=-1, keepdims=True) + EPSILON)
        unit = raw * scale * gain
        turned = pltpu.roll(unit, 64, 1)
        rotated[:, cut] = (unit * cos_rows[...] + turned * sin_rows[...]).astype(LOW)
    for sequence in range(2):
        rows = slice(sequence * 256, sequence * 256 + 256)
        allowed = allowed_of(scalars, sequence)
        tops = []
        for head in range(4):
            group = head // 2
            queries = rotated[rows, head * 128 : head * 128 + 128]
            keys = rotated[rows, 512 + group * 128 : 640 + group * 128]
            scores = jnp.where(allowed, contract_cols(queries, keys) * (128**-0.5), -1e30)
            top = jnp.max(scores, axis=-1, keepdims=True)
            weights = jnp.exp(scores - top)
            total = jnp.sum(weights, axis=-1, keepdims=True)
            probs = (weights / total).astype(LOW)
            mixed = matmul(probs, values_out[rows, group * 128 : group * 128 + 128])
            mixture[rows, head * 128 : head * 128 + 128] = mixed.astype(LOW)
            tops.append(jnp.broadcast_to(top + jnp.log(total), (256, 128)))
        lane = lax.broadcasted_iota(jnp.int32, (256, 128), 1)
        log_total[rows] = jnp.where(
            lane < 2, jnp.where(lane < 1, tops[0], tops[1]), jnp.where(lane < 3, tops[2], tops[3])
        )


def attend(scalars, tokens, parts, tables, gains, after=()):
    return call(
        attend_kernel,
        [SM, VM, VM, HB, HB, HB, HB, VM, VM, VM],
        [((512, 512), LOW), ((512, 768), WIDE), ((512, 768), LOW), ((512, 256), LOW), ((512, 128), WIDE)],
        [VM] * 5,
        [
            pltpu.VMEM((1024, 1024), LOW),
            pltpu.VMEM((512, 128), WIDE),
            pltpu.VMEM((512, 128), WIDE),
            pltpu.SemaphoreType.DMA((16,)),
        ],
        2 * 10**9,
        8 * 10**6,
        after,
    )(scalars, *tokens, *parts, *tables, gains)


def output_kernel(scalars, mixture, part_a, part_b, part_c, part_d, same, sibling, whole, sems):
    copies = row_copies(scalars[0], (part_a, part_b, part_c, part_d), whole, sems, False)
    start_all(copies)
    wait_all(copies)
    store_tokens(matmul(mixture[...], whole[...]), same, sibling)


def row_product(scalars, left, parts, after=()):
    depth = left.shape[1]
    return call(
        output_kernel,
        [SM, VM, HB, HB, HB, HB],
        [((2, 128, 1024), LOW)] * 2,
        [VM] * 2,
        [pltpu.VMEM((depth, 1024), LOW), pltpu.SemaphoreType.DMA((8,))],
        2 * 512 * 1024 * depth,
        4 * 10**6,
        after,
    )(scalars, left, *parts)


def gate_kernel(
    scalars, same, sibling, part_a, part_b, part_c, part_d, gate_up, active, whole, sems
):
    copies = column_copies(scalars[0], (part_a, part_b, part_c, part_d), whole, sems, False)
    start_all(copies)
    tokens = load_tokens(same, sibling)
    wait_all(copies)
    for at in range(0, 768, 256):
        gate = matmul(tokens, whole[:, at : at + 256])
        upward = matmul(tokens, whole[:, 768 + at : 1024 + at])
        gate_up[:, at : at + 256] = gate
        gate_up[:, 768 + at : 1024 + at] = upward
        active[:, at : at + 256] = (gate * jax.nn.sigmoid(gate) * upward).astype(LOW)


def gate_product(scalars, tokens, parts, after=()):
    return call(
        gate_kernel,
        [SM, VM, VM, HB, HB, HB, HB],
        [((512, 1536), WIDE), ((512, 768), LOW)],
        [VM] * 2,
        [pltpu.VMEM((1024, 1536), LOW), pltpu.SemaphoreType.DMA((16,))],
        2 * 512 * 1024 * 1536,
        10 * 10**6,
        after,
    )(scalars, *tokens, *parts)


def swiglu_back_kernel(
    scalars, same, sibling, gate_up, row_a, row_b, row_c, row_d, col_a, col_b, col_c, col_d,
    grad_gate_up, grad_same, grad_sibling, down, both, row_sems, col_sems,
):
    down_copies = row_copies(scalars[0], (row_a, row_b, row_c, row_d), down, row_sems, False)
    both_copies = column_copies(scalars[0], (col_a, col_b, col_c, col_d), both, col_sems, False)
    start_all(down_copies)
    start_all(both_copies)
    grad_out = load_tokens(same, sibling)
    wait_all(down_copies)
    for at in range(0, 768, 256):
        grad_active = contract_cols(grad_out, down[at : at + 256])
        gate = gate_up[:, at : at + 256]
        upward = gate_up[:, 768 + at : 1024 + at]
        sigmoid = jax.nn.sigmoid(gate)
        grad_gate_up[:, at : at + 256] = (
            grad_active * upward * (sigmoid * (1.0 + gate * (1.0 - sigmoid)))
        ).astype(LOW)
        grad_gate_up[:, 768 + at : 1024 + at] = (grad_active * (gate * sigmoid)).astype(LOW)
    wait_all(both_copies)
    store_tokens(contract_cols(grad_gate_up[...], both[...]), grad_same, grad_sibling)


def swiglu_back(scalars, grad_out, gate_up, down_parts, gate_up_parts, after=()):
    return call(
        swiglu_back_kernel,
        [SM, VM, VM, VM] + [HB] * 8,
        [((512, 1536), LOW), ((2, 128, 1024), LOW), ((2, 128, 1024), LOW)],
        [VM] * 3,
        [
            pltpu.VMEM((768, 1024), LOW),
            pltpu.VMEM((1024, 1536), LOW),
            pltpu.SemaphoreType.DMA((8,)),
            pltpu.SemaphoreType.DMA((16,)),
        ],
        2 * 512 * 1024 * 2304,
        12 * 10**6,
        after,
    )(scalars, *grad_out, gate_up, *down_parts, *gate_up_parts)


def attend_back_kernel(
    scalars, same, sibling, part_a, part_b, part_c, part_d, pre, rotated, values, log_total,
    cosine, sine, gains, grad_all, grad_gains, whole, cos_rows, sin_rows, grad_rot, sems,
):
    copies = row_copies(scalars[0], (part_a, part_b, part_c, part_d), whole, sems, False)
    start_all(copies)
    fill_tables(scalars, cosine, sine, cos_rows, sin_rows)
    branch = load_tokens(same, sibling)
    wait_all(copies)
    grad_mixed = contract_cols(branch, whole[...]).astype(LOW)
    scaling = 128**-0.5
    for sequence in range(2):
        rows = slice(sequence * 256, sequence * 256 + 256)
        allowed = allowed_of(scalars, sequence)
        for group in range(2):
            keys = rotated[rows, 512 + group * 128 : 640 + group * 128]
            value_rows = values[rows, group * 128 : group * 128 + 128]
            grad_keys = jnp.zeros((256, 128), WIDE)
            grad_values = jnp.zeros((256, 128), WIDE)
            for head in (2 * group, 2 * group + 1):
                cut = slice(head * 128, head * 128 + 128)
                queries = rotated[rows, cut]
                grad_mix = grad_mixed[rows, cut]
                scores = jnp.where(allowed, contract_cols(queries, keys) * scaling, -1e30)
                probs = jnp.exp(scores - log_total[rows, head : head + 1])
                grad_values += contract_rows(probs.astype(LOW), grad_mix)
                grad_probs = contract_cols(grad_mix, value_rows)
                inner = jnp.sum(probs * grad_probs, axis=-1, keepdims=True)
                grad_scores = (probs * (grad_probs - inner)).astype(LOW)
                grad_rot[rows, cut] = matmul(grad_scores, keys) * scaling
                grad_keys += contract_rows(grad_scores, queries)
            grad_rot[rows, 512 + group * 128 : 640 + group * 128] = grad_keys * scaling
            grad_all[rows, 768 + group * 128 : 896 + group * 128] = grad_values.astype(LOW)
    gain_sums = [jnp.zeros((1, 128), WIDE), jnp.zeros((1, 128), WIDE)]
    for head in range(6):
        cut = slice(head * 128, head * 128 + 128)
        which = 0 if head < 4 else 1
        raw = pre[:, cut]
        scale = lax.rsqrt(jnp.mean(raw * raw, axis=-1, keepdims=True) + EPSILON)
        unit = raw * scale
        coming = grad_rot[:, cut]
        back = coming * cos_rows[...] - pltpu.roll(coming, 64, 1) * sin_rows[...]
        gain_sums[which] += jnp.sum(back * unit, axis=0, keepdims=True)
        back = back * gains[which : which + 1]
        along = jnp.mean(back * unit, axis=-1, keepdims=True)
        grad_all[:, cut] = (scale * (back - unit * along)).astype(LOW)
    grad_gains[...] = jnp.zeros((8, 128), WIDE)
    grad_gains[0:1] = gain_sums[0]
    grad_gains[1:2] = gain_sums[1]


def attend_back_call(scalars, branch, parts, pre, rotated, values, log_total, tables, gains, after=()):
    return call(
        attend_back_kernel,
        [SM, VM, VM, HB, HB, HB, HB] + [VM] * 7,
        [((512, 1024), LOW), ((8, 128), WIDE)],
        [VM] * 2,
        [
            pltpu.VMEM((512, 1024), LOW),
            pltpu.VMEM((512, 128), WIDE),
            pltpu.VMEM((512, 128), WIDE),
            pltpu.VMEM((512, 768), WIDE),
            pltpu.SemaphoreType.DMA((8,)),
        ],
        2 * 10**9,
        8 * 10**6,
        after,
    )(scalars, *branch, *parts, pre, rotated, values, log_total, *tables, gains)


def column_back_kernel(scalars, grads, part_a, part_b, part_c, part_d, same, sibling, whole, sems):
    copies = column_copies(scalars[0], (part_a, part_b, part_c, part_d), whole, sems, False)
    start_all(copies)
    wait_all(copies)
    store_tokens(contract_cols(grads[...], whole[...]), same, sibling)


def column_back(scalars, grads, parts, after=()):
    width = grads.shape[1]
    return call(
        column_back_kernel,
        [SM, VM, HB, HB, HB, HB],
        [((2, 128, 1024), LOW)] * 2,
        [VM] * 2,
        [pltpu.VMEM((1024, width), LOW), pltpu.SemaphoreType.DMA((16,))],
        2 * 512 * 1024 * width,
        5 * 10**6,
        after,
    )(scalars, grads, *parts)


def column_grad_kernel(
    scalars, same, sibling, grads, keep_one, send_one, keep_two, send_two, whole, sems
):
    for at in range(0, 1024, 256):
        cut = slice(at, at + 256)
        left = jnp.concatenate(
            [same[0, :, cut], sibling[0, :, cut], same[1, :, cut], sibling[1, :, cut]]
        )
        whole[cut] = contract_rows(left, grads[...]).astype(LOW)
    copies = column_copies(
        scalars[0], (keep_one, send_one, keep_two, send_two), whole, sems, True
    )
    start_all(copies)
    wait_all(copies)


def column_grad(scalars, tokens, grads, after=()):
    width = grads.shape[1]
    return call(
        column_grad_kernel,
        [SM, VM, VM, VM],
        [((256, width), LOW)] * 4,
        [HB] * 4,
        [pltpu.VMEM((1024, width), LOW), pltpu.SemaphoreType.DMA((16,))],
        2 * 512 * 1024 * width,
        6 * 10**6,
        after,
    )(scalars, *tokens, grads)


def row_grad_kernel(
    scalars, left, same, sibling, keep_one, send_one, keep_two, send_two, whole, sems
):
    right = load_tokens(same, sibling)
    for at in range(0, whole.shape[0], 256):
        cut = slice(at, at + 256)
        whole[cut] = contract_rows(left[:, cut], right).astype(LOW)
    copies = row_copies(scalars[0], (keep_one, send_one, keep_two, send_two), whole, sems, True)
    start_all(copies)
    wait_all(copies)


def row_grad(scalars, left, tokens, after=()):
    depth = left.shape[1]
    return call(
        row_grad_kernel,
        [SM, VM, VM, VM],
        [((depth // 4, 1024), LOW)] * 4,
        [HB] * 4,
        [pltpu.VMEM((depth, 1024), LOW), pltpu.SemaphoreType.DMA((8,))],
        2 * 512 * 1024 * depth,
        4 * 10**6,
        after,
    )(scalars, left, *tokens)


def fast_body(
    hidden_in,
    cotangent,
    block_order,
    w_query,
    key_weight,
    value_weight,
    w_output,
    w_gate,
    w_up,
    w_down,
    norm_gains,
    momentum_query,
    key_momentum,
    value_momentum,
    momentum_output,
    momentum_gate,
    momentum_up,
    momentum_down,
    momentum_gains,
):
    index = lax.axis_index("dp")
    core = lax.axis_index("ctx")
    p_index = (index // P_BIT) % 2
    mine = h_of(index) == core
    slice_own = 2 * core + p_index
    slice_give = 2 * core + 1 - p_index

    def column_slice(weight, which):
        size = weight.shape[1] // 4
        return lax.dynamic_slice_in_dim(weight, which * size, size, axis=1).astype(LOW)

    def column_pack(weights, which):
        return jnp.concatenate([column_slice(weight, which) for weight in weights], axis=1)

    gains_low = norm_gains.astype(LOW)[None]
    for bit in (P_BIT, H_BIT, Y_BIT, X_BIT):
        gains_low = jnp.concatenate([gains_low, swap(gains_low, bit)])
    order = [0]
    for bit in (P_BIT, H_BIT, Y_BIT, X_BIT):
        order = order + [o ^ bit for o in order]
    inverse = [0] * 16
    for at, relative in enumerate(order):
        inverse[relative] = at
    lookup = jnp.array(inverse, jnp.int32)[index ^ jnp.arange(16)]
    gains_all = jnp.take(gains_low, lookup, axis=0).reshape(-1).astype(WIDE)

    width = hidden_in.shape[2]
    head_size = 128
    gain_attn = gains_all[:width]
    gain_mlp = gains_all[width : 2 * width]
    head_gains = gains_all[2 * width :].reshape(2, head_size)

    qkv = (w_query, key_weight, value_weight)
    qkv_parts = gather_column_slices(column_pack(qkv, slice_own), column_pack(qkv, slice_give))
    output_parts = gather_row_slices(w_output.astype(LOW), mine)
    gate_up = (w_gate, w_up)
    gate_up_parts = gather_column_slices(
        column_pack(gate_up, slice_own), column_pack(gate_up, slice_give)
    )
    down_parts, _, down_first = gather_row_slices(w_down.astype(LOW), mine, True)

    tokens_own = hidden_in[0]
    count = tokens_own.shape[0]
    orders = jnp.concatenate([block_order, swap(block_order, P_BIT)])
    orders = jnp.where(core == 0, orders, jnp.roll(orders, 2, axis=1))
    scalars = jnp.concatenate([index[None], orders.reshape(-1)]).astype(jnp.int32)
    cosine, sine_table = rotary_tables(jnp.arange(2 * count, dtype=jnp.int32), head_size)
    sign = jnp.where(jnp.arange(head_size) < head_size // 2, -1.0, 1.0)
    tables = (cosine, sine_table * sign)

    tokens_f = tokens_own.astype(WIDE)
    normed_f, norm_pull = jax.vjp(rms_norm, tokens_f, gain_attn)
    normed = gather_tokens(normed_f.astype(LOW))
    grad_out = gather_tokens(cotangent[0])

    mixed_low, pre, rotated, value_low, log_total = attend(
        scalars, normed, qkv_parts, tables, head_gains
    )
    attended = sum_tokens(*row_product(scalars, mixed_low, output_parts, down_first))
    middle = tokens_f + attended
    normed_two_f, norm_two_pull = jax.vjp(rms_norm, middle, gain_mlp)
    normed_two = gather_tokens(normed_two_f.astype(LOW))
    gate_up_act, active = gate_product(scalars, normed_two, gate_up_parts, down_parts)
    grad_gate_up, back_same, back_sibling = swiglu_back(
        scalars, grad_out, gate_up_act, down_parts, gate_up_parts
    )
    grad_down = row_grad(scalars, active, grad_out, [back_same])
    grad_normed_two = sum_tokens(back_same, back_sibling)
    grad_gate_up_mat = column_grad(scalars, normed_two, grad_gate_up, [back_same])

    grad_middle_norm, grad_gain_mlp = norm_two_pull(grad_normed_two)
    grad_middle = cotangent[0].astype(WIDE) + grad_middle_norm
    grad_branch = gather_tokens(grad_middle.astype(LOW))
    grad_qkv, grad_head_gains = attend_back_call(
        scalars, grad_branch, output_parts, pre, rotated, value_low, log_total, tables, head_gains
    )
    grad_qkv_mat = column_grad(scalars, normed, grad_qkv, ())
    grad_output_mat = row_grad(scalars, mixed_low, grad_branch, [grad_qkv_mat[0]])
    grad_normed = sum_tokens(*column_back(scalars, grad_qkv, qkv_parts, [grad_qkv_mat[0]]))
    grad_tokens_norm, grad_gain_attn = norm_pull(grad_normed)
    input_grad = (grad_middle + grad_tokens_norm).astype(LOW)[None]

    layer_sum = sum_tokens(*row_product(scalars, active, down_parts, [grad_qkv_mat[0]]))
    layer_out = (middle + layer_sum).astype(LOW)[None]
    grad_gains = jnp.concatenate([grad_gain_attn, grad_gain_mlp, grad_head_gains[:2].reshape(-1)])
    grad_gains = grad_gains.reshape(16, -1)
    grad_gains = grad_gains + swap_core(grad_gains.astype(LOW)).astype(WIDE)
    for bit in (P_BIT, H_BIT, Y_BIT, X_BIT):
        grad_gains = grad_gains + swap(grad_gains.astype(LOW), bit).astype(WIDE)
    grad_gains = lax.dynamic_index_in_dim(grad_gains, index, keepdims=False)

    down_sum = scatter_row_slices(*grad_down, mine)
    gate_up_sum = join_column_slices(*scatter_column_slices(*grad_gate_up_mat), p_index, core)
    output_sum = scatter_row_slices(*grad_output_mat, mine)
    qkv_sum = join_column_slices(*scatter_column_slices(*grad_qkv_mat), p_index, core)

    def columns(parts, start, size):
        return jnp.concatenate([part[:, start : start + size] for part in parts], axis=1)

    query_width = w_query.shape[1] // 4
    kv_width = key_weight.shape[1] // 4
    hidden_units = w_gate.shape[1] // 4
    sums = (
        columns(qkv_sum, 0, query_width),
        columns(qkv_sum, query_width, kv_width),
        columns(qkv_sum, query_width + kv_width, kv_width),
        output_sum,
        columns(gate_up_sum, 0, hidden_units),
        columns(gate_up_sum, hidden_units, hidden_units),
        down_sum,
        grad_gains,
    )
    masters = (w_query, key_weight, value_weight, w_output, w_gate, w_up, w_down, norm_gains)
    moments = (
        momentum_query,
        key_momentum,
        value_momentum,
        momentum_output,
        momentum_gate,
        momentum_up,
        momentum_down,
        momentum_gains,
    )
    norm_scale = lax.rsqrt(jnp.float32(16 * 2 * count))
    summed = tuple(part.astype(WIDE) for part in sums)
    updates, new_moments = lion_step(masters, moments, summed, norm_scale)
    return (layer_out, input_grad) + tuple(updates) + tuple(new_moments)


def solution(mesh):
    body = fast_body if dict(mesh.shape) == {"dp": 16, "ctx": 2} else general_body
    return jax.shard_map(
        body,
        mesh=mesh,
        in_specs=(
            P("dp", "ctx", None),
            P("dp", "ctx", None),
            P("dp", None),
            P("dp", None),
            P("dp", None),
            P("dp", None),
            P("dp", None),
            P("dp", None),
            P("dp", None),
            P("dp", None),
            P("dp"),
            P("dp", None),
            P("dp", None),
            P("dp", None),
            P("dp", None),
            P("dp", None),
            P("dp", None),
            P("dp", None),
            P("dp"),
        ),
        out_specs=(
            P("dp", "ctx", None),
            P("dp", "ctx", None),
            P("dp", None),
            P("dp", None),
            P("dp", None),
            P("dp", None),
            P("dp", None),
            P("dp", None),
            P("dp", None),
            P("dp"),
            P("dp", None),
            P("dp", None),
            P("dp", None),
            P("dp", None),
            P("dp", None),
            P("dp", None),
            P("dp", None),
            P("dp"),
        ),
        check_vma=False,
    )
```

```python
import jax
import jax.numpy as jnp
from jax import lax
from jax.experimental import pallas as pl
from jax.experimental.pallas import tpu as pltpu
from jax.sharding import PartitionSpec as P

EPSILON = 1e-06
THETA = 1000000.0
BETA_ONE = 0.9
BETA_TWO = 0.5
SOFTEN = 0.005
DECAY_FACTOR = 1.0


def rms_norm(values, gain_vec):
    return (
        values * lax.rsqrt(jnp.mean(values * values, axis=-1, keepdims=True) + EPSILON) * gain_vec
    )


def rotary_tables(positions, head_size):
    half_size = head_size // 2
    frequency = THETA ** (-(jnp.arange(half_size, dtype=jnp.float32) * 2.0 / head_size))
    angles = positions.astype(jnp.float32)[:, None] * frequency[None, :]
    angles = jnp.concatenate([angles, angles], axis=1)
    return (jnp.cos(angles), jnp.sin(angles))


def rotate(values, cosine, sine_table):
    half_size = values.shape[-1] // 2
    turned = jnp.concatenate([-values[..., half_size:], values[..., :half_size]], axis=-1)
    return values * cosine[:, None, :] + turned * sine_table[:, None, :]


def head_prep(projected, gain_vec, cosine, sine_table):
    shaped = projected.reshape(projected.shape[0], -1, gain_vec.shape[0])
    return rotate(rms_norm(shaped, gain_vec), cosine, sine_table)


def matmul(left, right):
    return jnp.dot(left, right, preferred_element_type=jnp.float32)


def contract_rows(left, right):
    return lax.dot_general(
        left, right, (((0,), (0,)), ((), ())), preferred_element_type=jnp.float32
    )


def contract_cols(left, right):
    return lax.dot_general(
        left, right, (((1,), (1,)), ((), ())), preferred_element_type=jnp.float32
    )


def head_scores(queries, key_row_block, query_pos, key_pos):
    scaling = queries.shape[-1] ** (-0.5)
    scores = (
        jnp.einsum("trd,kd->rtk", queries, key_row_block, preferred_element_type=jnp.float32)
        * scaling
    )
    allowed = query_pos[:, None] >= key_pos[None, :]
    return jnp.where(allowed[None], scores, -1e30)


def attend_head(query_pos, key_pos):

    def attend(group_item):
        queries, key_row_block, value_row_block = group_item
        scores = head_scores(queries, key_row_block, query_pos, key_pos)
        row_top = jnp.max(scores, axis=-1, keepdims=True)
        weights = jnp.exp(scores - row_top)
        row_total = jnp.sum(weights, axis=-1, keepdims=True)
        probs_low = (weights / row_total).astype(jnp.bfloat16)
        mixture = jnp.einsum(
            "rtk,kd->trd", probs_low, value_row_block, preferred_element_type=jnp.float32
        )
        return (mixture, (row_top + jnp.log(row_total))[..., 0])

    return attend


def attend_back(query_pos, key_pos):

    def backward(group_item):
        queries, key_row_block, value_row_block, grad_mix, log_total = group_item
        scaling = queries.shape[-1] ** (-0.5)
        scores = head_scores(queries, key_row_block, query_pos, key_pos)
        probs = jnp.exp(scores - log_total[..., None])
        grad_values = jnp.einsum(
            "rtk,trd->kd", probs.astype(jnp.bfloat16), grad_mix, preferred_element_type=jnp.float32
        )
        grad_probs = jnp.einsum(
            "trd,kd->rtk", grad_mix, value_row_block, preferred_element_type=jnp.float32
        )
        inner = jnp.sum(probs * grad_probs, axis=-1, keepdims=True)
        grad_scores = (probs * (grad_probs - inner)).astype(jnp.bfloat16)
        grad_queries = (
            jnp.einsum(
                "rtk,kd->trd", grad_scores, key_row_block, preferred_element_type=jnp.float32
            )
            * scaling
        )
        grad_keys = (
            jnp.einsum("rtk,trd->kd", grad_scores, queries, preferred_element_type=jnp.float32)
            * scaling
        )
        return (grad_queries, grad_keys, grad_values)

    return backward


def lion_step(masters, moments, gradients, norm_scale):
    updates = []
    new_moments = []
    for tensor_index in range(8):
        scaled = gradients[tensor_index] * norm_scale
        moment_arr = moments[tensor_index]
        blend_arr = BETA_ONE * moment_arr + (1.0 - BETA_ONE) * scaled
        direction = blend_arr / jnp.sqrt(blend_arr * blend_arr + SOFTEN)
        decay_here = DECAY_FACTOR if tensor_index < 7 else 0.0
        updates.append(direction + decay_here * masters[tensor_index])
        new_moments.append(BETA_TWO * moment_arr + (1.0 - BETA_TWO) * scaled)
    return (updates, new_moments)


def general_body(
    hidden_in,
    cotangent,
    block_order,
    w_query,
    key_weight,
    value_weight,
    w_output,
    w_gate,
    w_up,
    w_down,
    norm_gains,
    momentum_query,
    key_momentum,
    value_momentum,
    momentum_output,
    momentum_gate,
    momentum_up,
    momentum_down,
    momentum_gains,
):
    copies = (
        lax.all_gather(w_query.astype(jnp.bfloat16), "dp", axis=0, tiled=True),
        lax.all_gather(key_weight.astype(jnp.bfloat16), "dp", axis=0, tiled=True),
        lax.all_gather(value_weight.astype(jnp.bfloat16), "dp", axis=0, tiled=True),
        lax.all_gather(w_output.astype(jnp.bfloat16), "dp", axis=0, tiled=True),
        lax.all_gather(w_gate.astype(jnp.bfloat16), "dp", axis=0, tiled=True),
        lax.all_gather(w_up.astype(jnp.bfloat16), "dp", axis=0, tiled=True),
        lax.all_gather(w_down.astype(jnp.bfloat16), "dp", axis=0, tiled=True),
        lax.all_gather(norm_gains.astype(jnp.bfloat16), "dp", axis=0, tiled=True),
    )
    query_mat, key_mat, value_mat, output_mat, gate_mat, up_mat, down_mat, gains_low = copies
    gains_all = gains_low.astype(jnp.float32)
    width = hidden_in.shape[2]
    head_size = (gains_all.shape[0] - 2 * width) // 2
    kv_heads = key_mat.shape[1] // head_size
    query_heads = query_mat.shape[1] // head_size
    group_repeat_count = query_heads // kv_heads
    gain_attn = gains_all[:width]
    gain_mlp = gains_all[width : 2 * width]
    gain_query = gains_all[2 * width : 2 * width + head_size]
    gain_key = gains_all[2 * width + head_size :]
    tokens_in = hidden_in[0]
    token_count = tokens_in.shape[0]
    block_size = token_count // 2
    slot_order = block_order[0]
    key_pos = (
        slot_order[:, None] * block_size + jnp.arange(block_size, dtype=jnp.int32)[None, :]
    ).reshape(-1)
    query_pos = lax.dynamic_slice_in_dim(key_pos, lax.axis_index("ctx") * token_count, token_count)
    cosine, sine_table = rotary_tables(query_pos, head_size)
    tokens_f = tokens_in.astype(jnp.float32)
    normed_f, norm_pull = jax.vjp(rms_norm, tokens_f, gain_attn)
    normalized_input = normed_f.astype(jnp.bfloat16)
    query_pre = matmul(normalized_input, query_mat)
    key_pre = matmul(normalized_input, key_mat)
    value_low = matmul(normalized_input, value_mat).astype(jnp.bfloat16)
    query_rot, query_pull = jax.vjp(
        lambda projected, gain_vec: head_prep(projected, gain_vec, cosine, sine_table),
        query_pre,
        gain_query,
    )
    key_rot, key_pull = jax.vjp(
        lambda projected, gain_vec: head_prep(projected, gain_vec, cosine, sine_table),
        key_pre,
        gain_key,
    )
    query_low = query_rot.astype(jnp.bfloat16)
    key_heads = key_rot.astype(jnp.bfloat16).transpose(1, 0, 2)
    value_heads = value_low.reshape(token_count, kv_heads, head_size).transpose(1, 0, 2)
    gathered = (
        lax.all_gather(key_heads, "ctx", axis=1, tiled=True),
        lax.all_gather(value_heads, "ctx", axis=1, tiled=True),
    )
    query_groups = query_low.reshape(
        token_count, kv_heads, group_repeat_count, head_size
    ).transpose(1, 0, 2, 3)
    mixture, log_total = lax.map(
        attend_head(query_pos, key_pos), (query_groups, gathered[0], gathered[1])
    )
    mixed_low = mixture.transpose(1, 0, 2, 3).reshape(token_count, -1).astype(jnp.bfloat16)
    middle = tokens_f + matmul(mixed_low, output_mat)
    normed_two_f, norm_two_pull = jax.vjp(rms_norm, middle, gain_mlp)
    normed_two = normed_two_f.astype(jnp.bfloat16)
    gate_act = matmul(normed_two, gate_mat)
    upward = matmul(normed_two, up_mat)
    active_f, swiglu_pull = jax.vjp(
        lambda gate_in, up_in: jax.nn.silu(gate_in) * up_in, gate_act, upward
    )
    active = active_f.astype(jnp.bfloat16)
    layer_out = (middle + matmul(active, down_mat)).astype(jnp.bfloat16)[None]
    grad_out = cotangent[0]
    grad_down = contract_rows(active, grad_out)
    grad_active = contract_cols(grad_out, down_mat)
    grad_gate_f, grad_up_f = swiglu_pull(grad_active)
    grad_gate = grad_gate_f.astype(jnp.bfloat16)
    grad_upward = grad_up_f.astype(jnp.bfloat16)
    grad_gate_mat = contract_rows(normed_two, grad_gate)
    grad_up_mat = contract_rows(normed_two, grad_upward)
    grad_normed_two = contract_cols(grad_gate, gate_mat) + contract_cols(grad_upward, up_mat)
    grad_middle_norm, grad_gain_mlp = norm_two_pull(grad_normed_two)
    grad_middle = grad_out.astype(jnp.float32) + grad_middle_norm
    grad_branch = grad_middle.astype(jnp.bfloat16)
    grad_output_mat = contract_rows(mixed_low, grad_branch)
    grad_mixed = contract_cols(grad_branch, output_mat).astype(jnp.bfloat16)
    grad_groups = grad_mixed.reshape(
        token_count, kv_heads, group_repeat_count, head_size
    ).transpose(1, 0, 2, 3)
    grad_query_groups, grad_key_all, grad_value_all = lax.map(
        attend_back(query_pos, key_pos),
        (query_groups, gathered[0], gathered[1], grad_groups, log_total),
    )
    grad_key_own, grad_value_own = (
        lax.psum_scatter(
            grad_key_all.astype(jnp.bfloat16), "ctx", scatter_dimension=1, tiled=True
        ).astype(jnp.float32),
        lax.psum_scatter(
            grad_value_all.astype(jnp.bfloat16), "ctx", scatter_dimension=1, tiled=True
        ).astype(jnp.float32),
    )
    grad_query_rot = grad_query_groups.transpose(1, 0, 2, 3).reshape(
        token_count, query_heads, head_size
    )
    grad_query_pre, grad_gain_query = query_pull(grad_query_rot)
    grad_key_pre, grad_gain_key = key_pull(grad_key_own.transpose(1, 0, 2))
    grad_query_low = grad_query_pre.astype(jnp.bfloat16)
    grad_key_low = grad_key_pre.astype(jnp.bfloat16)
    grad_value_low = grad_value_own.transpose(1, 0, 2).reshape(token_count, -1).astype(jnp.bfloat16)
    grad_query_mat = contract_rows(normalized_input, grad_query_low)
    grad_key_mat = contract_rows(normalized_input, grad_key_low)
    grad_value_mat = contract_rows(normalized_input, grad_value_low)
    grad_normed = (
        contract_cols(grad_query_low, query_mat)
        + contract_cols(grad_key_low, key_mat)
        + contract_cols(grad_value_low, value_mat)
    )
    grad_tokens_norm, grad_gain_attn = norm_pull(grad_normed)
    input_grad = (grad_middle + grad_tokens_norm).astype(jnp.bfloat16)[None]
    grad_gains = jnp.concatenate([grad_gain_attn, grad_gain_mlp, grad_gain_query, grad_gain_key])
    masters = (w_query, key_weight, value_weight, w_output, w_gate, w_up, w_down, norm_gains)
    moments = (
        momentum_query,
        key_momentum,
        value_momentum,
        momentum_output,
        momentum_gate,
        momentum_up,
        momentum_down,
        momentum_gains,
    )
    token_total = lax.axis_size("dp") * key_pos.shape[0]
    norm_scale = lax.rsqrt(jnp.float32(token_total))
    shares = (
        lax.psum_scatter(
            grad_query_mat.astype(jnp.bfloat16), "dp", scatter_dimension=0, tiled=True
        ).astype(jnp.float32),
        lax.psum_scatter(
            grad_key_mat.astype(jnp.bfloat16), "dp", scatter_dimension=0, tiled=True
        ).astype(jnp.float32),
        lax.psum_scatter(
            grad_value_mat.astype(jnp.bfloat16), "dp", scatter_dimension=0, tiled=True
        ).astype(jnp.float32),
        lax.psum_scatter(
            grad_output_mat.astype(jnp.bfloat16), "dp", scatter_dimension=0, tiled=True
        ).astype(jnp.float32),
        lax.psum_scatter(
            grad_gate_mat.astype(jnp.bfloat16), "dp", scatter_dimension=0, tiled=True
        ).astype(jnp.float32),
        lax.psum_scatter(
            grad_up_mat.astype(jnp.bfloat16), "dp", scatter_dimension=0, tiled=True
        ).astype(jnp.float32),
        lax.psum_scatter(
            grad_down.astype(jnp.bfloat16), "dp", scatter_dimension=0, tiled=True
        ).astype(jnp.float32),
        lax.psum_scatter(
            grad_gains.astype(jnp.bfloat16), "dp", scatter_dimension=0, tiled=True
        ).astype(jnp.float32),
    )
    summed = (
        lax.psum(shares[0].astype(jnp.bfloat16), "ctx").astype(jnp.float32),
        lax.psum(shares[1].astype(jnp.bfloat16), "ctx").astype(jnp.float32),
        lax.psum(shares[2].astype(jnp.bfloat16), "ctx").astype(jnp.float32),
        lax.psum(shares[3].astype(jnp.bfloat16), "ctx").astype(jnp.float32),
        lax.psum(shares[4].astype(jnp.bfloat16), "ctx").astype(jnp.float32),
        lax.psum(shares[5].astype(jnp.bfloat16), "ctx").astype(jnp.float32),
        lax.psum(shares[6].astype(jnp.bfloat16), "ctx").astype(jnp.float32),
        lax.psum(shares[7].astype(jnp.bfloat16), "ctx").astype(jnp.float32),
    )
    updates, new_moments = lion_step(masters, moments, summed, norm_scale)
    return (layer_out, input_grad) + tuple(updates) + tuple(new_moments)


X_BIT, Y_BIT, P_BIT, H_BIT = 1, 2, 4, 8
LOW = jnp.bfloat16
WIDE = jnp.float32
VMEM_BYTES = 24 * 1024 * 1024
COLUMN_GROUPS = ((0, Y_BIT), (X_BIT, Y_BIT), (P_BIT, X_BIT), (P_BIT + Y_BIT, X_BIT))
ROW_GROUPS = ((0, Y_BIT, 0), (X_BIT, Y_BIT, 0), (0, X_BIT, 1), (Y_BIT, X_BIT, 1))


def swap(values, bit):
    return lax.ppermute(values, "dp", [(i, i ^ bit) for i in range(16)])


def swap_core(values):
    return lax.ppermute(values, "ctx", [(0, 1), (1, 0)])


def h_of(index):
    return (index // H_BIT) % 2


def row_cross(values, to_owner):
    pairs = []
    for index in range(16):
        for core in range(2):
            if (core == h_of(index)) != to_owner:
                pairs.append((index * 2 + core, (index ^ H_BIT) * 2 + core))
    return lax.ppermute(values, ("dp", "ctx"), pairs)


def gather_column_slices(own, give):
    rows = own.shape[0]
    got = swap(give, P_BIT)
    far = swap(jnp.concatenate([own, got]), H_BIT)
    first = jnp.concatenate([own, far[:rows]])
    second = jnp.concatenate([got, far[rows:]])
    first = jnp.concatenate([first, swap(first, Y_BIT)])
    second = jnp.concatenate([second, swap(second, X_BIT)])
    return first, swap(first, X_BIT), second, swap(second, Y_BIT)


def gather_row_slices(own, mine, stages=False):
    rows = own.shape[0] // 2
    far = row_cross(own, False)
    held = jnp.where(mine, own, far)
    first, second = held[:rows], held[rows:]
    came_y, came_x = swap(first, Y_BIT), swap(second, X_BIT)
    first = jnp.concatenate([first, came_y])
    second = jnp.concatenate([second, came_x])
    parts = first, swap(first, X_BIT), second, swap(second, Y_BIT)
    return (parts, [far], [came_y, came_x]) if stages else parts


def add_low(left, right):
    return (left.astype(WIDE) + right.astype(WIDE)).astype(LOW)


def scatter_column_slices(keep_one, send_one, keep_two, send_two):
    rows = keep_one.shape[0] // 4
    first = add_low(keep_one, swap(send_one, X_BIT))
    second = add_low(keep_two, swap(send_two, Y_BIT))
    first = add_low(first[: 2 * rows], swap(first[2 * rows :], Y_BIT))
    second = add_low(second[: 2 * rows], swap(second[2 * rows :], X_BIT))
    near = jnp.concatenate([first[:rows], second[:rows]])
    far = jnp.concatenate([first[rows:], second[rows:]])
    near = add_low(near, swap(far, H_BIT))
    return near[:rows], swap(near[rows:], P_BIT)


def scatter_row_slices(keep_one, send_one, keep_two, send_two, mine):
    rows = keep_one.shape[0] // 2
    first = add_low(keep_one, swap(send_one, X_BIT))
    second = add_low(keep_two, swap(send_two, Y_BIT))
    first = add_low(first[:rows], swap(first[rows:], Y_BIT))
    second = add_low(second[:rows], swap(second[rows:], X_BIT))
    held = jnp.concatenate([first, second])
    summed = add_low(held, row_cross(held, True))
    pairs = [(i * 2 + h_of(i), i * 2 + 1 - h_of(i)) for i in range(16)]
    return jnp.where(mine, summed, lax.ppermute(summed, ("dp", "ctx"), pairs))


def join_column_slices(own, partner, p_index, core):
    low_pair = jnp.where(p_index == 0, own, partner)
    high_pair = jnp.where(p_index == 0, partner, own)
    pair = jnp.stack([low_pair, high_pair])
    other = swap_core(pair)
    lower = jnp.where(core == 0, pair, other)
    upper = jnp.where(core == 0, other, pair)
    return [lower[0], lower[1], upper[0], upper[1]]


def gather_tokens(own):
    same = jnp.stack([own, swap(own, P_BIT)])
    return same, swap_core(same)


def sum_tokens(same, sibling):
    pair = same.astype(WIDE) + swap_core(sibling).astype(WIDE)
    return pair[0] + swap(pair[1].astype(LOW), P_BIT).astype(WIDE)


VM = pl.BlockSpec(memory_space=pltpu.VMEM)
SM = pl.BlockSpec(memory_space=pltpu.SMEM)
HB = pl.BlockSpec(memory_space=pl.ANY)


def call(kernel, in_specs, outs, out_specs, scratch, flops, moved, after=()):
    held, late = len(in_specs), len(after)

    def body(*refs):
        kernel(*refs[:held], *refs[held + late :])

    made = pl.pallas_call(
        body,
        in_specs=in_specs + [HB] * late,
        out_specs=out_specs,
        out_shape=[jax.ShapeDtypeStruct(shape, dtype) for shape, dtype in outs],
        scratch_shapes=scratch,
        compiler_params=pltpu.CompilerParams(vmem_limit_bytes=VMEM_BYTES),
        cost_estimate=pl.CostEstimate(flops=flops, bytes_accessed=moved, transcendentals=0),
    )
    return lambda *operands: made(*operands, *after)


def column_copies(index, parts, whole, sems, outward):
    copies = []
    rows = whole.shape[0] // 16
    for part, (base, outer) in zip(parts, COLUMN_GROUPS):
        for place in range(4):
            relative = base + (place // 2) * outer + (place % 2) * H_BIT
            start = pl.multiple_of((index ^ relative) * rows, rows)
            block = part.at[pl.ds(place * rows, rows)]
            inside = whole.at[pl.ds(start, rows)]
            ends = (inside, block) if outward else (block, inside)
            copies.append(pltpu.make_async_copy(*ends, sems.at[len(copies)]))
    return copies


def row_copies(index, parts, whole, sems, outward):
    copies = []
    rows = whole.shape[0] // 8
    for part, (base, outer, half) in zip(parts, ROW_GROUPS):
        for place in range(2):
            relative = base + place * outer
            start = pl.multiple_of((((index ^ relative) % 4) * 2 + half) * rows, rows)
            block = part.at[pl.ds(place * rows, rows)]
            inside = whole.at[pl.ds(start, rows)]
            ends = (inside, block) if outward else (block, inside)
            copies.append(pltpu.make_async_copy(*ends, sems.at[len(copies)]))
    return copies


def start_all(copies):
    for copy in copies:
        copy.start()


def wait_all(copies):
    for copy in copies:
        copy.wait()


def load_tokens(same, sibling):
    return jnp.concatenate([same[0], sibling[0], same[1], sibling[1]])


def store_tokens(values, same, sibling):
    count = same.shape[1]
    for sequence in range(2):
        at = 2 * count * sequence
        same[sequence] = values[at : at + count].astype(same.dtype)
        sibling[sequence] = values[at + count : at + 2 * count].astype(sibling.dtype)


def place_of(scalars, sequence, at):
    block = jnp.where(
        at < 128,
        jnp.where(at < 64, scalars[1 + 4 * sequence], scalars[2 + 4 * sequence]),
        jnp.where(at < 192, scalars[3 + 4 * sequence], scalars[4 + 4 * sequence]),
    )
    return block * 64 + at % 64


def allowed_of(scalars, sequence):
    rows = place_of(scalars, sequence, lax.broadcasted_iota(jnp.int32, (256, 1), 0))
    cols = place_of(scalars, sequence, lax.broadcasted_iota(jnp.int32, (1, 256), 1))
    return rows >= cols


def fill_tables(scalars, cosine, sine, cos_rows, sin_rows):
    for slot in range(8):
        start = pl.multiple_of(scalars[1 + slot] * 64, 64)
        cos_rows[slot * 64 : slot * 64 + 64] = cosine[pl.ds(start, 64)]
        sin_rows[slot * 64 : slot * 64 + 64] = sine[pl.ds(start, 64)]


def attend_kernel(
    scalars, same, sibling, part_a, part_b, part_c, part_d, cosine, sine, gains,
    mixture, pre, rotated, values_out, log_total, whole, cos_rows, sin_rows, sems,
):
    copies = column_copies(scalars[0], (part_a, part_b, part_c, part_d), whole, sems, False)
    start_all(copies)
    fill_tables(scalars, cosine, sine, cos_rows, sin_rows)
    tokens = load_tokens(same, sibling)
    wait_all(copies)
    projected = matmul(tokens, whole[...])
    pre[...] = projected[:, :768]
    values_out[...] = projected[:, 768:].astype(LOW)
    for head in range(6):
        cut = slice(head * 128, head * 128 + 128)
        raw = pre[:, cut]
        gain = gains[0:1] if head < 4 else gains[1:2]
        scale = lax.rsqrt(jnp.mean(raw * raw, axis=-1, keepdims=True) + EPSILON)
        unit = raw * scale * gain
        turned = pltpu.roll(unit, 64, 1)
        rotated[:, cut] = (unit * cos_rows[...] + turned * sin_rows[...]).astype(LOW)
    for sequence in range(2):
        rows = slice(sequence * 256, sequence * 256 + 256)
        allowed = allowed_of(scalars, sequence)
        tops = []
        for head in range(4):
            group = head // 2
            queries = rotated[rows, head * 128 : head * 128 + 128]
            keys = rotated[rows, 512 + group * 128 : 640 + group * 128]
            scores = jnp.where(allowed, contract_cols(queries, keys) * (128**-0.5), -1e30)
            top = jnp.max(scores, axis=-1, keepdims=True)
            weights = jnp.exp(scores - top)
            total = jnp.sum(weights, axis=-1, keepdims=True)
            probs = (weights / total).astype(LOW)
            mixed = matmul(probs, values_out[rows, group * 128 : group * 128 + 128])
            mixture[rows, head * 128 : head * 128 + 128] = mixed.astype(LOW)
            tops.append(jnp.broadcast_to(top + jnp.log(total), (256, 128)))
        lane = lax.broadcasted_iota(jnp.int32, (256, 128), 1)
        log_total[rows] = jnp.where(
            lane < 2, jnp.where(lane < 1, tops[0], tops[1]), jnp.where(lane < 3, tops[2], tops[3])
        )


def attend(scalars, tokens, parts, tables, gains, after=()):
    return call(
        attend_kernel,
        [SM, VM, VM, HB, HB, HB, HB, VM, VM, VM],
        [((512, 512), LOW), ((512, 768), WIDE), ((512, 768), LOW), ((512, 256), LOW), ((512, 128), WIDE)],
        [VM] * 5,
        [
            pltpu.VMEM((1024, 1024), LOW),
            pltpu.VMEM((512, 128), WIDE),
            pltpu.VMEM((512, 128), WIDE),
            pltpu.SemaphoreType.DMA((16,)),
        ],
        2 * 10**9,
        8 * 10**6,
        after,
    )(scalars, *tokens, *parts, *tables, gains)


def output_kernel(scalars, mixture, part_a, part_b, part_c, part_d, same, sibling, whole, sems):
    copies = row_copies(scalars[0], (part_a, part_b, part_c, part_d), whole, sems, False)
    start_all(copies)
    wait_all(copies)
    store_tokens(matmul(mixture[...], whole[...]), same, sibling)


def row_product(scalars, left, parts, after=()):
    depth = left.shape[1]
    return call(
        output_kernel,
        [SM, VM, HB, HB, HB, HB],
        [((2, 128, 1024), LOW)] * 2,
        [VM] * 2,
        [pltpu.VMEM((depth, 1024), LOW), pltpu.SemaphoreType.DMA((8,))],
        2 * 512 * 1024 * depth,
        4 * 10**6,
        after,
    )(scalars, left, *parts)


def gate_kernel(
    scalars, same, sibling, part_a, part_b, part_c, part_d, gate_up, active, whole, sems
):
    copies = column_copies(scalars[0], (part_a, part_b, part_c, part_d), whole, sems, False)
    start_all(copies)
    tokens = load_tokens(same, sibling)
    wait_all(copies)
    for at in range(0, 768, 256):
        gate = matmul(tokens, whole[:, at : at + 256])
        upward = matmul(tokens, whole[:, 768 + at : 1024 + at])
        gate_up[:, at : at + 256] = gate.astype(LOW)
        gate_up[:, 768 + at : 1024 + at] = upward.astype(LOW)
        active[:, at : at + 256] = (gate * jax.nn.sigmoid(gate) * upward).astype(LOW)


def gate_product(scalars, tokens, parts, after=()):
    return call(
        gate_kernel,
        [SM, VM, VM, HB, HB, HB, HB],
        [((512, 1536), LOW), ((512, 768), LOW)],
        [VM] * 2,
        [pltpu.VMEM((1024, 1536), LOW), pltpu.SemaphoreType.DMA((16,))],
        2 * 512 * 1024 * 1536,
        10 * 10**6,
        after,
    )(scalars, *tokens, *parts)


def swiglu_back_kernel(
    scalars, same, sibling, gate_up, row_a, row_b, row_c, row_d, col_a, col_b, col_c, col_d,
    grad_gate_up, grad_same, grad_sibling, down, both, row_sems, col_sems,
):
    down_copies = row_copies(scalars[0], (row_a, row_b, row_c, row_d), down, row_sems, False)
    both_copies = column_copies(scalars[0], (col_a, col_b, col_c, col_d), both, col_sems, False)
    start_all(down_copies)
    start_all(both_copies)
    grad_out = load_tokens(same, sibling)
    wait_all(down_copies)
    for at in range(0, 768, 256):
        grad_active = contract_cols(grad_out, down[at : at + 256])
        gate = gate_up[:, at : at + 256].astype(WIDE)
        upward = gate_up[:, 768 + at : 1024 + at].astype(WIDE)
        sigmoid = jax.nn.sigmoid(gate)
        grad_gate_up[:, at : at + 256] = (
            grad_active * upward * (sigmoid * (1.0 + gate * (1.0 - sigmoid)))
        ).astype(LOW)
        grad_gate_up[:, 768 + at : 1024 + at] = (grad_active * (gate * sigmoid)).astype(LOW)
    wait_all(both_copies)
    store_tokens(contract_cols(grad_gate_up[...], both[...]), grad_same, grad_sibling)


def swiglu_back(scalars, grad_out, gate_up, down_parts, gate_up_parts, after=()):
    return call(
        swiglu_back_kernel,
        [SM, VM, VM, VM] + [HB] * 8,
        [((512, 1536), LOW), ((2, 128, 1024), LOW), ((2, 128, 1024), LOW)],
        [VM] * 3,
        [
            pltpu.VMEM((768, 1024), LOW),
            pltpu.VMEM((1024, 1536), LOW),
            pltpu.SemaphoreType.DMA((8,)),
            pltpu.SemaphoreType.DMA((16,)),
        ],
        2 * 512 * 1024 * 2304,
        12 * 10**6,
        after,
    )(scalars, *grad_out, gate_up, *down_parts, *gate_up_parts)


def attend_back_kernel(
    scalars, same, sibling, part_a, part_b, part_c, part_d, pre, rotated, values, log_total,
    cosine, sine, gains, grad_all, grad_gains, whole, cos_rows, sin_rows, grad_rot, sems,
):
    copies = row_copies(scalars[0], (part_a, part_b, part_c, part_d), whole, sems, False)
    start_all(copies)
    fill_tables(scalars, cosine, sine, cos_rows, sin_rows)
    branch = load_tokens(same, sibling)
    wait_all(copies)
    grad_mixed = contract_cols(branch, whole[...]).astype(LOW)
    scaling = 128**-0.5
    for sequence in range(2):
        rows = slice(sequence * 256, sequence * 256 + 256)
        allowed = allowed_of(scalars, sequence)
        for group in range(2):
            keys = rotated[rows, 512 + group * 128 : 640 + group * 128]
            value_rows = values[rows, group * 128 : group * 128 + 128]
            grad_keys = jnp.zeros((256, 128), WIDE)
            grad_values = jnp.zeros((256, 128), WIDE)
            for head in (2 * group, 2 * group + 1):
                cut = slice(head * 128, head * 128 + 128)
                queries = rotated[rows, cut]
                grad_mix = grad_mixed[rows, cut]
                scores = jnp.where(allowed, contract_cols(queries, keys) * scaling, -1e30)
                probs = jnp.exp(scores - log_total[rows, head : head + 1])
                grad_values += contract_rows(probs.astype(LOW), grad_mix)
                grad_probs = contract_cols(grad_mix, value_rows)
                inner = jnp.sum(probs * grad_probs, axis=-1, keepdims=True)
                grad_scores = (probs * (grad_probs - inner)).astype(LOW)
                grad_rot[rows, cut] = matmul(grad_scores, keys) * scaling
                grad_keys += contract_rows(grad_scores, queries)
            grad_rot[rows, 512 + group * 128 : 640 + group * 128] = grad_keys * scaling
            grad_all[rows, 768 + group * 128 : 896 + group * 128] = grad_values.astype(LOW)
    gain_sums = [jnp.zeros((1, 128), WIDE), jnp.zeros((1, 128), WIDE)]
    for head in range(6):
        cut = slice(head * 128, head * 128 + 128)
        which = 0 if head < 4 else 1
        raw = pre[:, cut]
        scale = lax.rsqrt(jnp.mean(raw * raw, axis=-1, keepdims=True) + EPSILON)
        unit = raw * scale
        coming = grad_rot[:, cut]
        back = coming * cos_rows[...] - pltpu.roll(coming, 64, 1) * sin_rows[...]
        gain_sums[which] += jnp.sum(back * unit, axis=0, keepdims=True)
        back = back * gains[which : which + 1]
        along = jnp.mean(back * unit, axis=-1, keepdims=True)
        grad_all[:, cut] = (scale * (back - unit * along)).astype(LOW)
    grad_gains[...] = jnp.zeros((8, 128), WIDE)
    grad_gains[0:1] = gain_sums[0]
    grad_gains[1:2] = gain_sums[1]


def attend_back_call(scalars, branch, parts, pre, rotated, values, log_total, tables, gains, after=()):
    return call(
        attend_back_kernel,
        [SM, VM, VM, HB, HB, HB, HB] + [VM] * 7,
        [((512, 1024), LOW), ((8, 128), WIDE)],
        [VM] * 2,
        [
            pltpu.VMEM((512, 1024), LOW),
            pltpu.VMEM((512, 128), WIDE),
            pltpu.VMEM((512, 128), WIDE),
            pltpu.VMEM((512, 768), WIDE),
            pltpu.SemaphoreType.DMA((8,)),
        ],
        2 * 10**9,
        8 * 10**6,
        after,
    )(scalars, *branch, *parts, pre, rotated, values, log_total, *tables, gains)


def column_back_kernel(scalars, grads, part_a, part_b, part_c, part_d, same, sibling, whole, sems):
    copies = column_copies(scalars[0], (part_a, part_b, part_c, part_d), whole, sems, False)
    start_all(copies)
    wait_all(copies)
    store_tokens(contract_cols(grads[...], whole[...]), same, sibling)


def column_back(scalars, grads, parts, after=()):
    width = grads.shape[1]
    return call(
        column_back_kernel,
        [SM, VM, HB, HB, HB, HB],
        [((2, 128, 1024), LOW)] * 2,
        [VM] * 2,
        [pltpu.VMEM((1024, width), LOW), pltpu.SemaphoreType.DMA((16,))],
        2 * 512 * 1024 * width,
        5 * 10**6,
        after,
    )(scalars, grads, *parts)


def column_grad_kernel(
    scalars, same, sibling, grads, keep_one, send_one, keep_two, send_two, whole, sems
):
    for at in range(0, 1024, 256):
        cut = slice(at, at + 256)
        left = jnp.concatenate(
            [same[0, :, cut], sibling[0, :, cut], same[1, :, cut], sibling[1, :, cut]]
        )
        whole[cut] = contract_rows(left, grads[...]).astype(LOW)
    copies = column_copies(
        scalars[0], (keep_one, send_one, keep_two, send_two), whole, sems, True
    )
    start_all(copies)
    wait_all(copies)


def column_grad(scalars, tokens, grads, after=()):
    width = grads.shape[1]
    return call(
        column_grad_kernel,
        [SM, VM, VM, VM],
        [((256, width), LOW)] * 4,
        [HB] * 4,
        [pltpu.VMEM((1024, width), LOW), pltpu.SemaphoreType.DMA((16,))],
        2 * 512 * 1024 * width,
        6 * 10**6,
        after,
    )(scalars, *tokens, grads)


def row_grad_kernel(
    scalars, left, same, sibling, keep_one, send_one, keep_two, send_two, whole, sems
):
    right = load_tokens(same, sibling)
    for at in range(0, whole.shape[0], 256):
        cut = slice(at, at + 256)
        whole[cut] = contract_rows(left[:, cut], right).astype(LOW)
    copies = row_copies(scalars[0], (keep_one, send_one, keep_two, send_two), whole, sems, True)
    start_all(copies)
    wait_all(copies)


def row_grad(scalars, left, tokens, after=()):
    depth = left.shape[1]
    return call(
        row_grad_kernel,
        [SM, VM, VM, VM],
        [((depth // 4, 1024), LOW)] * 4,
        [HB] * 4,
        [pltpu.VMEM((depth, 1024), LOW), pltpu.SemaphoreType.DMA((8,))],
        2 * 512 * 1024 * depth,
        4 * 10**6,
        after,
    )(scalars, left, *tokens)


def fast_body(
    hidden_in,
    cotangent,
    block_order,
    w_query,
    key_weight,
    value_weight,
    w_output,
    w_gate,
    w_up,
    w_down,
    norm_gains,
    momentum_query,
    key_momentum,
    value_momentum,
    momentum_output,
    momentum_gate,
    momentum_up,
    momentum_down,
    momentum_gains,
):
    index = lax.axis_index("dp")
    core = lax.axis_index("ctx")
    p_index = (index // P_BIT) % 2
    mine = h_of(index) == core
    slice_own = 2 * core + p_index
    slice_give = 2 * core + 1 - p_index

    def column_slice(weight, which):
        size = weight.shape[1] // 4
        return lax.dynamic_slice_in_dim(weight, which * size, size, axis=1).astype(LOW)

    def column_pack(weights, which):
        return jnp.concatenate([column_slice(weight, which) for weight in weights], axis=1)

    gains_low = norm_gains.astype(LOW)[None]
    for bit in (P_BIT, H_BIT, Y_BIT, X_BIT):
        gains_low = jnp.concatenate([gains_low, swap(gains_low, bit)])
    order = [0]
    for bit in (P_BIT, H_BIT, Y_BIT, X_BIT):
        order = order + [o ^ bit for o in order]
    inverse = [0] * 16
    for at, relative in enumerate(order):
        inverse[relative] = at
    lookup = jnp.array(inverse, jnp.int32)[index ^ jnp.arange(16)]
    gains_all = jnp.take(gains_low, lookup, axis=0).reshape(-1).astype(WIDE)

    width = hidden_in.shape[2]
    head_size = 128
    gain_attn = gains_all[:width]
    gain_mlp = gains_all[width : 2 * width]
    head_gains = gains_all[2 * width :].reshape(2, head_size)

    qkv = (w_query, key_weight, value_weight)
    qkv_parts = gather_column_slices(column_pack(qkv, slice_own), column_pack(qkv, slice_give))
    output_parts = gather_row_slices(w_output.astype(LOW), mine)
    gate_up = (w_gate, w_up)
    gate_up_parts = gather_column_slices(
        column_pack(gate_up, slice_own), column_pack(gate_up, slice_give)
    )
    down_parts, _, down_first = gather_row_slices(w_down.astype(LOW), mine, True)

    tokens_own = hidden_in[0]
    count = tokens_own.shape[0]
    orders = jnp.concatenate([block_order, swap(block_order, P_BIT)])
    orders = jnp.where(core == 0, orders, jnp.roll(orders, 2, axis=1))
    scalars = jnp.concatenate([index[None], orders.reshape(-1)]).astype(jnp.int32)
    cosine, sine_table = rotary_tables(jnp.arange(2 * count, dtype=jnp.int32), head_size)
    sign = jnp.where(jnp.arange(head_size) < head_size // 2, -1.0, 1.0)
    tables = (cosine, sine_table * sign)

    tokens_f = tokens_own.astype(WIDE)
    normed_f, norm_pull = jax.vjp(rms_norm, tokens_f, gain_attn)
    normed = gather_tokens(normed_f.astype(LOW))
    grad_out = gather_tokens(cotangent[0])

    mixed_low, pre, rotated, value_low, log_total = attend(
        scalars, normed, qkv_parts, tables, head_gains
    )
    attended = sum_tokens(*row_product(scalars, mixed_low, output_parts, down_first))
    middle = tokens_f + attended
    normed_two_f, norm_two_pull = jax.vjp(rms_norm, middle, gain_mlp)
    normed_two = gather_tokens(normed_two_f.astype(LOW))
    gate_up_act, active = gate_product(scalars, normed_two, gate_up_parts, down_parts)
    grad_gate_up, back_same, back_sibling = swiglu_back(
        scalars, grad_out, gate_up_act, down_parts, gate_up_parts
    )
    grad_down = row_grad(scalars, active, grad_out, [back_same])
    grad_normed_two = sum_tokens(back_same, back_sibling)
    grad_gate_up_mat = column_grad(scalars, normed_two, grad_gate_up, [back_same])

    grad_middle_norm, grad_gain_mlp = norm_two_pull(grad_normed_two)
    grad_middle = cotangent[0].astype(WIDE) + grad_middle_norm
    grad_branch = gather_tokens(grad_middle.astype(LOW))
    grad_qkv, grad_head_gains = attend_back_call(
        scalars, grad_branch, output_parts, pre, rotated, value_low, log_total, tables, head_gains
    )
    grad_qkv_mat = column_grad(scalars, normed, grad_qkv, ())
    grad_output_mat = row_grad(scalars, mixed_low, grad_branch, [grad_qkv_mat[0]])
    grad_normed = sum_tokens(*column_back(scalars, grad_qkv, qkv_parts, [grad_qkv_mat[0]]))
    grad_tokens_norm, grad_gain_attn = norm_pull(grad_normed)
    input_grad = (grad_middle + grad_tokens_norm).astype(LOW)[None]

    layer_sum = sum_tokens(*row_product(scalars, active, down_parts, [grad_qkv_mat[0]]))
    layer_out = (middle + layer_sum).astype(LOW)[None]
    grad_gains = jnp.concatenate([grad_gain_attn, grad_gain_mlp, grad_head_gains[:2].reshape(-1)])
    grad_gains = grad_gains.reshape(16, -1)
    grad_gains = grad_gains + swap_core(grad_gains.astype(LOW)).astype(WIDE)
    for bit in (P_BIT, H_BIT, Y_BIT, X_BIT):
        grad_gains = grad_gains + swap(grad_gains.astype(LOW), bit).astype(WIDE)
    grad_gains = lax.dynamic_index_in_dim(grad_gains, index, keepdims=False)

    down_sum = scatter_row_slices(*grad_down, mine)
    gate_up_sum = join_column_slices(*scatter_column_slices(*grad_gate_up_mat), p_index, core)
    output_sum = scatter_row_slices(*grad_output_mat, mine)
    qkv_sum = join_column_slices(*scatter_column_slices(*grad_qkv_mat), p_index, core)

    def columns(parts, start, size):
        return jnp.concatenate([part[:, start : start + size] for part in parts], axis=1)

    query_width = w_query.shape[1] // 4
    kv_width = key_weight.shape[1] // 4
    hidden_units = w_gate.shape[1] // 4
    sums = (
        columns(qkv_sum, 0, query_width),
        columns(qkv_sum, query_width, kv_width),
        columns(qkv_sum, query_width + kv_width, kv_width),
        output_sum,
        columns(gate_up_sum, 0, hidden_units),
        columns(gate_up_sum, hidden_units, hidden_units),
        down_sum,
        grad_gains,
    )
    masters = (w_query, key_weight, value_weight, w_output, w_gate, w_up, w_down, norm_gains)
    moments = (
        momentum_query,
        key_momentum,
        value_momentum,
        momentum_output,
        momentum_gate,
        momentum_up,
        momentum_down,
        momentum_gains,
    )
    norm_scale = lax.rsqrt(jnp.float32(16 * 2 * count))
    summed = tuple(part.astype(WIDE) for part in sums)
    updates, new_moments = lion_step(masters, moments, summed, norm_scale)
    return (layer_out, input_grad) + tuple(updates) + tuple(new_moments)


def solution(mesh):
    body = fast_body if dict(mesh.shape) == {"dp": 16, "ctx": 2} else general_body
    return jax.shard_map(
        body,
        mesh=mesh,
        in_specs=(
            P("dp", "ctx", None),
            P("dp", "ctx", None),
            P("dp", None),
            P("dp", None),
            P("dp", None),
            P("dp", None),
            P("dp", None),
            P("dp", None),
            P("dp", None),
            P("dp", None),
            P("dp"),
            P("dp", None),
            P("dp", None),
            P("dp", None),
            P("dp", None),
            P("dp", None),
            P("dp", None),
            P("dp", None),
            P("dp"),
        ),
        out_specs=(
            P("dp", "ctx", None),
            P("dp", "ctx", None),
            P("dp", None),
            P("dp", None),
            P("dp", None),
            P("dp", None),
            P("dp", None),
            P("dp", None),
            P("dp", None),
            P("dp"),
            P("dp", None),
            P("dp", None),
            P("dp", None),
            P("dp", None),
            P("dp", None),
            P("dp", None),
            P("dp", None),
            P("dp"),
        ),
        check_vma=False,
    )
```
